32 devices in a mesh: tx: 4 (over x, core), ty: 8 (over z, y).
Axes of the slice: x: 2, y: 2, z: 4, core: 2. Of those that a mesh axis runs over, the one named last changes fastest.
Arguments:
- granule_blocks: bfloat16 [2048, 13, 16, 128], P(('tx', 'ty')), may hold values from -6 to 6
- row_weights: bfloat16 [2048, 8, 16], P(('tx', 'ty')), may hold values from -1.5 to 1.5
- column_bank: bfloat16 [8, 128, 128], replicated, may hold values from -0.5 to 0.5
- destination: int32 [2048], P(('tx', 'ty')), may hold values from 0 to 31, as said below
- window_index: int32 [2048], P(('tx', 'ty')), may hold values from 0 to 31
- bank_index: int32 [2048], P(('tx', 'ty')), may hold values from 0 to 7
- kernel_one: bfloat16 [3, 3, 13, 64], replicated, may hold values from -1 to 1
- reduce_two: bfloat16 [2, 2, 64, 128], replicated, may hold values from -0.5 to 0.5
- kernel_two: bfloat16 [3, 3, 128, 128], replicated, may hold values from -0.25 to 0.25
- reduce_three: bfloat16 [2, 2, 128, 256], replicated, may hold values from -0.375 to 0.375
- kernel_three: bfloat16 [3, 3, 256, 256], replicated, may hold values from -0.1875 to 0.1875
- reduce_four: bfloat16 [2, 2, 256, 512], replicated, may hold values from -0.25 to 0.25
- kernel_four: bfloat16 [3, 3, 512, 512], replicated, may hold values from -0.125 to 0.125
Outputs:
- gridded: bfloat16 [13, 2048, 512], P(None, 'ty', 'tx')
- bottleneck: bfloat16 [512, 256, 64], P(None, 'ty', 'tx')
The draws below stay inside these ranges and needn't reach their ends.
Inputs may be any that keep to these rules, and one draw needn't show every extreme that they name: At most 2 of the blocks that one device holds name the same destination; in every draw one destination is named by 2 blocks of every device.
All inputs are finite; a program needn't handle non-finite values.
Results may differ from the reference program's by a relative error of at most 0.015.
Values may be sent and summed in bfloat16 or wider, within the bound.
No kernel may reach another device: no remote copies, remote signals or barrier semaphores. Data moves between devices by JAX's collectives and lax.ppermute only.
A program may use at most 128 MiB of HBM per device.

```python
import jax
import jax.numpy as jnp
from jax import lax

CH_ONE = 64
CH_TWO = 128
CH_THREE = 256
CH_FOUR = 512
BANDS = 13
SRC_ROWS = 16
SRC_COLS = 128
WIN_ROWS = 8
TILE_COLS = 128
BANK = 8
CAP = 2
BLK_DEV = 64
TILE_ROWS = 256
TILES = 32
BLOCKS = 2048
NWIN = 32
ROWS = 2048
COLS = 512
N_TX = 4
N_TY = 8


def draw_destination(key, part):
    key_hot, key_tier, key_score = jax.random.split(key, 3)
    slot_total = TILES * CAP
    hottest = jax.random.randint(key_hot, (), 0, TILES)
    tier_level = jax.random.randint(key_tier, (TILES,), 0, 4)
    slot_ids = jnp.arange(slot_total, dtype=jnp.int32)
    owning = slot_ids // CAP
    scores = jax.random.randint(key_score, (TILES, slot_total), 0, 65536)
    scores = scores + ((3 - tier_level[owning]) * 16384)[None, :]
    scores = scores * slot_total + slot_ids[None, :]
    scores = jnp.where((owning == hottest)[None, :], (slot_ids - slot_total)[None, :], scores)
    ranking = jnp.argsort(scores, axis=1, stable=True)
    chosen = ranking[:, :BLK_DEV]
    return (chosen // CAP).astype(jnp.int32).reshape(BLOCKS)


def with_ends(result, key, low, largest):
    shape = result.shape
    spot = [jax.random.randint(jax.random.fold_in(key, axis), (), 0, shape[axis]) for axis in range(len(shape))]
    result = result.at[tuple(spot)].set(low)
    longest = shape.index(max(shape))
    spot[longest] = (spot[longest] + 1) % shape[longest]
    return result.at[tuple(spot)].set(largest)


def shard_levels(key, dims, shards, low, high):
    level, own = 1.0, jax.random.fold_in(key, 6)
    for dim, blocks in shards:
        heights = jnp.exp(jax.random.uniform(jax.random.fold_in(own, dim), (blocks,), jnp.float32, low / len(shards), high / len(shards)))
        level = level * jnp.repeat(heights, dims[dim] // blocks).reshape([-1 if axis == dim else 1 for axis in range(len(dims))])
    return level


def gaussian(own_key, dims, scale, reach, cuts=(), held_as=jnp.bfloat16):
    entries = scale * jax.random.normal(own_key, dims, jnp.float32)
    if cuts:
        entries = entries * shard_levels(own_key, dims, cuts, -0.22, 0.18)
    return jnp.clip(entries, -reach, reach).astype(held_as)


def setup_inputs(seed: int = 0) -> dict:
    arg_keys = jax.random.split(jax.random.key(seed), 14)
    return {
        "granule_blocks": gaussian(arg_keys[0], (BLOCKS, BANDS, SRC_ROWS, SRC_COLS), 1.0, 6.0, ((0, 32),)),
        "row_weights": gaussian(arg_keys[1], (BLOCKS, WIN_ROWS, SRC_ROWS), SRC_ROWS ** -0.5, 1.5, ((0, 32),)),
        "column_bank": gaussian(arg_keys[2], (BANK, SRC_COLS, TILE_COLS), SRC_COLS ** -0.5, 0.5),
        "destination": draw_destination(jax.random.fold_in(arg_keys[13], 71), 0),
        "window_index": with_ends(jax.random.randint(arg_keys[4], (BLOCKS,), 0, NWIN), jax.random.fold_in(arg_keys[4], 1), 0, NWIN - 1).astype(jnp.int32),
        "bank_index": with_ends(jax.random.randint(arg_keys[5], (BLOCKS,), 0, BANK), jax.random.fold_in(arg_keys[5], 1), 0, BANK - 1).astype(jnp.int32),
        "kernel_one": gaussian(arg_keys[6], (3, 3, BANDS, CH_ONE), (9 * BANDS // 4) ** -0.5, 1.0),
        "reduce_two": gaussian(arg_keys[7], (2, 2, CH_ONE, CH_TWO), (2 * CH_ONE) ** -0.5, 0.5),
        "kernel_two": gaussian(arg_keys[8], (3, 3, CH_TWO, CH_TWO), (9 * CH_TWO // 2) ** -0.5, 0.25),
        "reduce_three": gaussian(arg_keys[9], (2, 2, CH_TWO, CH_THREE), (2 * CH_TWO) ** -0.5, 0.375),
        "kernel_three": gaussian(arg_keys[10], (3, 3, CH_THREE, CH_THREE), (9 * CH_THREE // 2) ** -0.5, 0.1875),
        "reduce_four": gaussian(arg_keys[11], (2, 2, CH_THREE, CH_FOUR), (2 * CH_THREE) ** -0.5, 0.25),
        "kernel_four": gaussian(arg_keys[12], (3, 3, CH_FOUR, CH_FOUR), (9 * CH_FOUR // 2) ** -0.5, 0.125),
    }


def conv_same(field, kernel):
    output = lax.conv_general_dilated(field[None].astype(jnp.float32), kernel.astype(jnp.float32), (1, 1), ((1, 1), (1, 1)), dimension_numbers=("NCHW", "HWIO", "NCHW"), precision=lax.Precision.HIGHEST)[0]
    return jnp.maximum(output, 0.0).astype(jnp.bfloat16)


def reduce_half(field, kernel):
    output = lax.conv_general_dilated(field[None].astype(jnp.float32), kernel.astype(jnp.float32), (2, 2), "VALID", dimension_numbers=("NCHW", "HWIO", "NCHW"), precision=lax.Precision.HIGHEST)[0]
    return jnp.maximum(output, 0.0).astype(jnp.bfloat16)


def reference(granule_blocks, row_weights, column_bank, destination, window_index, bank_index, kernel_one, reduce_two, kernel_two, reduce_three, kernel_three, reduce_four, kernel_four):
    tile_count = N_TX * N_TY
    windows = TILE_ROWS // WIN_ROWS
    segments = tile_count * windows
    raw_parts = granule_blocks.reshape(tile_count, BLK_DEV, BANDS, SRC_ROWS, SRC_COLS)
    weight_parts = row_weights.reshape(tile_count, BLK_DEV, WIN_ROWS, SRC_ROWS)
    dest_parts = destination.reshape(tile_count, BLK_DEV).astype(jnp.int32)
    window_parts = window_index.reshape(tile_count, BLK_DEV).astype(jnp.int32)
    bank_parts = bank_index.reshape(tile_count, BLK_DEV).astype(jnp.int32)

    def step_over(carry, inputs):
        sums, counts = carry
        raw_part, weight_part, dest_part, window_part, bank_part = inputs
        rowed = jnp.einsum("nrk,nbkc->nbrc", weight_part.astype(jnp.float32), raw_part.astype(jnp.float32), precision=lax.Precision.HIGHEST).astype(jnp.bfloat16)
        matrices = column_bank[bank_part].astype(jnp.float32)
        resampled = jnp.einsum("nbrc,nct->nbrt", rowed.astype(jnp.float32), matrices, precision=lax.Precision.HIGHEST).astype(jnp.bfloat16)
        target = (dest_part * windows + window_part).astype(jnp.int32)
        sums = sums + jax.ops.segment_sum(resampled.astype(jnp.float32), target, num_segments=segments)
        counts = counts + jax.ops.segment_sum(jnp.ones((BLK_DEV,), jnp.int32), target, num_segments=segments)
        return (sums, counts), None

    start = (jnp.zeros((segments, BANDS, WIN_ROWS, TILE_COLS), jnp.float32), jnp.zeros((segments,), jnp.int32))
    (sums, counts), unused = lax.scan(step_over, start, (raw_parts, weight_parts, dest_parts, window_parts, bank_parts))
    divisor = jnp.maximum(counts, 1).astype(jnp.float32)
    averaged = sums / divisor[:, None, None, None]
    averaged = averaged.reshape(N_TX, N_TY, windows, BANDS, WIN_ROWS, TILE_COLS)
    gridded = jnp.transpose(averaged, (3, 1, 2, 4, 0, 5)).reshape(BANDS, ROWS, COLS).astype(jnp.bfloat16)
    level_one = conv_same(gridded, kernel_one)
    level_two = conv_same(reduce_half(level_one, reduce_two), kernel_two)
    level_three = conv_same(reduce_half(level_two, reduce_three), kernel_three)
    bottleneck = conv_same(reduce_half(level_three, reduce_four), kernel_four)
    return gridded, bottleneck
```

```python
import functools

import jax
import jax.numpy as jnp
import numpy as np
from jax import lax
from jax.experimental import pallas as pl
from jax.experimental.pallas import tpu as pltpu
from jax.sharding import PartitionSpec as P

BF16 = jnp.bfloat16
F32 = jnp.float32
BANDS = 13
SRC_ROWS = 16
WIN_ROWS = 8
CAP = 2
NWIN = 32
TILE_COLS = 128
LINES = BANDS * WIN_ROWS
STEP_BLOCKS = 8
PHASES = 8
SPOTS = TILE_COLS // PHASES
HALO = 2
WIDE = SPOTS + 2 * HALO
TALL = NWIN + 2 * HALO
POINTS = WIDE * TALL
GROUP = 4
GROUP_POINTS = GROUP * WIDE
VMEM_BYTES = 60 * 1024 * 1024


def dot(a, b):
    return jnp.dot(a, b, preferred_element_type=F32)


def dot_nt(a, b):
    return lax.dot_general(a, b, (((1,), (1,)), ((), ())), preferred_element_type=F32)


def resample_kernel(
    dest_ref, win_ref, choice_ref, weight_ref, raw_ref, bank_ref, spread_ref, mask_ref,
    out_ref, slot_win_ref, held_ref,
):
    step = pl.program_id(0)

    @pl.when(step == 0)
    def _():
        def clear_slot(i, carry):
            slot_win_ref[i] = -1
            return carry

        def clear_tile(i, carry):
            held_ref[i] = 0
            return carry

        lax.fori_loop(0, slot_win_ref.shape[0], clear_slot, 0)
        lax.fori_loop(0, held_ref.shape[0], clear_tile, 0)

    spread = dot(weight_ref[...], spread_ref[...])
    mask = mask_ref[...]
    rowed = []
    for j in range(STEP_BLOCKS):
        rows = spread[j * WIN_ROWS:(j + 1) * WIN_ROWS]
        weights = jnp.concatenate([rows] * BANDS, axis=0) * mask
        rowed.append(dot(weights.astype(BF16), raw_ref[j]).astype(BF16))
    for j in range(STEP_BLOCKS):
        n = step * STEP_BLOCKS + j
        tile = dest_ref[n]
        rank = held_ref[tile]
        held_ref[tile] = rank + 1
        slot = tile * CAP + rank
        slot_win_ref[slot] = win_ref[n]
        out_ref[slot] = dot(rowed[j], bank_ref[choice_ref[n]]).astype(BF16)


def resample(granule_blocks, row_weights, column_bank, destination, window_index, bank_index, tiles):
    blocks = granule_blocks.shape[0]
    deep = BANDS * SRC_ROWS
    slots = tiles * CAP
    lane = np.arange(deep)
    spread = (lane[None, :] % SRC_ROWS == np.arange(SRC_ROWS)[:, None]).astype(np.float32)
    mask = (lane[None, :] // SRC_ROWS == np.arange(LINES)[:, None] // WIN_ROWS).astype(np.float32)
    return pl.pallas_call(
        resample_kernel,
        grid_spec=pltpu.PrefetchScalarGridSpec(
            num_scalar_prefetch=3,
            grid=(blocks // STEP_BLOCKS,),
            in_specs=[
                pl.BlockSpec((STEP_BLOCKS * WIN_ROWS, SRC_ROWS), lambda i, *_: (i, 0)),
                pl.BlockSpec((STEP_BLOCKS, deep, TILE_COLS), lambda i, *_: (i, 0, 0)),
                pl.BlockSpec(column_bank.shape, lambda i, *_: (0, 0, 0)),
                pl.BlockSpec((SRC_ROWS, deep), lambda i, *_: (0, 0)),
                pl.BlockSpec((LINES, deep), lambda i, *_: (0, 0)),
            ],
            out_specs=[
                pl.BlockSpec((slots, LINES, TILE_COLS), lambda i, *_: (0, 0, 0)),
                pl.BlockSpec(memory_space=pltpu.SMEM),
            ],
            scratch_shapes=[pltpu.SMEM((tiles,), jnp.int32)],
        ),
        out_shape=[
            jax.ShapeDtypeStruct((slots, LINES, TILE_COLS), BF16),
            jax.ShapeDtypeStruct((slots,), jnp.int32),
        ],
        compiler_params=pltpu.CompilerParams(vmem_limit_bytes=VMEM_BYTES),
        name="resample",
    )(
        destination, window_index, bank_index,
        row_weights.reshape(blocks * WIN_ROWS, SRC_ROWS),
        granule_blocks.reshape(blocks, deep, TILE_COLS),
        column_bank, jnp.asarray(spread, BF16), jnp.asarray(mask, F32),
    )


def grid_kernel(
    win_ref, got_ref, perm_ref, grid_ref, main_ref, left_ref, right_ref, sum_ref, count_ref
):
    def clear(w, carry):
        sum_ref[w] = jnp.zeros(sum_ref.shape[1:], F32)
        count_ref[w] = 0
        return carry

    lax.fori_loop(0, NWIN + 1, clear, 0)

    def add(s, carry):
        w = win_ref[s]
        w = jnp.where(w < 0, NWIN, w)
        sum_ref[w, 0:LINES] = sum_ref[w, 0:LINES] + got_ref[s].astype(F32)
        count_ref[w] = count_ref[w] + 1
        return carry

    lax.fori_loop(0, got_ref.shape[0], add, 0)

    def finish(pair, carry):
        means = []
        for k in range(2):
            w = pair * 2 + k
            divisor = jnp.maximum(count_ref[w], 1).astype(F32)
            mean = (sum_ref[w, 0:LINES] / divisor).astype(BF16).astype(F32)
            sum_ref[w, 0:LINES] = mean
            means.append(mean)
        row = pl.multiple_of(pair * 2 * WIN_ROWS, 2 * WIN_ROWS)
        for b in range(BANDS):
            both = jnp.concatenate([m[b * WIN_ROWS:(b + 1) * WIN_ROWS] for m in means], axis=0)
            grid_ref[b, pl.ds(row, 2 * WIN_ROWS), :] = both.astype(BF16)
        for k in range(2):
            w = pair * 2 + k
            lines = jnp.concatenate(
                [sum_ref[w, pl.ds(r, 16, stride=WIN_ROWS), :] for r in range(WIN_ROWS)], axis=0
            )
            turned = dot_nt(perm_ref[...], lines.astype(BF16)).astype(BF16)
            main_ref[pl.ds(pl.multiple_of(w * 128, 128), 128), :] = turned[0:128]
            left_ref[pl.ds(pl.multiple_of(w * 16, 16), 16), :] = turned[128:144]
            right_ref[pl.ds(pl.multiple_of(w * 16, 16), 16), :] = turned[144:160]
        return carry

    lax.fori_loop(0, NWIN // 2, finish, 0)


def grid(received, windows):
    perm = np.zeros((TILE_COLS + 32, TILE_COLS), np.float32)
    for p in range(PHASES):
        for a in range(SPOTS):
            perm[p * SPOTS + a, a * PHASES + p] = 1.0
        for a in range(HALO):
            perm[128 + p * HALO + a, a * PHASES + p] = 1.0
            perm[144 + p * HALO + a, (SPOTS - HALO + a) * PHASES + p] = 1.0
    vmem = pl.BlockSpec(memory_space=pltpu.VMEM)
    return pl.pallas_call(
        grid_kernel,
        in_specs=[pl.BlockSpec(memory_space=pltpu.SMEM), vmem, vmem],
        out_specs=[vmem] * 4,
        out_shape=[
            jax.ShapeDtypeStruct((BANDS, NWIN * WIN_ROWS, TILE_COLS), BF16),
            jax.ShapeDtypeStruct((NWIN * 128, 128), BF16),
            jax.ShapeDtypeStruct((NWIN * 16, 128), BF16),
            jax.ShapeDtypeStruct((NWIN * 16, 128), BF16),
        ],
        scratch_shapes=[
            pltpu.VMEM((NWIN + 1, 128, TILE_COLS), F32),
            pltpu.SMEM((NWIN + 1,), jnp.int32),
        ],
        compiler_params=pltpu.CompilerParams(vmem_limit_bytes=VMEM_BYTES),
        name="grid",
    )(windows, received, jnp.asarray(perm, BF16))


def exchange(main, left, right):
    across, down = lax.axis_size("tx"), lax.axis_size("ty")
    right_ward = [(i, i + 1) for i in range(across - 1)]
    left_ward = [(t, s) for s, t in right_ward]
    down_ward = [(i, i + 1) for i in range(down - 1)]
    up_ward = [(t, s) for s, t in down_ward]
    from_left = lax.ppermute(right, "tx", right_ward)
    from_right = lax.ppermute(left, "tx", left_ward)
    m, h = HALO * 128, HALO * 16
    first = jnp.concatenate([main[:m], from_left[:h], from_right[:h]], axis=0)
    last = jnp.concatenate([main[-m:], from_left[-h:], from_right[-h:]], axis=0)
    from_above = lax.ppermute(last, "ty", down_ward)
    from_below = lax.ppermute(first, "ty", up_ward)
    return from_left, from_right, from_above, from_below


def spread_matrix():
    out = np.zeros((PHASES + 2, GROUP_POINTS, GROUP * 48), np.float32)
    for index in range(PHASES + 2):
        p = (index - 1) % PHASES
        shift = -1 if index == 0 else (1 if index == PHASES + 1 else 0)
        for k in range(GROUP):
            for a in range(WIDE):
                s = a + shift
                row = k * WIDE + a
                if s < 0 or s >= WIDE:
                    continue
                if s < HALO:
                    out[index, row, GROUP * 16 + k * 16 + p * HALO + s] = 1.0
                elif s < HALO + SPOTS:
                    out[index, row, k * 16 + s - HALO] = 1.0
                else:
                    out[index, row, GROUP * 32 + k * 16 + p * HALO + s - HALO - SPOTS] = 1.0
    return out


def relu(x):
    return jnp.maximum(x, 0.0)


def encoder_kernel(
    main_ref, fl_ref, fr_ref, above_ref, below_ref, spread_ref, mask_ref, one_ref, down2_ref,
    two_ref, down3_hbm, three_hbm, down4_hbm, four_hbm,
    out_ref,
    ext1, ext2, x1, x2, d2, d3, d4, flat, down3_ref, three_ref, down4_ref, four_ref, sems,
):
    copies = [
        pltpu.make_async_copy(src, dst, sems.at[i])
        for i, (src, dst) in enumerate(
            (
                (down3_hbm, down3_ref),
                (three_hbm, three_ref),
                (down4_hbm, down4_ref),
                (four_hbm, four_ref),
            )
        )
    ]
    for copy in copies:
        copy.start()

    for h in range(HALO):
        for source, w in ((above_ref, h), (below_ref, HALO + NWIN + h)):
            ext1[w, 0:128] = source[h * 128:(h + 1) * 128]
            base = HALO * 128 + h * 16
            ext1[w, 128:144] = source[base:base + 16]
            ext1[w, 144:160] = source[base + HALO * 16:base + HALO * 16 + 16]

    def gather(w, carry):
        ext1[w + HALO, 0:128] = main_ref[pl.ds(pl.multiple_of(w * 128, 128), 128), :]
        ext1[w + HALO, 128:144] = fl_ref[pl.ds(pl.multiple_of(w * 16, 16), 16), :]
        ext1[w + HALO, 144:160] = fr_ref[pl.ds(pl.multiple_of(w * 16, 16), 16), :]
        return carry

    lax.fori_loop(0, NWIN, gather, 0)

    low = lax.broadcasted_iota(jnp.int32, (160, 128), 1) < 64

    def lower(w, carry):
        after = jnp.minimum(w + 1, TALL - 1)
        both = jnp.where(low, ext1[after].astype(F32), ext1[w].astype(F32))
        ext2[w] = pltpu.roll(both, 64, 1).astype(BF16)
        return carry

    lax.fori_loop(0, TALL, lower, 0)

    def place(g, carry):
        row = pl.multiple_of(g * GROUP_POINTS, GROUP_POINTS)
        for index in range(PHASES + 2):
            p = (index - 1) % PHASES
            sides = []
            for ext in (ext1, ext2):
                pieces = [ext[g * GROUP + k, p * 16:(p + 1) * 16] for k in range(GROUP)]
                pieces += [ext[g * GROUP + k, 128:144] for k in range(GROUP)]
                pieces += [ext[g * GROUP + k, 144:160] for k in range(GROUP)]
                sides.append(jnp.concatenate(pieces, axis=0))
            laid = dot(spread_ref[index], jnp.concatenate(sides, axis=1)).astype(BF16)
            x1[index, pl.ds(row, GROUP_POINTS), :] = laid[:, 0:128]
            x2[index, pl.ds(row, GROUP_POINTS), :] = laid[:, 128:256]
        return carry

    lax.fori_loop(0, TALL // GROUP, place, 0)

    mask = mask_ref[...]
    mask2 = jnp.concatenate([mask, mask], axis=1)
    mask4 = jnp.concatenate([mask2, mask2], axis=1)

    def put(dst, i, j, value, last):
        rows = [(i + 1, 0)]
        if i == last:
            rows.append((0, WIDE))
        if i == 0:
            rows.append((last + 2, -WIDE))
        cols = [(j + 1, 0)]
        if j == last:
            cols.append((0, 1))
        if j == 0:
            cols.append((last + 2, -1))
        for r, row_shift in rows:
            for c, col_shift in cols:
                shift = (row_shift + col_shift) % POINTS
                moved = pltpu.roll(value, shift, 0) if shift else value
                dst[r, c] = moved.astype(BF16)

    for cb in range(4):
        for version, x in enumerate((x1, x2)):
            taps = jnp.concatenate([x[2 * cb + k] for k in range(4)], axis=1)
            level = relu(dot(taps, one_ref[...])).astype(BF16)
            for half in range(2):
                down = relu(dot(level[:, half * 256:(half + 1) * 256], down2_ref[...]))
                if version == 0:
                    rb = 1 + half
                elif half == 0:
                    rb = 3
                else:
                    rb = 0
                    down = pltpu.roll(down, WIDE, 0)
                put(d2, rb, cb, down * mask, 3)

    copies[0].wait()
    for rp in range(2):
        for j in range(2):
            total = None
            for v2 in range(2):
                taps = jnp.concatenate(
                    [d2[2 * rp + r, 2 * j + v2 + v] for r in range(4) for v in range(3)], axis=1
                )
                level = relu(dot(taps, two_ref[...])).astype(BF16)
                part = dot(level, down3_ref[v2])
                total = part if total is None else total + part
            put(d3, rp, j, relu(total) * mask2, 1)

    copies[1].wait()
    copies[2].wait()
    total = None
    for i in range(2):
        for j in range(2):
            taps = jnp.concatenate(
                [d3[i + u, j + v] for u in range(3) for v in range(3)], axis=1
            )
            level = relu(dot(taps, three_ref[...])).astype(BF16)
            part = dot(level, down4_ref[i * 2 + j])
            total = part if total is None else total + part
    put(d4, 0, 0, relu(total) * mask4, 0)

    copies[3].wait()
    first, count = HALO * WIDE, NWIN * WIDE
    taps = jnp.concatenate(
        [d4[u, v, first:first + count] for u in range(3) for v in range(3)], axis=1
    )
    flat[...] = relu(dot(taps, four_ref[...]))
    for w in range(NWIN):
        start = w * WIDE + HALO
        out_ref[w] = flat[start:start + SPOTS].astype(BF16)


def encoder(main, halos, mask, one, down2, two, down3, three, down4, four):
    vmem = pl.BlockSpec(memory_space=pltpu.VMEM)
    hbm = pl.BlockSpec(memory_space=pl.ANY)
    return pl.pallas_call(
        encoder_kernel,
        in_specs=[vmem] * 10 + [hbm] * 4,
        out_specs=vmem,
        out_shape=jax.ShapeDtypeStruct((NWIN, SPOTS, four.shape[-1]), BF16),
        scratch_shapes=[
            pltpu.VMEM((TALL, 160, 128), BF16),
            pltpu.VMEM((TALL, 160, 128), BF16),
            pltpu.VMEM((PHASES + 2, POINTS, 128), BF16),
            pltpu.VMEM((PHASES + 2, POINTS, 128), BF16),
            pltpu.VMEM((6, 6, POINTS, 128), BF16),
            pltpu.VMEM((4, 4, POINTS, 256), BF16),
            pltpu.VMEM((3, 3, POINTS, 512), BF16),
            pltpu.VMEM((NWIN * WIDE, 512), F32),
            pltpu.VMEM(down3.shape, BF16),
            pltpu.VMEM(three.shape, BF16),
            pltpu.VMEM(down4.shape, BF16),
            pltpu.VMEM(four.shape, BF16),
            pltpu.SemaphoreType.DMA((4,)),
        ],
        compiler_params=pltpu.CompilerParams(vmem_limit_bytes=VMEM_BYTES),
        name="encoder",
    )(
        main, *halos, jnp.asarray(spread_matrix(), BF16), mask, one, down2,
        two, down3, three, down4, four,
    )


def level_one_weights(kernel):
    kernel = jnp.pad(kernel, ((0, 0), (0, 0), (0, 16 - BANDS), (0, 0)))
    columns = []
    for rb in range(2):
        for i in range(2):
            for j in range(2):
                top = 1 + 2 * rb + i
                wide = jnp.pad(kernel, ((top, 5 - top), (j, 1 - j), (0, 0), (0, 0)))
                columns.append(wide.transpose(1, 0, 2, 3).reshape(4 * 8 * 16, -1))
    return jnp.concatenate(columns, axis=1)


def level_two_weights(kernel):
    none = ((0, 0),) * 3
    pair = [jnp.pad(kernel, ((i, 1 - i),) + none) for i in range(2)]
    return jnp.concatenate(pair, axis=3).reshape(12 * kernel.shape[2], -1)


def inside_map():
    across, down = lax.axis_size("tx"), lax.axis_size("ty")
    x, y = lax.axis_index("tx"), lax.axis_index("ty")
    w = jnp.arange(TALL)[:, None, None]
    a = jnp.arange(WIDE)[None, :, None]
    rows = ((w >= HALO) | (y > 0)) & ((w < HALO + NWIN) | (y < down - 1))
    cols = ((a >= HALO) | (x > 0)) & ((a < HALO + SPOTS) | (x < across - 1))
    return jnp.broadcast_to(rows & cols, (TALL, WIDE, 128)).reshape(POINTS, 128).astype(F32)


def body(
    granule_blocks, row_weights, column_bank, destination, window_index, bank_index,
    kernel_one, reduce_two, kernel_two, reduce_three, kernel_three, reduce_four, kernel_four,
):
    axes = ("tx", "ty")
    tiles = lax.axis_size("tx") * lax.axis_size("ty")
    slots, slot_windows = resample(
        granule_blocks, row_weights, column_bank, destination, window_index, bank_index, tiles
    )
    received = lax.all_to_all(
        slots.reshape(tiles, CAP, LINES, TILE_COLS), axes, split_axis=0, concat_axis=0, tiled=True
    ).reshape(tiles * CAP, LINES, TILE_COLS)
    windows = lax.all_gather(slot_windows.reshape(tiles, CAP), axes, axis=0)
    me = lax.axis_index(axes)
    windows = lax.dynamic_index_in_dim(windows, me, axis=1, keepdims=False).reshape(-1)
    gridded, main, left, right = grid(received, windows)
    halos = exchange(main, left, right)
    flat = encoder(
        main, halos, inside_map(),
        level_one_weights(kernel_one),
        reduce_two.reshape(256, 128),
        level_two_weights(kernel_two),
        reduce_three.transpose(1, 0, 2, 3).reshape(2, 256, 256),
        kernel_three.reshape(9 * 256, 256),
        reduce_four.reshape(4, 256, 512),
        kernel_four.reshape(9 * 512, 512),
    )
    return gridded, flat.transpose(2, 0, 1)


def solution(mesh):
    both = P(("tx", "ty"))
    in_specs = (both, both, P(), both, both, both) + (P(),) * 7
    out_specs = (P(None, "ty", "tx"), P(None, "ty", "tx"))
    return jax.shard_map(body, mesh=mesh, in_specs=in_specs, out_specs=out_specs, check_vma=False)
```

```python
import functools

import jax
import jax.numpy as jnp
import numpy as np
from jax import lax
from jax.experimental import pallas as pl
from jax.experimental.pallas import tpu as pltpu
from jax.sharding import PartitionSpec as P

BF16 = jnp.bfloat16
F32 = jnp.float32
BANDS = 13
SRC_ROWS = 16
WIN_ROWS = 8
CAP = 2
NWIN = 32
TILE_COLS = 128
LINES = BANDS * WIN_ROWS
PACKED = CAP * LINES + WIN_ROWS
STEP_BLOCKS = 8
PHASES = 8
SPOTS = TILE_COLS // PHASES
HALO = 2
WIDE = SPOTS + 2 * HALO
TALL = NWIN + 2 * HALO
POINTS = WIDE * TALL
GROUP = 4
GROUP_POINTS = GROUP * WIDE
VMEM_BYTES = 60 * 1024 * 1024


def dot(a, b):
    return jnp.dot(a, b, preferred_element_type=F32)


def dot_nt(a, b):
    return lax.dot_general(a, b, (((1,), (1,)), ((), ())), preferred_element_type=F32)


def resample_kernel(
    dest_ref, win_ref, choice_ref, weight_ref, raw_ref, bank_ref, spread_ref, mask_ref,
    out_ref, slot_ref, slot_win_ref, held_ref, rows_ref,
):
    step = pl.program_id(0)
    tiles = held_ref.shape[0]

    @pl.when(step == 0)
    def _():
        def clear(i, carry):
            held_ref[i] = 0
            for k in range(CAP):
                slot_win_ref[i * CAP + k] = -1
            return carry

        lax.fori_loop(0, tiles, clear, 0)
        turned = jnp.transpose(weight_ref[...].astype(F32)).astype(BF16)
        blocks = turned.shape[0]
        for r in range(WIN_ROWS):
            wide = dot(turned, spread_ref[r])
            for h in range(2):
                rows_ref[h, pl.ds(r, blocks, stride=WIN_ROWS), :] = wide[:, h * 128:(h + 1) * 128]

    mask = mask_ref[...]
    rowed = []
    for j in range(STEP_BLOCKS):
        row = pl.multiple_of((step * STEP_BLOCKS + j) * WIN_ROWS, WIN_ROWS)
        rows = jnp.concatenate([rows_ref[h, pl.ds(row, WIN_ROWS), :] for h in range(2)], axis=1)
        weights = jnp.concatenate([rows] * BANDS, axis=0) * mask
        weights = weights.astype(BF16)[:, 0:BANDS * SRC_ROWS]
        rowed.append(dot(weights, raw_ref[j]).astype(BF16))
    for j in range(STEP_BLOCKS):
        n = step * STEP_BLOCKS + j
        tile = dest_ref[n]
        rank = held_ref[tile]
        held_ref[tile] = rank + 1
        slot = tile * CAP + rank
        slot_win_ref[slot] = win_ref[n]
        slot_ref[slot] = dot(rowed[j], bank_ref[choice_ref[n]]).astype(BF16)

    @pl.when(step == pl.num_programs(0) - 1)
    def _():
        lane = lax.broadcasted_iota(jnp.int32, (WIN_ROWS, TILE_COLS), 1)

        def pack(i, carry):
            window = jnp.where(lane == 0, slot_win_ref[i * CAP], slot_win_ref[i * CAP + 1])
            for k in range(CAP):
                out_ref[i, k * LINES:(k + 1) * LINES] = slot_ref[i * CAP + k]
            out_ref[i, CAP * LINES:] = window.astype(F32).astype(BF16)
            return carry

        lax.fori_loop(0, tiles, pack, 0)


def resample(granule_blocks, row_weights, column_bank, destination, window_index, bank_index, tiles):
    blocks = granule_blocks.shape[0]
    deep = BANDS * SRC_ROWS
    lane = np.arange(256)
    depth = np.arange(WIN_ROWS * SRC_ROWS)
    spread = np.stack(
        [
            (depth[:, None] == r * SRC_ROWS + lane[None, :] % SRC_ROWS) & (lane[None, :] < deep)
            for r in range(WIN_ROWS)
        ]
    )
    mask = lane[None, :] // SRC_ROWS == np.arange(LINES)[:, None] // WIN_ROWS
    return pl.pallas_call(
        resample_kernel,
        grid_spec=pltpu.PrefetchScalarGridSpec(
            num_scalar_prefetch=3,
            grid=(blocks // STEP_BLOCKS,),
            in_specs=[
                pl.BlockSpec((WIN_ROWS * SRC_ROWS, blocks), lambda i, *_: (0, 0)),
                pl.BlockSpec((STEP_BLOCKS, deep, TILE_COLS), lambda i, *_: (i, 0, 0)),
                pl.BlockSpec(column_bank.shape, lambda i, *_: (0, 0, 0)),
                pl.BlockSpec(spread.shape, lambda i, *_: (0, 0, 0)),
                pl.BlockSpec(mask.shape, lambda i, *_: (0, 0)),
            ],
            out_specs=pl.BlockSpec((tiles, PACKED, TILE_COLS), lambda i, *_: (0, 0, 0)),
            scratch_shapes=[
                pltpu.VMEM((tiles * CAP, LINES, TILE_COLS), BF16),
                pltpu.SMEM((tiles * CAP,), jnp.int32),
                pltpu.SMEM((tiles,), jnp.int32),
                pltpu.VMEM((2, blocks * WIN_ROWS, 128), F32),
            ],
        ),
        out_shape=jax.ShapeDtypeStruct((tiles, PACKED, TILE_COLS), BF16),
        compiler_params=pltpu.CompilerParams(vmem_limit_bytes=VMEM_BYTES),
        name="resample",
    )(
        destination, window_index, bank_index,
        row_weights.transpose(1, 2, 0).reshape(WIN_ROWS * SRC_ROWS, blocks),
        granule_blocks.reshape(blocks, deep, TILE_COLS),
        column_bank, jnp.asarray(spread, BF16), jnp.asarray(mask, F32),
    )


def grid_kernel(
    got_ref, perm_ref, grid_ref, main_ref, left_ref, right_ref,
    sum_ref, number_ref, win_ref, count_ref, sem,
):
    tiles = got_ref.shape[0]
    numbers = got_ref[:, CAP * LINES:, :].astype(F32)
    number_ref[...] = jnp.max(numbers, axis=1).astype(jnp.int32)
    copy = pltpu.make_async_copy(number_ref, win_ref, sem)
    copy.start()

    def clear(w, carry):
        sum_ref[w] = jnp.zeros(sum_ref.shape[1:], F32)
        count_ref[w] = 0
        return carry

    lax.fori_loop(0, NWIN + 1, clear, 0)
    copy.wait()

    def add(t, carry):
        for k in range(CAP):
            w = win_ref[t, k]
            w = jnp.where(w < 0, NWIN, w)
            block = got_ref[t, k * LINES:(k + 1) * LINES].astype(F32)
            sum_ref[w, 0:LINES] = sum_ref[w, 0:LINES] + block
            count_ref[w] = count_ref[w] + 1
        return carry

    lax.fori_loop(0, tiles, add, 0, unroll=2)

    def finish(group, carry):
        first = group * GROUP
        means = []
        for k in range(GROUP):
            w = first + k
            divisor = jnp.maximum(count_ref[w], 1).astype(F32)
            mean = (sum_ref[w, 0:LINES] / divisor).astype(BF16).astype(F32)
            sum_ref[w, 0:LINES] = mean
            means.append(mean)
        row = pl.multiple_of(first * WIN_ROWS, GROUP * WIN_ROWS)
        for b in range(BANDS):
            part = jnp.concatenate([m[b * WIN_ROWS:(b + 1) * WIN_ROWS] for m in means], axis=0)
            grid_ref[b, pl.ds(row, GROUP * WIN_ROWS), :] = part.astype(BF16)
        for pair in range(GROUP // 2):
            lines = jnp.concatenate(
                [
                    sum_ref[first + pair * 2 + k, pl.ds(r, 16, stride=WIN_ROWS), :]
                    for k in range(2)
                    for r in range(WIN_ROWS)
                ],
                axis=0,
            )
            both = dot_nt(perm_ref[...], lines.astype(BF16)).astype(BF16)
            for k in range(2):
                w = first + pair * 2 + k
                turned = both[:, k * 128:(k + 1) * 128]
                main_ref[pl.ds(pl.multiple_of(w * 128, 128), 128), :] = turned[0:128]
                left_ref[pl.ds(pl.multiple_of(w * 16, 16), 16), :] = turned[128:144]
                right_ref[pl.ds(pl.multiple_of(w * 16, 16), 16), :] = turned[144:160]
        return carry

    lax.fori_loop(0, NWIN // GROUP, finish, 0)


def grid(received):
    tiles = received.shape[0]
    perm = np.zeros((TILE_COLS + 32, TILE_COLS), np.float32)
    for p in range(PHASES):
        for a in range(SPOTS):
            perm[p * SPOTS + a, a * PHASES + p] = 1.0
        for a in range(HALO):
            perm[128 + p * HALO + a, a * PHASES + p] = 1.0
            perm[144 + p * HALO + a, (SPOTS - HALO + a) * PHASES + p] = 1.0
    vmem = pl.BlockSpec(memory_space=pltpu.VMEM)
    return pl.pallas_call(
        grid_kernel,
        in_specs=[vmem, vmem],
        out_specs=[vmem] * 4,
        out_shape=[
            jax.ShapeDtypeStruct((BANDS, NWIN * WIN_ROWS, TILE_COLS), BF16),
            jax.ShapeDtypeStruct((NWIN * 128, 128), BF16),
            jax.ShapeDtypeStruct((NWIN * 16, 128), BF16),
            jax.ShapeDtypeStruct((NWIN * 16, 128), BF16),
        ],
        scratch_shapes=[
            pltpu.VMEM((NWIN + 1, 128, TILE_COLS), F32),
            pltpu.VMEM((tiles, TILE_COLS), jnp.int32),
            pltpu.SMEM((tiles, TILE_COLS), jnp.int32),
            pltpu.SMEM((NWIN + 1,), jnp.int32),
            pltpu.SemaphoreType.DMA,
        ],
        compiler_params=pltpu.CompilerParams(vmem_limit_bytes=VMEM_BYTES),
        name="grid",
    )(received, jnp.asarray(perm, BF16))


def exchange(main, left, right):
    across, down = lax.axis_size("tx"), lax.axis_size("ty")
    right_ward = [(i, i + 1) for i in range(across - 1)]
    left_ward = [(t, s) for s, t in right_ward]
    down_ward = [(i, i + 1) for i in range(down - 1)]
    up_ward = [(t, s) for s, t in down_ward]
    from_left = lax.ppermute(right, "tx", right_ward)
    from_right = lax.ppermute(left, "tx", left_ward)
    m, h = HALO * 128, HALO * 16
    first = jnp.concatenate([main[:m], from_left[:h], from_right[:h]], axis=0)
    last = jnp.concatenate([main[-m:], from_left[-h:], from_right[-h:]], axis=0)
    from_above = lax.ppermute(last, "ty", down_ward)
    from_below = lax.ppermute(first, "ty", up_ward)
    return from_left, from_right, from_above, from_below


def spread_matrix():
    out = np.zeros((PHASES + 2, GROUP_POINTS, GROUP * 48), np.float32)
    for index in range(PHASES + 2):
        p = (index - 1) % PHASES
        shift = -1 if index == 0 else (1 if index == PHASES + 1 else 0)
        for k in range(GROUP):
            for a in range(WIDE):
                s = a + shift
                row = k * WIDE + a
                if s < 0 or s >= WIDE:
                    continue
                if s < HALO:
                    out[index, row, GROUP * 16 + k * 16 + p * HALO + s] = 1.0
                elif s < HALO + SPOTS:
                    out[index, row, k * 16 + s - HALO] = 1.0
                else:
                    out[index, row, GROUP * 32 + k * 16 + p * HALO + s - HALO - SPOTS] = 1.0
    return out


def relu(x):
    return jnp.maximum(x, 0.0)


def encoder_kernel(
    main_ref, fl_ref, fr_ref, above_ref, below_ref, spread_ref, one_ref, down2_ref,
    two_ref, down3_hbm, three_hbm, down4_hbm, four_hbm,
    out_ref,
    ext1, ext2, x1, x2, d2, d3, d4, flat, down3_ref, three_ref, down4_ref, four_ref, sems,
):
    copies = [
        pltpu.make_async_copy(src, dst, sems.at[i])
        for i, (src, dst) in enumerate(
            (
                (down3_hbm, down3_ref),
                (three_hbm, three_ref),
                (down4_hbm, down4_ref),
                (four_hbm, four_ref),
            )
        )
    ]
    for copy in copies:
        copy.start()

    for h in range(HALO):
        for source, w in ((above_ref, h), (below_ref, HALO + NWIN + h)):
            ext1[w, 0:128] = source[h * 128:(h + 1) * 128]
            base = HALO * 128 + h * 16
            ext1[w, 128:144] = source[base:base + 16]
            ext1[w, 144:160] = source[base + HALO * 16:base + HALO * 16 + 16]

    def gather(w, carry):
        ext1[w + HALO, 0:128] = main_ref[pl.ds(pl.multiple_of(w * 128, 128), 128), :]
        ext1[w + HALO, 128:144] = fl_ref[pl.ds(pl.multiple_of(w * 16, 16), 16), :]
        ext1[w + HALO, 144:160] = fr_ref[pl.ds(pl.multiple_of(w * 16, 16), 16), :]
        return carry

    lax.fori_loop(0, NWIN, gather, 0)

    low = lax.broadcasted_iota(jnp.int32, (160, 128), 1) < 64

    def lower(w, carry):
        after = jnp.minimum(w + 1, TALL - 1)
        both = jnp.where(low, ext1[after].astype(F32), ext1[w].astype(F32))
        ext2[w] = pltpu.roll(both, 64, 1).astype(BF16)
        return carry

    lax.fori_loop(0, TALL, lower, 0)

    def place(g, carry):
        row = pl.multiple_of(g * GROUP_POINTS, GROUP_POINTS)
        for index in range(PHASES + 2):
            p = (index - 1) % PHASES
            sides = []
            for ext in (ext1, ext2):
                pieces = [ext[g * GROUP + k, p * 16:(p + 1) * 16] for k in range(GROUP)]
                pieces += [ext[g * GROUP + k, 128:144] for k in range(GROUP)]
                pieces += [ext[g * GROUP + k, 144:160] for k in range(GROUP)]
                sides.append(jnp.concatenate(pieces, axis=0))
            laid = dot(spread_ref[index], jnp.concatenate(sides, axis=1)).astype(BF16)
            x1[index, pl.ds(row, GROUP_POINTS), :] = laid[:, 0:128]
            x2[index, pl.ds(row, GROUP_POINTS), :] = laid[:, 128:256]
        return carry

    lax.fori_loop(0, TALL // GROUP, place, 0)

    across, below = lax.axis_size("tx"), lax.axis_size("ty")
    x, y = lax.axis_index("tx"), lax.axis_index("ty")
    least_w, most_w = jnp.where(y > 0, 0, HALO), jnp.where(y < below - 1, TALL, HALO + NWIN)
    least_a, most_a = jnp.where(x > 0, 0, HALO), jnp.where(x < across - 1, WIDE, HALO + SPOTS)
    point = lax.broadcasted_iota(jnp.int32, (POINTS, 128), 0)
    w = (point * (65536 // WIDE + 1)) >> 16
    a = point - w * WIDE
    inside = (w >= least_w) & (w < most_w) & (a >= least_a) & (a < most_a)
    mask = inside.astype(F32)
    mask2 = jnp.concatenate([mask, mask], axis=1)
    mask4 = jnp.concatenate([mask2, mask2], axis=1)

    def put(dst, i, j, value, last):
        rows = [(i + 1, 0)]
        if i == last:
            rows.append((0, WIDE))
        if i == 0:
            rows.append((last + 2, -WIDE))
        cols = [(j + 1, 0)]
        if j == last:
            cols.append((0, 1))
        if j == 0:
            cols.append((last + 2, -1))
        for r, row_shift in rows:
            for c, col_shift in cols:
                shift = (row_shift + col_shift) % POINTS
                moved = pltpu.roll(value, shift, 0) if shift else value
                dst[r, c] = moved.astype(BF16)

    for cb in range(4):
        for version, x in enumerate((x1, x2)):
            taps = jnp.concatenate([x[2 * cb + k] for k in range(4)], axis=1)
            level = relu(dot(taps, one_ref[...])).astype(BF16)
            for half in range(2):
                down = relu(dot(level[:, half * 256:(half + 1) * 256], down2_ref[...]))
                if version == 0:
                    rb = 1 + half
                elif half == 0:
                    rb = 3
                else:
                    rb = 0
                    down = pltpu.roll(down, WIDE, 0)
                put(d2, rb, cb, down * mask, 3)

    copies[0].wait()
    for rp in range(2):
        for j in range(2):
            total = None
            for v2 in range(2):
                taps = jnp.concatenate(
                    [d2[2 * rp + r, 2 * j + v2 + v] for r in range(4) for v in range(3)], axis=1
                )
                level = relu(dot(taps, two_ref[...])).astype(BF16)
                part = dot(level, down3_ref[v2])
                total = part if total is None else total + part
            put(d3, rp, j, relu(total) * mask2, 1)

    copies[1].wait()
    copies[2].wait()
    total = None
    for i in range(2):
        for j in range(2):
            taps = jnp.concatenate(
                [d3[i + u, j + v] for u in range(3) for v in range(3)], axis=1
            )
            level = relu(dot(taps, three_ref[...])).astype(BF16)
            part = dot(level, down4_ref[i * 2 + j])
            total = part if total is None else total + part
    put(d4, 0, 0, relu(total) * mask4, 0)

    copies[3].wait()
    first, count = HALO * WIDE, NWIN * WIDE
    taps = jnp.concatenate(
        [d4[u, v, first:first + count] for u in range(3) for v in range(3)], axis=1
    )
    flat[...] = relu(dot(taps, four_ref[...]))
    for w in range(NWIN):
        start = w * WIDE + HALO
        out_ref[w] = flat[start:start + SPOTS].astype(BF16)


def encoder(main, halos, one, down2, two, down3, three, down4, four):
    vmem = pl.BlockSpec(memory_space=pltpu.VMEM)
    hbm = pl.BlockSpec(memory_space=pl.ANY)
    return pl.pallas_call(
        encoder_kernel,
        in_specs=[vmem] * 9 + [hbm] * 4,
        out_specs=vmem,
        out_shape=jax.ShapeDtypeStruct((NWIN, SPOTS, four.shape[-1]), BF16),
        scratch_shapes=[
            pltpu.VMEM((TALL, 160, 128), BF16),
            pltpu.VMEM((TALL, 160, 128), BF16),
            pltpu.VMEM((PHASES + 2, POINTS, 128), BF16),
            pltpu.VMEM((PHASES + 2, POINTS, 128), BF16),
            pltpu.VMEM((6, 6, POINTS, 128), BF16),
            pltpu.VMEM((4, 4, POINTS, 256), BF16),
            pltpu.VMEM((3, 3, POINTS, 512), BF16),
            pltpu.VMEM((NWIN * WIDE, 512), F32),
            pltpu.VMEM(down3.shape, BF16),
            pltpu.VMEM(three.shape, BF16),
            pltpu.VMEM(down4.shape, BF16),
            pltpu.VMEM(four.shape, BF16),
            pltpu.SemaphoreType.DMA((4,)),
        ],
        compiler_params=pltpu.CompilerParams(vmem_limit_bytes=VMEM_BYTES),
        name="encoder",
    )(
        main, *halos, jnp.asarray(spread_matrix(), BF16), one, down2,
        two, down3, three, down4, four,
    )


def level_one_weights(kernel):
    kernel = jnp.pad(kernel, ((0, 0), (0, 0), (0, 16 - BANDS), (0, 0)))
    columns = []
    for rb in range(2):
        for i in range(2):
            for j in range(2):
                top = 1 + 2 * rb + i
                wide = jnp.pad(kernel, ((top, 5 - top), (j, 1 - j), (0, 0), (0, 0)))
                columns.append(wide.transpose(1, 0, 2, 3).reshape(4 * 8 * 16, -1))
    return jnp.concatenate(columns, axis=1)


def level_two_weights(kernel):
    none = ((0, 0),) * 3
    pair = [jnp.pad(kernel, ((i, 1 - i),) + none) for i in range(2)]
    return jnp.concatenate(pair, axis=3).reshape(12 * kernel.shape[2], -1)


def body(
    granule_blocks, row_weights, column_bank, destination, window_index, bank_index,
    kernel_one, reduce_two, kernel_two, reduce_three, kernel_three, reduce_four, kernel_four,
):
    axes = ("tx", "ty")
    tiles = lax.axis_size("tx") * lax.axis_size("ty")
    slots = resample(
        granule_blocks, row_weights, column_bank, destination, window_index, bank_index, tiles
    )
    received = lax.all_to_all(slots, axes, split_axis=0, concat_axis=0, tiled=True)
    gridded, main, left, right = grid(received)
    halos = exchange(main, left, right)
    flat = encoder(
        main, halos,
        level_one_weights(kernel_one),
        reduce_two.reshape(256, 128),
        level_two_weights(kernel_two),
        reduce_three.transpose(1, 0, 2, 3).reshape(2, 256, 256),
        kernel_three.reshape(9 * 256, 256),
        reduce_four.reshape(4, 256, 512),
        kernel_four.reshape(9 * 512, 512),
    )
    return gridded, flat.transpose(2, 0, 1)


def solution(mesh):
    both = P(("tx", "ty"))
    in_specs = (both, both, P(), both, both, both) + (P(),) * 7
    out_specs = (P(None, "ty", "tx"), P(None, "ty", "tx"))
    return jax.shard_map(body, mesh=mesh, in_specs=in_specs, out_specs=out_specs, check_vma=False)
```

```python
import functools

import jax
import jax.numpy as jnp
import numpy as np
from jax import lax
from jax.experimental import pallas as pl
from jax.experimental.pallas import tpu as pltpu
from jax.sharding import PartitionSpec as P

BF16 = jnp.bfloat16
F32 = jnp.float32
BANDS = 13
SRC_ROWS = 16
WIN_ROWS = 8
CAP = 2
NWIN = 32
TILE_COLS = 128
LINES = BANDS * WIN_ROWS
STEP_BLOCKS = 16
PHASES = 8
SPOTS = TILE_COLS // PHASES
HALO = 2
WIDE = SPOTS + 2 * HALO
TALL = NWIN + 2 * HALO
POINTS = WIDE * TALL
GROUP = 4
GROUP_POINTS = GROUP * WIDE
VMEM_BYTES = 60 * 1024 * 1024


def dot(a, b):
    return jnp.dot(a, b, preferred_element_type=F32)


def dot_nt(a, b):
    return lax.dot_general(a, b, (((1,), (1,)), ((), ())), preferred_element_type=F32)


def resample_kernel(
    chosen, dest_ref, win_ref, choice_ref, weight_ref, raw_hbm, bank_ref, out_ref,
    raw_ref, rows_ref, held_ref, block_ref, slot_win_ref, sems,
):
    tiles, blocks = held_ref.shape[0], dest_ref.shape[0]
    deep = BANDS * SRC_ROWS

    def clear(i, carry):
        held_ref[i] = 0
        block_ref[i] = 0
        for k in range(CAP):
            slot_win_ref[i * CAP + k] = -1
        return carry

    lax.fori_loop(0, tiles, clear, 0, unroll=4)

    def find(n, carry):
        tile = dest_ref[n]
        rank = held_ref[tile]
        held_ref[tile] = rank + 1
        slot_win_ref[tile * CAP + rank] = win_ref[n]
        block_ref[tile] = jnp.where(rank == chosen, n, block_ref[tile])
        return carry

    lax.fori_loop(0, blocks, find, 0, unroll=4)

    def fetch(t):
        return pltpu.make_async_copy(raw_hbm.at[block_ref[t]], raw_ref.at[t], sems.at[t])

    def start(t, carry):
        fetch(t).start()
        return carry

    lax.fori_loop(0, tiles, start, 0)

    turned = jnp.transpose(weight_ref[...].astype(F32)).astype(BF16)
    depth = lax.broadcasted_iota(jnp.int32, (WIN_ROWS * SRC_ROWS, 256), 0)
    lane = lax.broadcasted_iota(jnp.int32, (WIN_ROWS * SRC_ROWS, 256), 1)
    offset = depth - (lane & (SRC_ROWS - 1))
    for r in range(WIN_ROWS):
        wide = dot(turned, (offset == r * SRC_ROWS).astype(F32).astype(BF16))
        for h in range(2):
            rows_ref[h, pl.ds(r, blocks, stride=WIN_ROWS), :] = wide[:, h * 128:(h + 1) * 128]

    line = lax.broadcasted_iota(jnp.int32, (LINES, 256), 0)
    lane = lax.broadcasted_iota(jnp.int32, (LINES, 256), 1)
    own = (line >> 3) == (lane >> 4)
    spot = lax.broadcasted_iota(jnp.int32, (WIN_ROWS, TILE_COLS), 1)

    def work(group, carry):
        rowed = []
        for j in range(STEP_BLOCKS):
            t = group * STEP_BLOCKS + j
            fetch(t).wait()
            row = pl.multiple_of(block_ref[t] * WIN_ROWS, WIN_ROWS)
            rows = jnp.concatenate(
                [rows_ref[h, pl.ds(row, WIN_ROWS), :] for h in range(2)], axis=1
            )
            weights = jnp.where(own, jnp.concatenate([rows] * BANDS, axis=0), 0.0)
            rowed.append(dot(weights.astype(BF16)[:, 0:deep], raw_ref[t]).astype(BF16))
        for j in range(STEP_BLOCKS):
            t = group * STEP_BLOCKS + j
            bank = bank_ref[choice_ref[block_ref[t]]]
            out_ref[t, 0:LINES] = dot(rowed[j], bank).astype(BF16)
            if chosen == 0:
                window = jnp.where(spot == 0, slot_win_ref[t * CAP], slot_win_ref[t * CAP + 1])
                out_ref[t, LINES:] = window.astype(F32).astype(BF16)
        return carry

    lax.fori_loop(0, tiles // STEP_BLOCKS, work, 0)


def resample(
    chosen, granule_blocks, row_weights, column_bank, destination, window_index, bank_index, tiles
):
    blocks = granule_blocks.shape[0]
    deep = BANDS * SRC_ROWS
    height = LINES + (WIN_ROWS if chosen == 0 else 0)
    vmem = pl.BlockSpec(memory_space=pltpu.VMEM)
    smem = pl.BlockSpec(memory_space=pltpu.SMEM)
    return pl.pallas_call(
        functools.partial(resample_kernel, chosen),
        in_specs=[smem, smem, smem, vmem, pl.BlockSpec(memory_space=pl.ANY), vmem],
        out_specs=vmem,
        scratch_shapes=[
            pltpu.VMEM((tiles, deep, TILE_COLS), BF16),
            pltpu.VMEM((2, blocks * WIN_ROWS, 128), F32),
            pltpu.SMEM((tiles,), jnp.int32),
            pltpu.SMEM((tiles,), jnp.int32),
            pltpu.SMEM((tiles * CAP,), jnp.int32),
            pltpu.SemaphoreType.DMA((tiles,)),
        ],
        out_shape=jax.ShapeDtypeStruct((tiles, height, TILE_COLS), BF16),
        compiler_params=pltpu.CompilerParams(vmem_limit_bytes=VMEM_BYTES),
        cost_estimate=pl.CostEstimate(
            flops=2 * tiles * LINES * 128 * 384,
            bytes_accessed=tiles * 80000 * 8,
            transcendentals=0,
        ),
        name=f"resample_{chosen}",
    )(
        destination, window_index, bank_index,
        row_weights.transpose(1, 2, 0).reshape(WIN_ROWS * SRC_ROWS, blocks),
        granule_blocks.reshape(blocks, deep, TILE_COLS),
        column_bank,
    )


def grid_kernel(
    got0_ref, got1_ref, perm_ref, grid_ref, main_ref, left_ref, right_ref,
    sum_ref, number_ref, win_ref, count_ref, sem,
):
    tiles = got0_ref.shape[0]
    numbers = got0_ref[:, LINES:, :].astype(F32)
    number_ref[...] = jnp.max(numbers, axis=1).astype(jnp.int32)
    copy = pltpu.make_async_copy(number_ref, win_ref, sem)
    copy.start()

    def clear(w, carry):
        sum_ref[w] = jnp.zeros(sum_ref.shape[1:], F32)
        count_ref[w] = 0
        return carry

    lax.fori_loop(0, NWIN + 1, clear, 0)
    copy.wait()

    def add(t, carry):
        for k, got_ref in enumerate((got0_ref, got1_ref)):
            w = win_ref[t, k]
            w = jnp.where(w < 0, NWIN, w)
            block = got_ref[t, 0:LINES].astype(F32)
            sum_ref[w, 0:LINES] = sum_ref[w, 0:LINES] + block
            count_ref[w] = count_ref[w] + 1
        return carry

    lax.fori_loop(0, tiles, add, 0, unroll=2)

    def finish(group, carry):
        first = group * GROUP
        means = []
        for k in range(GROUP):
            w = first + k
            divisor = jnp.maximum(count_ref[w], 1).astype(F32)
            mean = (sum_ref[w, 0:LINES] / divisor).astype(BF16).astype(F32)
            sum_ref[w, 0:LINES] = mean
            means.append(mean)
        row = pl.multiple_of(first * WIN_ROWS, GROUP * WIN_ROWS)
        for b in range(BANDS):
            part = jnp.concatenate([m[b * WIN_ROWS:(b + 1) * WIN_ROWS] for m in means], axis=0)
            grid_ref[b, pl.ds(row, GROUP * WIN_ROWS), :] = part.astype(BF16)
        for pair in range(GROUP // 2):
            lines = jnp.concatenate(
                [
                    sum_ref[first + pair * 2 + k, pl.ds(r, 16, stride=WIN_ROWS), :]
                    for k in range(2)
                    for r in range(WIN_ROWS)
                ],
                axis=0,
            )
            both = dot_nt(perm_ref[...], lines.astype(BF16)).astype(BF16)
            for k in range(2):
                w = first + pair * 2 + k
                turned = both[:, k * 128:(k + 1) * 128]
                main_ref[pl.ds(pl.multiple_of(w * 128, 128), 128), :] = turned[0:128]
                left_ref[pl.ds(pl.multiple_of(w * 16, 16), 16), :] = turned[128:144]
                right_ref[pl.ds(pl.multiple_of(w * 16, 16), 16), :] = turned[144:160]
        return carry

    lax.fori_loop(0, NWIN // GROUP, finish, 0)


def grid(first, second):
    tiles = first.shape[0]
    perm = np.zeros((TILE_COLS + 32, TILE_COLS), np.float32)
    for p in range(PHASES):
        for a in range(SPOTS):
            perm[p * SPOTS + a, a * PHASES + p] = 1.0
        for a in range(HALO):
            perm[128 + p * HALO + a, a * PHASES + p] = 1.0
            perm[144 + p * HALO + a, (SPOTS - HALO + a) * PHASES + p] = 1.0
    vmem = pl.BlockSpec(memory_space=pltpu.VMEM)
    return pl.pallas_call(
        grid_kernel,
        in_specs=[vmem] * 3,
        out_specs=[vmem] * 4,
        out_shape=[
            jax.ShapeDtypeStruct((BANDS, NWIN * WIN_ROWS, TILE_COLS), BF16),
            jax.ShapeDtypeStruct((NWIN * 128, 128), BF16),
            jax.ShapeDtypeStruct((NWIN * 16, 128), BF16),
            jax.ShapeDtypeStruct((NWIN * 16, 128), BF16),
        ],
        scratch_shapes=[
            pltpu.VMEM((NWIN + 1, 128, TILE_COLS), F32),
            pltpu.VMEM((tiles, TILE_COLS), jnp.int32),
            pltpu.SMEM((tiles, TILE_COLS), jnp.int32),
            pltpu.SMEM((NWIN + 1,), jnp.int32),
            pltpu.SemaphoreType.DMA,
        ],
        compiler_params=pltpu.CompilerParams(vmem_limit_bytes=VMEM_BYTES),
        name="grid",
    )(first, second, jnp.asarray(perm, BF16))


def exchange(main, left, right):
    across, down = lax.axis_size("tx"), lax.axis_size("ty")
    right_ward = [(i, i + 1) for i in range(across - 1)]
    left_ward = [(t, s) for s, t in right_ward]
    down_ward = [(i, i + 1) for i in range(down - 1)]
    up_ward = [(t, s) for s, t in down_ward]
    from_left = lax.ppermute(right, "tx", right_ward)
    from_right = lax.ppermute(left, "tx", left_ward)
    m, h = HALO * 128, HALO * 16
    first = jnp.concatenate([main[:m], from_left[:h], from_right[:h]], axis=0)
    last = jnp.concatenate([main[-m:], from_left[-h:], from_right[-h:]], axis=0)
    from_above = lax.ppermute(last, "ty", down_ward)
    from_below = lax.ppermute(first, "ty", up_ward)
    return from_left, from_right, from_above, from_below


def spread_matrix():
    out = np.zeros((PHASES + 2, GROUP_POINTS, GROUP * 48), np.float32)
    for index in range(PHASES + 2):
        p = (index - 1) % PHASES
        shift = -1 if index == 0 else (1 if index == PHASES + 1 else 0)
        for k in range(GROUP):
            for a in range(WIDE):
                s = a + shift
                row = k * WIDE + a
                if s < 0 or s >= WIDE:
                    continue
                if s < HALO:
                    out[index, row, GROUP * 16 + k * 16 + p * HALO + s] = 1.0
                elif s < HALO + SPOTS:
                    out[index, row, k * 16 + s - HALO] = 1.0
                else:
                    out[index, row, GROUP * 32 + k * 16 + p * HALO + s - HALO - SPOTS] = 1.0
    return out


def relu(x):
    return jnp.maximum(x, 0.0)


def encoder_kernel(
    main_ref, fl_ref, fr_ref, above_ref, below_ref, spread_ref, one_ref, down2_ref,
    two_ref, down3_hbm, three_hbm, down4_hbm, four_hbm,
    out_ref,
    ext1, ext2, x1, x2, d2, d3, d4, flat, down3_ref, three_ref, down4_ref, four_ref, sems,
):
    copies = [
        pltpu.make_async_copy(src, dst, sems.at[i])
        for i, (src, dst) in enumerate(
            (
                (down3_hbm, down3_ref),
                (three_hbm, three_ref),
                (down4_hbm, down4_ref),
                (four_hbm, four_ref),
            )
        )
    ]
    for copy in copies:
        copy.start()

    for h in range(HALO):
        for source, w in ((above_ref, h), (below_ref, HALO + NWIN + h)):
            ext1[w, 0:128] = source[h * 128:(h + 1) * 128]
            base = HALO * 128 + h * 16
            ext1[w, 128:144] = source[base:base + 16]
            ext1[w, 144:160] = source[base + HALO * 16:base + HALO * 16 + 16]

    def gather(w, carry):
        ext1[w + HALO, 0:128] = main_ref[pl.ds(pl.multiple_of(w * 128, 128), 128), :]
        ext1[w + HALO, 128:144] = fl_ref[pl.ds(pl.multiple_of(w * 16, 16), 16), :]
        ext1[w + HALO, 144:160] = fr_ref[pl.ds(pl.multiple_of(w * 16, 16), 16), :]
        return carry

    lax.fori_loop(0, NWIN, gather, 0)

    low = lax.broadcasted_iota(jnp.int32, (160, 128), 1) < 64

    def lower(w, carry):
        after = jnp.minimum(w + 1, TALL - 1)
        both = jnp.where(low, ext1[after].astype(F32), ext1[w].astype(F32))
        ext2[w] = pltpu.roll(both, 64, 1).astype(BF16)
        return carry

    lax.fori_loop(0, TALL, lower, 0)

    def place(g, carry):
        row = pl.multiple_of(g * GROUP_POINTS, GROUP_POINTS)
        for index in range(PHASES + 2):
            p = (index - 1) % PHASES
            sides = []
            for ext in (ext1, ext2):
                pieces = [ext[g * GROUP + k, p * 16:(p + 1) * 16] for k in range(GROUP)]
                pieces += [ext[g * GROUP + k, 128:144] for k in range(GROUP)]
                pieces += [ext[g * GROUP + k, 144:160] for k in range(GROUP)]
                sides.append(jnp.concatenate(pieces, axis=0))
            laid = dot(spread_ref[index], jnp.concatenate(sides, axis=1)).astype(BF16)
            x1[index, pl.ds(row, GROUP_POINTS), :] = laid[:, 0:128]
            x2[index, pl.ds(row, GROUP_POINTS), :] = laid[:, 128:256]
        return carry

    lax.fori_loop(0, TALL // GROUP, place, 0)

    across, below = lax.axis_size("tx"), lax.axis_size("ty")
    x, y = lax.axis_index("tx"), lax.axis_index("ty")
    least_w, most_w = jnp.where(y > 0, 0, HALO), jnp.where(y < below - 1, TALL, HALO + NWIN)
    least_a, most_a = jnp.where(x > 0, 0, HALO), jnp.where(x < across - 1, WIDE, HALO + SPOTS)
    point = lax.broadcasted_iota(jnp.int32, (POINTS, 128), 0)
    w = (point * (65536 // WIDE + 1)) >> 16
    a = point - w * WIDE
    inside = (w >= least_w) & (w < most_w) & (a >= least_a) & (a < most_a)
    mask = inside.astype(F32)
    mask2 = jnp.concatenate([mask, mask], axis=1)
    mask4 = jnp.concatenate([mask2, mask2], axis=1)

    def put(dst, i, j, value, last):
        rows = [(i + 1, 0)]
        if i == last:
            rows.append((0, WIDE))
        if i == 0:
            rows.append((last + 2, -WIDE))
        cols = [(j + 1, 0)]
        if j == last:
            cols.append((0, 1))
        if j == 0:
            cols.append((last + 2, -1))
        for r, row_shift in rows:
            for c, col_shift in cols:
                shift = (row_shift + col_shift) % POINTS
                moved = pltpu.roll(value, shift, 0) if shift else value
                dst[r, c] = moved.astype(BF16)

    for cb in range(4):
        for version, x in enumerate((x1, x2)):
            taps = jnp.concatenate([x[2 * cb + k] for k in range(4)], axis=1)
            level = relu(dot(taps, one_ref[...])).astype(BF16)
            for half in range(2):
                down = relu(dot(level[:, half * 256:(half + 1) * 256], down2_ref[...]))
                if version == 0:
                    rb = 1 + half
                elif half == 0:
                    rb = 3
                else:
                    rb = 0
                    down = pltpu.roll(down, WIDE, 0)
                put(d2, rb, cb, down * mask, 3)

    copies[0].wait()
    for rp in range(2):
        for j in range(2):
            total = None
            for v2 in range(2):
                taps = jnp.concatenate(
                    [d2[2 * rp + r, 2 * j + v2 + v] for r in range(4) for v in range(3)], axis=1
                )
                level = relu(dot(taps, two_ref[...])).astype(BF16)
                part = dot(level, down3_ref[v2])
                total = part if total is None else total + part
            put(d3, rp, j, relu(total) * mask2, 1)

    copies[1].wait()
    copies[2].wait()
    total = None
    for i in range(2):
        for j in range(2):
            taps = jnp.concatenate(
                [d3[i + u, j + v] for u in range(3) for v in range(3)], axis=1
            )
            level = relu(dot(taps, three_ref[...])).astype(BF16)
            part = dot(level, down4_ref[i * 2 + j])
            total = part if total is None else total + part
    put(d4, 0, 0, relu(total) * mask4, 0)

    copies[3].wait()
    first, count = HALO * WIDE, NWIN * WIDE
    taps = jnp.concatenate(
        [d4[u, v, first:first + count] for u in range(3) for v in range(3)], axis=1
    )
    flat[...] = relu(dot(taps, four_ref[...]))
    for w in range(NWIN):
        start = w * WIDE + HALO
        out_ref[w] = flat[start:start + SPOTS].astype(BF16)


def encoder(main, halos, one, down2, two, down3, three, down4, four):
    vmem = pl.BlockSpec(memory_space=pltpu.VMEM)
    hbm = pl.BlockSpec(memory_space=pl.ANY)
    return pl.pallas_call(
        encoder_kernel,
        in_specs=[vmem] * 9 + [hbm] * 4,
        out_specs=vmem,
        out_shape=jax.ShapeDtypeStruct((NWIN, SPOTS, four.shape[-1]), BF16),
        scratch_shapes=[
            pltpu.VMEM((TALL, 160, 128), BF16),
            pltpu.VMEM((TALL, 160, 128), BF16),
            pltpu.VMEM((PHASES + 2, POINTS, 128), BF16),
            pltpu.VMEM((PHASES + 2, POINTS, 128), BF16),
            pltpu.VMEM((6, 6, POINTS, 128), BF16),
            pltpu.VMEM((4, 4, POINTS, 256), BF16),
            pltpu.VMEM((3, 3, POINTS, 512), BF16),
            pltpu.VMEM((NWIN * WIDE, 512), F32),
            pltpu.VMEM(down3.shape, BF16),
            pltpu.VMEM(three.shape, BF16),
            pltpu.VMEM(down4.shape, BF16),
            pltpu.VMEM(four.shape, BF16),
            pltpu.SemaphoreType.DMA((4,)),
        ],
        compiler_params=pltpu.CompilerParams(vmem_limit_bytes=VMEM_BYTES),
        name="encoder",
    )(
        main, *halos, jnp.asarray(spread_matrix(), BF16), one, down2,
        two, down3, three, down4, four,
    )


def level_one_weights(kernel):
    kernel = jnp.pad(kernel, ((0, 0), (0, 0), (0, 16 - BANDS), (0, 0)))
    columns = []
    for rb in range(2):
        for i in range(2):
            for j in range(2):
                top = 1 + 2 * rb + i
                wide = jnp.pad(kernel, ((top, 5 - top), (j, 1 - j), (0, 0), (0, 0)))
                columns.append(wide.transpose(1, 0, 2, 3).reshape(4 * 8 * 16, -1))
    return jnp.concatenate(columns, axis=1)


def level_two_weights(kernel):
    none = ((0, 0),) * 3
    pair = [jnp.pad(kernel, ((i, 1 - i),) + none) for i in range(2)]
    return jnp.concatenate(pair, axis=3).reshape(12 * kernel.shape[2], -1)


def body(
    granule_blocks, row_weights, column_bank, destination, window_index, bank_index,
    kernel_one, reduce_two, kernel_two, reduce_three, kernel_three, reduce_four, kernel_four,
):
    axes = ("tx", "ty")
    tiles = lax.axis_size("tx") * lax.axis_size("ty")
    received = [
        lax.all_to_all(
            resample(
                chosen, granule_blocks, row_weights, column_bank, destination, window_index,
                bank_index, tiles,
            ),
            axes, split_axis=0, concat_axis=0, tiled=True,
        )
        for chosen in range(CAP)
    ]
    gridded, main, left, right = grid(*received)
    halos = exchange(main, left, right)
    flat = encoder(
        main, halos,
        level_one_weights(kernel_one),
        reduce_two.reshape(256, 128),
        level_two_weights(kernel_two),
        reduce_three.transpose(1, 0, 2, 3).reshape(2, 256, 256),
        kernel_three.reshape(9 * 256, 256),
        reduce_four.reshape(4, 256, 512),
        kernel_four.reshape(9 * 512, 512),
    )
    return gridded, flat.transpose(2, 0, 1)


def solution(mesh):
    both = P(("tx", "ty"))
    in_specs = (both, both, P(), both, both, both) + (P(),) * 7
    out_specs = (P(None, "ty", "tx"), P(None, "ty", "tx"))
    return jax.shard_map(body, mesh=mesh, in_specs=in_specs, out_specs=out_specs, check_vma=False)
```

```python
import functools

import jax
import jax.numpy as jnp
import numpy as np
from jax import lax
from jax.experimental import pallas as pl
from jax.experimental.pallas import tpu as pltpu
from jax.sharding import PartitionSpec as P

BF16 = jnp.bfloat16
F32 = jnp.float32
BANDS = 13
SRC_ROWS = 16
WIN_ROWS = 8
CAP = 2
NWIN = 32
TILE_COLS = 128
LINES = BANDS * WIN_ROWS
PACKED = CAP * LINES + WIN_ROWS
STEP_BLOCKS = 16
PIECES = 4
PHASES = 8
SPOTS = TILE_COLS // PHASES
HALO = 2
WIDE = SPOTS + 2 * HALO
TALL = NWIN + 2 * HALO
POINTS = WIDE * TALL
GROUP = 4
GROUP_POINTS = GROUP * WIDE
VMEM_BYTES = 60 * 1024 * 1024


def dot(a, b):
    return jnp.dot(a, b, preferred_element_type=F32)


def dot_nt(a, b):
    return lax.dot_general(a, b, (((1,), (1,)), ((), ())), preferred_element_type=F32)


def resample_kernel(
    dest_ref, win_ref, choice_ref, weight_ref, raw_hbm, bank_ref, out_ref,
    raw_ref, rows_ref, held_ref, slot_win_ref, sems,
):
    tiles, blocks = held_ref.shape[0], dest_ref.shape[0]
    deep = BANDS * SRC_ROWS

    def fetch(group):
        part = pl.ds(group * STEP_BLOCKS, STEP_BLOCKS)
        return pltpu.make_async_copy(raw_hbm.at[part], raw_ref.at[part], sems.at[group])

    for group in range(blocks // STEP_BLOCKS):
        fetch(group).start()

    def clear(i, carry):
        held_ref[i] = 0
        for k in range(CAP):
            slot_win_ref[i * CAP + k] = -1
        return carry

    lax.fori_loop(0, tiles, clear, 0, unroll=8)

    turned = jnp.transpose(weight_ref[...].astype(F32)).astype(BF16)
    depth = lax.broadcasted_iota(jnp.int32, (WIN_ROWS * SRC_ROWS, 256), 0)
    lane = lax.broadcasted_iota(jnp.int32, (WIN_ROWS * SRC_ROWS, 256), 1)
    offset = depth - (lane & (SRC_ROWS - 1))
    for r in range(WIN_ROWS):
        wide = dot(turned, (offset == r * SRC_ROWS).astype(F32).astype(BF16))
        for h in range(2):
            rows_ref[h, pl.ds(r, blocks, stride=WIN_ROWS), :] = wide[:, h * 128:(h + 1) * 128]

    line = lax.broadcasted_iota(jnp.int32, (LINES, 256), 0)
    lane = lax.broadcasted_iota(jnp.int32, (LINES, 256), 1)
    own = (line >> 3) == (lane >> 4)
    spot = lax.broadcasted_iota(jnp.int32, (WIN_ROWS, TILE_COLS), 1)

    def work(group, carry):
        fetch(group).wait()
        rowed = []
        for j in range(STEP_BLOCKS):
            n = group * STEP_BLOCKS + j
            row = pl.multiple_of(n * WIN_ROWS, WIN_ROWS)
            rows = jnp.concatenate(
                [rows_ref[h, pl.ds(row, WIN_ROWS), :] for h in range(2)], axis=1
            )
            weights = jnp.where(own, jnp.concatenate([rows] * BANDS, axis=0), 0.0)
            rowed.append(dot(weights.astype(BF16)[:, 0:deep], raw_ref[n]).astype(BF16))
        done = []
        for j in range(STEP_BLOCKS):
            n = group * STEP_BLOCKS + j
            done.append(dot(rowed[j], bank_ref[choice_ref[n]]).astype(BF16))
        for j in range(STEP_BLOCKS):
            n = group * STEP_BLOCKS + j
            tile = dest_ref[n]
            rank = held_ref[tile]
            held_ref[tile] = rank + 1
            slot_win_ref[tile * CAP + rank] = win_ref[n]
            place = pl.ds(pl.multiple_of(rank * LINES, WIN_ROWS), LINES)
            out_ref[tile, place, :] = done[j]
        return carry

    lax.fori_loop(0, blocks // STEP_BLOCKS, work, 0)

    def number(i, carry):
        window = jnp.where(spot == 0, slot_win_ref[i * CAP], slot_win_ref[i * CAP + 1])
        out_ref[i, CAP * LINES:] = window.astype(F32).astype(BF16)
        return carry

    lax.fori_loop(0, tiles, number, 0, unroll=4)


def resample(granule_blocks, row_weights, column_bank, destination, window_index, bank_index, tiles):
    blocks = granule_blocks.shape[0]
    deep = BANDS * SRC_ROWS
    vmem = pl.BlockSpec(memory_space=pltpu.VMEM)
    smem = pl.BlockSpec(memory_space=pltpu.SMEM)
    return pl.pallas_call(
        resample_kernel,
        in_specs=[smem, smem, smem, vmem, pl.BlockSpec(memory_space=pl.ANY), vmem],
        out_specs=vmem,
        scratch_shapes=[
            pltpu.VMEM((blocks, deep, TILE_COLS), BF16),
            pltpu.VMEM((2, blocks * WIN_ROWS, 128), F32),
            pltpu.SMEM((tiles,), jnp.int32),
            pltpu.SMEM((tiles * CAP,), jnp.int32),
            pltpu.SemaphoreType.DMA((blocks // STEP_BLOCKS,)),
        ],
        out_shape=jax.ShapeDtypeStruct((tiles, PACKED, TILE_COLS), BF16),
        compiler_params=pltpu.CompilerParams(vmem_limit_bytes=VMEM_BYTES),
        name="resample",
    )(
        destination, window_index, bank_index,
        row_weights.transpose(1, 2, 0).reshape(WIN_ROWS * SRC_ROWS, blocks),
        granule_blocks.reshape(blocks, deep, TILE_COLS),
        column_bank,
    )


def grid_kernel(
    got_hbm, perm_ref, grid_ref, main_ref, left_ref, right_ref,
    got_ref, sum_ref, number_ref, win_ref, count_ref, sem, sems,
):
    tiles = got_ref.shape[0]
    size = tiles // PIECES
    last = pl.ds(CAP * LINES, WIN_ROWS)
    head = pltpu.make_async_copy(got_hbm.at[:, last], got_ref.at[:, last], sems.at[PIECES])
    head.start()

    def fetch(piece):
        part = pl.ds(piece * size, size), pl.ds(0, CAP * LINES)
        return pltpu.make_async_copy(got_hbm.at[part], got_ref.at[part], sems.at[piece])

    for piece in range(PIECES):
        fetch(piece).start()
    head.wait()
    numbers = got_ref[:, CAP * LINES:, :].astype(F32)
    number_ref[...] = jnp.max(numbers, axis=1).astype(jnp.int32)
    copy = pltpu.make_async_copy(number_ref, win_ref, sem)
    copy.start()

    def clear(w, carry):
        sum_ref[w] = jnp.zeros(sum_ref.shape[1:], F32)
        count_ref[w] = 0
        return carry

    lax.fori_loop(0, NWIN + 1, clear, 0)
    copy.wait()

    def add(t, carry):
        for k in range(CAP):
            w = win_ref[t, k]
            w = jnp.where(w < 0, NWIN, w)
            block = got_ref[t, k * LINES:(k + 1) * LINES].astype(F32)
            sum_ref[w, 0:LINES] = sum_ref[w, 0:LINES] + block
            count_ref[w] = count_ref[w] + 1
        return carry

    def add_piece(piece, carry):
        fetch(piece).wait()
        return lax.fori_loop(piece * size, (piece + 1) * size, add, carry)

    lax.fori_loop(0, PIECES, add_piece, 0)

    def finish(group, carry):
        first = group * GROUP
        means = []
        for k in range(GROUP):
            w = first + k
            divisor = jnp.maximum(count_ref[w], 1).astype(F32)
            mean = (sum_ref[w, 0:LINES] / divisor).astype(BF16).astype(F32)
            sum_ref[w, 0:LINES] = mean
            means.append(mean)
        row = pl.multiple_of(first * WIN_ROWS, GROUP * WIN_ROWS)
        for b in range(BANDS):
            part = jnp.concatenate([m[b * WIN_ROWS:(b + 1) * WIN_ROWS] for m in means], axis=0)
            grid_ref[b, pl.ds(row, GROUP * WIN_ROWS), :] = part.astype(BF16)
        for pair in range(GROUP // 2):
            lines = jnp.concatenate(
                [
                    sum_ref[first + pair * 2 + k, pl.ds(r, 16, stride=WIN_ROWS), :]
                    for k in range(2)
                    for r in range(WIN_ROWS)
                ],
                axis=0,
            )
            both = dot_nt(perm_ref[...], lines.astype(BF16)).astype(BF16)
            for k in range(2):
                w = first + pair * 2 + k
                turned = both[:, k * 128:(k + 1) * 128]
                main_ref[pl.ds(pl.multiple_of(w * 128, 128), 128), :] = turned[0:128]
                left_ref[pl.ds(pl.multiple_of(w * 16, 16), 16), :] = turned[128:144]
                right_ref[pl.ds(pl.multiple_of(w * 16, 16), 16), :] = turned[144:160]
        return carry

    lax.fori_loop(0, NWIN // GROUP, finish, 0)


def grid(received):
    tiles = received.shape[0]
    perm = np.zeros((TILE_COLS + 32, TILE_COLS), np.float32)
    for p in range(PHASES):
        for a in range(SPOTS):
            perm[p * SPOTS + a, a * PHASES + p] = 1.0
        for a in range(HALO):
            perm[128 + p * HALO + a, a * PHASES + p] = 1.0
            perm[144 + p * HALO + a, (SPOTS - HALO + a) * PHASES + p] = 1.0
    vmem = pl.BlockSpec(memory_space=pltpu.VMEM)
    return pl.pallas_call(
        grid_kernel,
        in_specs=[pl.BlockSpec(memory_space=pl.ANY), vmem],
        out_specs=[vmem] * 4,
        out_shape=[
            jax.ShapeDtypeStruct((BANDS, NWIN * WIN_ROWS, TILE_COLS), BF16),
            jax.ShapeDtypeStruct((NWIN * 128, 128), BF16),
            jax.ShapeDtypeStruct((NWIN * 16, 128), BF16),
            jax.ShapeDtypeStruct((NWIN * 16, 128), BF16),
        ],
        scratch_shapes=[
            pltpu.VMEM(received.shape, BF16),
            pltpu.VMEM((NWIN + 1, 128, TILE_COLS), F32),
            pltpu.VMEM((tiles, TILE_COLS), jnp.int32),
            pltpu.SMEM((tiles, TILE_COLS), jnp.int32),
            pltpu.SMEM((NWIN + 1,), jnp.int32),
            pltpu.SemaphoreType.DMA,
            pltpu.SemaphoreType.DMA((PIECES + 1,)),
        ],
        compiler_params=pltpu.CompilerParams(vmem_limit_bytes=VMEM_BYTES),
        name="grid",
    )(received, jnp.asarray(perm, BF16))


def exchange(main, left, right):
    across, down = lax.axis_size("tx"), lax.axis_size("ty")
    right_ward = [(i, i + 1) for i in range(across - 1)]
    left_ward = [(t, s) for s, t in right_ward]
    down_ward = [(i, i + 1) for i in range(down - 1)]
    up_ward = [(t, s) for s, t in down_ward]
    from_left = lax.ppermute(right, "tx", right_ward)
    from_right = lax.ppermute(left, "tx", left_ward)
    m, h = HALO * 128, HALO * 16
    first = jnp.concatenate([main[:m], from_left[:h], from_right[:h]], axis=0)
    last = jnp.concatenate([main[-m:], from_left[-h:], from_right[-h:]], axis=0)
    from_above = lax.ppermute(last, "ty", down_ward)
    from_below = lax.ppermute(first, "ty", up_ward)
    return from_left, from_right, from_above, from_below


def spread_matrix():
    out = np.zeros((PHASES + 2, GROUP_POINTS, GROUP * 48), np.float32)
    for index in range(PHASES + 2):
        p = (index - 1) % PHASES
        shift = -1 if index == 0 else (1 if index == PHASES + 1 else 0)
        for k in range(GROUP):
            for a in range(WIDE):
                s = a + shift
                row = k * WIDE + a
                if s < 0 or s >= WIDE:
                    continue
                if s < HALO:
                    out[index, row, GROUP * 16 + k * 16 + p * HALO + s] = 1.0
                elif s < HALO + SPOTS:
                    out[index, row, k * 16 + s - HALO] = 1.0
                else:
                    out[index, row, GROUP * 32 + k * 16 + p * HALO + s - HALO - SPOTS] = 1.0
    return out


def relu(x):
    return jnp.maximum(x, 0.0)


def encoder_kernel(
    main_ref, fl_ref, fr_ref, above_ref, below_ref, spread_ref, one_ref, down2_ref,
    two_ref, down3_hbm, three_hbm, down4_hbm, four_hbm,
    out_ref,
    ext1, ext2, x1, x2, d2, d3, d4, flat, down3_ref, three_ref, down4_ref, four_ref, sems,
):
    copies = [
        pltpu.make_async_copy(src, dst, sems.at[i])
        for i, (src, dst) in enumerate(
            (
                (down3_hbm, down3_ref),
                (three_hbm, three_ref),
                (down4_hbm, down4_ref),
                (four_hbm, four_ref),
            )
        )
    ]
    for copy in copies:
        copy.start()

    for h in range(HALO):
        for source, w in ((above_ref, h), (below_ref, HALO + NWIN + h)):
            ext1[w, 0:128] = source[h * 128:(h + 1) * 128]
            base = HALO * 128 + h * 16
            ext1[w, 128:144] = source[base:base + 16]
            ext1[w, 144:160] = source[base + HALO * 16:base + HALO * 16 + 16]

    def gather(w, carry):
        ext1[w + HALO, 0:128] = main_ref[pl.ds(pl.multiple_of(w * 128, 128), 128), :]
        ext1[w + HALO, 128:144] = fl_ref[pl.ds(pl.multiple_of(w * 16, 16), 16), :]
        ext1[w + HALO, 144:160] = fr_ref[pl.ds(pl.multiple_of(w * 16, 16), 16), :]
        return carry

    lax.fori_loop(0, NWIN, gather, 0)

    low = lax.broadcasted_iota(jnp.int32, (160, 128), 1) < 64

    def lower(w, carry):
        after = jnp.minimum(w + 1, TALL - 1)
        both = jnp.where(low, ext1[after].astype(F32), ext1[w].astype(F32))
        ext2[w] = pltpu.roll(both, 64, 1).astype(BF16)
        return carry

    lax.fori_loop(0, TALL, lower, 0)

    def place(g, carry):
        row = pl.multiple_of(g * GROUP_POINTS, GROUP_POINTS)
        for index in range(PHASES + 2):
            p = (index - 1) % PHASES
            sides = []
            for ext in (ext1, ext2):
                pieces = [ext[g * GROUP + k, p * 16:(p + 1) * 16] for k in range(GROUP)]
                pieces += [ext[g * GROUP + k, 128:144] for k in range(GROUP)]
                pieces += [ext[g * GROUP + k, 144:160] for k in range(GROUP)]
                sides.append(jnp.concatenate(pieces, axis=0))
            laid = dot(spread_ref[index], jnp.concatenate(sides, axis=1)).astype(BF16)
            x1[index, pl.ds(row, GROUP_POINTS), :] = laid[:, 0:128]
            x2[index, pl.ds(row, GROUP_POINTS), :] = laid[:, 128:256]
        return carry

    lax.fori_loop(0, TALL // GROUP, place, 0)

    across, below = lax.axis_size("tx"), lax.axis_size("ty")
    x, y = lax.axis_index("tx"), lax.axis_index("ty")
    least_w, most_w = jnp.where(y > 0, 0, HALO), jnp.where(y < below - 1, TALL, HALO + NWIN)
    least_a, most_a = jnp.where(x > 0, 0, HALO), jnp.where(x < across - 1, WIDE, HALO + SPOTS)
    point = lax.broadcasted_iota(jnp.int32, (POINTS, 128), 0)
    w = (point * (65536 // WIDE + 1)) >> 16
    a = point - w * WIDE
    inside = (w >= least_w) & (w < most_w) & (a >= least_a) & (a < most_a)
    mask = inside.astype(F32)
    mask2 = jnp.concatenate([mask, mask], axis=1)
    mask4 = jnp.concatenate([mask2, mask2], axis=1)

    def put(dst, i, j, value, last):
        rows = [(i + 1, 0)]
        if i == last:
            rows.append((0, WIDE))
        if i == 0:
            rows.append((last + 2, -WIDE))
        cols = [(j + 1, 0)]
        if j == last:
            cols.append((0, 1))
        if j == 0:
            cols.append((last + 2, -1))
        for r, row_shift in rows:
            for c, col_shift in cols:
                shift = (row_shift + col_shift) % POINTS
                moved = pltpu.roll(value, shift, 0) if shift else value
                dst[r, c] = moved.astype(BF16)

    for cb in range(4):
        for version, x in enumerate((x1, x2)):
            taps = jnp.concatenate([x[2 * cb + k] for k in range(4)], axis=1)
            level = relu(dot(taps, one_ref[...])).astype(BF16)
            for half in range(2):
                down = relu(dot(level[:, half * 256:(half + 1) * 256], down2_ref[...]))
                if version == 0:
                    rb = 1 + half
                elif half == 0:
                    rb = 3
                else:
                    rb = 0
                    down = pltpu.roll(down, WIDE, 0)
                put(d2, rb, cb, down * mask, 3)

    copies[0].wait()
    for rp in range(2):
        for j in range(2):
            total = None
            for v2 in range(2):
                taps = jnp.concatenate(
                    [d2[2 * rp + r, 2 * j + v2 + v] for r in range(4) for v in range(3)], axis=1
                )
                level = relu(dot(taps, two_ref[...])).astype(BF16)
                part = dot(level, down3_ref[v2])
                total = part if total is None else total + part
            put(d3, rp, j, relu(total) * mask2, 1)

    copies[1].wait()
    copies[2].wait()
    total = None
    for i in range(2):
        for j in range(2):
            taps = jnp.concatenate(
                [d3[i + u, j + v] for u in range(3) for v in range(3)], axis=1
            )
            level = relu(dot(taps, three_ref[...])).astype(BF16)
            part = dot(level, down4_ref[i * 2 + j])
            total = part if total is None else total + part
    put(d4, 0, 0, relu(total) * mask4, 0)

    copies[3].wait()
    first, count = HALO * WIDE, NWIN * WIDE
    taps = jnp.concatenate(
        [d4[u, v, first:first + count] for u in range(3) for v in range(3)], axis=1
    )
    flat[...] = relu(dot(taps, four_ref[...]))
    for w in range(NWIN):
        start = w * WIDE + HALO
        out_ref[w] = flat[start:start + SPOTS].astype(BF16)


def encoder(main, halos, one, down2, two, down3, three, down4, four):
    vmem = pl.BlockSpec(memory_space=pltpu.VMEM)
    hbm = pl.BlockSpec(memory_space=pl.ANY)
    return pl.pallas_call(
        encoder_kernel,
        in_specs=[vmem] * 9 + [hbm] * 4,
        out_specs=vmem,
        out_shape=jax.ShapeDtypeStruct((NWIN, SPOTS, four.shape[-1]), BF16),
        scratch_shapes=[
            pltpu.VMEM((TALL, 160, 128), BF16),
            pltpu.VMEM((TALL, 160, 128), BF16),
            pltpu.VMEM((PHASES + 2, POINTS, 128), BF16),
            pltpu.VMEM((PHASES + 2, POINTS, 128), BF16),
            pltpu.VMEM((6, 6, POINTS, 128), BF16),
            pltpu.VMEM((4, 4, POINTS, 256), BF16),
            pltpu.VMEM((3, 3, POINTS, 512), BF16),
            pltpu.VMEM((NWIN * WIDE, 512), F32),
            pltpu.VMEM(down3.shape, BF16),
            pltpu.VMEM(three.shape, BF16),
            pltpu.VMEM(down4.shape, BF16),
            pltpu.VMEM(four.shape, BF16),
            pltpu.SemaphoreType.DMA((4,)),
        ],
        compiler_params=pltpu.CompilerParams(vmem_limit_bytes=VMEM_BYTES),
        name="encoder",
    )(
        main, *halos, jnp.asarray(spread_matrix(), BF16), one, down2,
        two, down3, three, down4, four,
    )


def level_one_weights(kernel):
    kernel = jnp.pad(kernel, ((0, 0), (0, 0), (0, 16 - BANDS), (0, 0)))
    columns = []
    for rb in range(2):
        for i in range(2):
            for j in range(2):
                top = 1 + 2 * rb + i
                wide = jnp.pad(kernel, ((top, 5 - top), (j, 1 - j), (0, 0), (0, 0)))
                columns.append(wide.transpose(1, 0, 2, 3).reshape(4 * 8 * 16, -1))
    return jnp.concatenate(columns, axis=1)


def level_two_weights(kernel):
    none = ((0, 0),) * 3
    pair = [jnp.pad(kernel, ((i, 1 - i),) + none) for i in range(2)]
    return jnp.concatenate(pair, axis=3).reshape(12 * kernel.shape[2], -1)


def body(
    granule_blocks, row_weights, column_bank, destination, window_index, bank_index,
    kernel_one, reduce_two, kernel_two, reduce_three, kernel_three, reduce_four, kernel_four,
):
    axes = ("tx", "ty")
    tiles = lax.axis_size("tx") * lax.axis_size("ty")
    slots = resample(
        granule_blocks, row_weights, column_bank, destination, window_index, bank_index, tiles
    )
    received = lax.all_to_all(slots, axes, split_axis=0, concat_axis=0, tiled=True)
    gridded, main, left, right = grid(received)
    halos = exchange(main, left, right)
    flat = encoder(
        main, halos,
        level_one_weights(kernel_one),
        reduce_two.reshape(256, 128),
        level_two_weights(kernel_two),
        reduce_three.transpose(1, 0, 2, 3).reshape(2, 256, 256),
        kernel_three.reshape(9 * 256, 256),
        reduce_four.reshape(4, 256, 512),
        kernel_four.reshape(9 * 512, 512),
    )
    return gridded, flat.transpose(2, 0, 1)


def solution(mesh):
    both = P(("tx", "ty"))
    in_specs = (both, both, P(), both, both, both) + (P(),) * 7
    out_specs = (P(None, "ty", "tx"), P(None, "ty", "tx"))
    return jax.shard_map(body, mesh=mesh, in_specs=in_specs, out_specs=out_specs, check_vma=False)
```

```python
import functools

import jax
import jax.numpy as jnp
import numpy as np
from jax import lax
from jax.experimental import pallas as pl
from jax.experimental.pallas import tpu as pltpu
from jax.sharding import PartitionSpec as P

BF16 = jnp.bfloat16
F32 = jnp.float32
BANDS = 13
SRC_ROWS = 16
WIN_ROWS = 8
CAP = 2
NWIN = 32
TILE_COLS = 128
LINES = BANDS * WIN_ROWS
PACKED = CAP * LINES + WIN_ROWS
STEP_BLOCKS = 16
PIECES = 4
PHASES = 8
SPOTS = TILE_COLS // PHASES
HALO = 2
WIDE = SPOTS + 2 * HALO
TALL = NWIN + 2 * HALO
POINTS = WIDE * TALL
GROUP = 4
GROUP_POINTS = GROUP * WIDE
MIB = 1024 * 1024


def dot(a, b):
    return jnp.dot(a, b, preferred_element_type=F32)


def dot_nt(a, b):
    return lax.dot_general(a, b, (((1,), (1,)), ((), ())), preferred_element_type=F32)


def resample_kernel(
    dest_ref, win_ref, choice_ref, weight_ref, raw_hbm, bank_ref, out_ref,
    raw_ref, rows_ref, held_ref, slot_win_ref, sems,
):
    tiles, blocks = held_ref.shape[0], dest_ref.shape[0]
    deep = BANDS * SRC_ROWS

    def fetch(group):
        part = pl.ds(group * STEP_BLOCKS, STEP_BLOCKS)
        return pltpu.make_async_copy(raw_hbm.at[part], raw_ref.at[part], sems.at[group])

    for group in range(blocks // STEP_BLOCKS):
        fetch(group).start()

    def clear(i, carry):
        held_ref[i] = 0
        for k in range(CAP):
            slot_win_ref[i * CAP + k] = -1
        return carry

    lax.fori_loop(0, tiles, clear, 0, unroll=8)

    turned = jnp.transpose(weight_ref[...].astype(F32)).astype(BF16)
    depth = lax.broadcasted_iota(jnp.int32, (WIN_ROWS * SRC_ROWS, 256), 0)
    lane = lax.broadcasted_iota(jnp.int32, (WIN_ROWS * SRC_ROWS, 256), 1)
    offset = depth - (lane & (SRC_ROWS - 1))
    for r in range(WIN_ROWS):
        wide = dot(turned, (offset == r * SRC_ROWS).astype(F32).astype(BF16))
        for h in range(2):
            rows_ref[h, pl.ds(r, blocks, stride=WIN_ROWS), :] = wide[:, h * 128:(h + 1) * 128]

    line = lax.broadcasted_iota(jnp.int32, (LINES, 256), 0)
    lane = lax.broadcasted_iota(jnp.int32, (LINES, 256), 1)
    own = (line >> 3) == (lane >> 4)
    spot = lax.broadcasted_iota(jnp.int32, (WIN_ROWS, TILE_COLS), 1)

    def work(group, carry):
        fetch(group).wait()
        rowed = []
        for j in range(STEP_BLOCKS):
            n = group * STEP_BLOCKS + j
            row = pl.multiple_of(n * WIN_ROWS, WIN_ROWS)
            rows = jnp.concatenate(
                [rows_ref[h, pl.ds(row, WIN_ROWS), :] for h in range(2)], axis=1
            )
            weights = jnp.where(own, jnp.concatenate([rows] * BANDS, axis=0), 0.0)
            rowed.append(dot(weights.astype(BF16)[:, 0:deep], raw_ref[n]).astype(BF16))
        done = []
        for j in range(STEP_BLOCKS):
            n = group * STEP_BLOCKS + j
            done.append(dot(rowed[j], bank_ref[choice_ref[n]]).astype(BF16))
        for j in range(STEP_BLOCKS):
            n = group * STEP_BLOCKS + j
            tile = dest_ref[n]
            rank = held_ref[tile]
            held_ref[tile] = rank + 1
            slot_win_ref[tile * CAP + rank] = win_ref[n]
            place = pl.ds(pl.multiple_of(rank * LINES, WIN_ROWS), LINES)
            out_ref[tile, place, :] = done[j]
        return carry

    lax.fori_loop(0, blocks // STEP_BLOCKS, work, 0)

    def number(i, carry):
        window = jnp.where(spot == 0, slot_win_ref[i * CAP], slot_win_ref[i * CAP + 1])
        out_ref[i, CAP * LINES:] = window.astype(F32).astype(BF16)
        return carry

    lax.fori_loop(0, tiles, number, 0, unroll=4)


def resample(granule_blocks, row_weights, column_bank, destination, window_index, bank_index, tiles):
    blocks = granule_blocks.shape[0]
    deep = BANDS * SRC_ROWS
    vmem = pl.BlockSpec(memory_space=pltpu.VMEM)
    smem = pl.BlockSpec(memory_space=pltpu.SMEM)
    return pl.pallas_call(
        resample_kernel,
        in_specs=[smem, smem, smem, vmem, pl.BlockSpec(memory_space=pl.ANY), vmem],
        out_specs=vmem,
        scratch_shapes=[
            pltpu.VMEM((blocks, deep, TILE_COLS), BF16),
            pltpu.VMEM((2, blocks * WIN_ROWS, 128), F32),
            pltpu.SMEM((tiles,), jnp.int32),
            pltpu.SMEM((tiles * CAP,), jnp.int32),
            pltpu.SemaphoreType.DMA((blocks // STEP_BLOCKS,)),
        ],
        out_shape=jax.ShapeDtypeStruct((tiles, PACKED, TILE_COLS), BF16),
        compiler_params=pltpu.CompilerParams(vmem_limit_bytes=(24 * MIB if tiles <= 64 else 48 * MIB)),
        name="resample",
    )(
        destination, window_index, bank_index,
        row_weights.transpose(1, 2, 0).reshape(WIN_ROWS * SRC_ROWS, blocks),
        granule_blocks.reshape(blocks, deep, TILE_COLS),
        column_bank,
    )


def grid_kernel(
    got_hbm, perm_ref, grid_ref, lines_ref, left_ref, right_ref,
    got_ref, sum_ref, number_ref, win_ref, count_ref, sem, sems,
):
    tiles = got_ref.shape[0]
    size = tiles // PIECES
    last = pl.ds(CAP * LINES, WIN_ROWS)
    head = pltpu.make_async_copy(got_hbm.at[:, last], got_ref.at[:, last], sems.at[PIECES])
    head.start()

    def fetch(piece):
        part = pl.ds(piece * size, size), pl.ds(0, CAP * LINES)
        return pltpu.make_async_copy(got_hbm.at[part], got_ref.at[part], sems.at[piece])

    for piece in range(PIECES):
        fetch(piece).start()
    head.wait()
    numbers = got_ref[:, CAP * LINES:, :].astype(F32)
    number_ref[...] = jnp.max(numbers, axis=1).astype(jnp.int32)
    copy = pltpu.make_async_copy(number_ref, win_ref, sem)
    copy.start()

    def clear(w, carry):
        sum_ref[w] = jnp.zeros(sum_ref.shape[1:], F32)
        count_ref[w] = 0
        return carry

    lax.fori_loop(0, NWIN + 1, clear, 0)
    copy.wait()

    def add(t, carry):
        for k in range(CAP):
            w = win_ref[t, k]
            w = jnp.where(w < 0, NWIN, w)
            block = got_ref[t, k * LINES:(k + 1) * LINES].astype(F32)
            sum_ref[w, 0:LINES] = sum_ref[w, 0:LINES] + block
            count_ref[w] = count_ref[w] + 1
        return carry

    def add_piece(piece, carry):
        fetch(piece).wait()
        return lax.fori_loop(piece * size, (piece + 1) * size, add, carry)

    lax.fori_loop(0, PIECES, add_piece, 0)

    def finish(group, carry):
        first = group * GROUP
        means = []
        for k in range(GROUP):
            w = first + k
            divisor = jnp.maximum(count_ref[w], 1).astype(F32)
            mean = (sum_ref[w, 0:LINES] / divisor).astype(BF16).astype(F32)
            sum_ref[w, 0:LINES] = mean
            means.append(mean)
        row = pl.multiple_of(first * WIN_ROWS, GROUP * WIN_ROWS)
        for b in range(BANDS):
            part = jnp.concatenate([m[b * WIN_ROWS:(b + 1) * WIN_ROWS] for m in means], axis=0)
            grid_ref[b, pl.ds(row, GROUP * WIN_ROWS), :] = part.astype(BF16)
        for pair in range(GROUP // 2):
            lines = jnp.concatenate(
                [
                    sum_ref[first + pair * 2 + k, pl.ds(r, 16, stride=WIN_ROWS), :]
                    for k in range(2)
                    for r in range(WIN_ROWS)
                ],
                axis=0,
            ).astype(BF16)
            row = pl.multiple_of((first + pair * 2) * 128, 256)
            lines_ref[pl.ds(row, 256), :] = lines
            both = dot_nt(perm_ref[...], lines).astype(BF16)
            for k in range(2):
                w = first + pair * 2 + k
                turned = both[:, k * 128:(k + 1) * 128]
                left_ref[pl.ds(pl.multiple_of(w * 16, 16), 16), :] = turned[0:16]
                right_ref[pl.ds(pl.multiple_of(w * 16, 16), 16), :] = turned[16:32]
        return carry

    lax.fori_loop(0, NWIN // GROUP, finish, 0)


def grid(received):
    tiles = received.shape[0]
    perm = np.zeros((32, TILE_COLS), np.float32)
    for p in range(PHASES):
        for a in range(HALO):
            perm[p * HALO + a, a * PHASES + p] = 1.0
            perm[16 + p * HALO + a, (SPOTS - HALO + a) * PHASES + p] = 1.0
    vmem = pl.BlockSpec(memory_space=pltpu.VMEM)
    return pl.pallas_call(
        grid_kernel,
        in_specs=[pl.BlockSpec(memory_space=pl.ANY), vmem],
        out_specs=[vmem] * 4,
        out_shape=[
            jax.ShapeDtypeStruct((BANDS, NWIN * WIN_ROWS, TILE_COLS), BF16),
            jax.ShapeDtypeStruct((NWIN * 128, 128), BF16),
            jax.ShapeDtypeStruct((NWIN * 16, 128), BF16),
            jax.ShapeDtypeStruct((NWIN * 16, 128), BF16),
        ],
        scratch_shapes=[
            pltpu.VMEM(received.shape, BF16),
            pltpu.VMEM((NWIN + 1, 128, TILE_COLS), F32),
            pltpu.VMEM((tiles, TILE_COLS), jnp.int32),
            pltpu.SMEM((tiles, TILE_COLS), jnp.int32),
            pltpu.SMEM((NWIN + 1,), jnp.int32),
            pltpu.SemaphoreType.DMA,
            pltpu.SemaphoreType.DMA((PIECES + 1,)),
        ],
        compiler_params=pltpu.CompilerParams(vmem_limit_bytes=24 * MIB),
        name="grid",
    )(received, jnp.asarray(perm, BF16))


def turn_kernel(lines_ref, perm_ref, main_ref, lower_ref, top_ref, bottom_ref):
    def step(i, carry):
        for k in range(2):
            w = i * 2 + k
            start = pl.multiple_of(w * 128, 128)
            below = pl.multiple_of(jnp.minimum(w * 128 + 64, (NWIN - 1) * 128), 64)
            lines = jnp.concatenate(
                [lines_ref[pl.ds(start, 128), :], lines_ref[pl.ds(below, 128), :]], axis=0
            )
            both = dot_nt(perm_ref[...], lines).astype(BF16)
            main_ref[pl.ds(start, 128), :] = both[:, 0:128]
            lower_ref[pl.ds(start, 128), :] = both[:, 128:256]
        return carry

    lax.fori_loop(0, NWIN // 2, step, 0, unroll=2)
    top_ref[...] = main_ref[0:top_ref.shape[0]]
    bottom_ref[...] = main_ref[(NWIN - HALO) * 128:]


def turn(lines):
    perm = np.zeros((TILE_COLS, TILE_COLS), np.float32)
    for p in range(PHASES):
        for a in range(SPOTS):
            perm[p * SPOTS + a, a * PHASES + p] = 1.0
    vmem = pl.BlockSpec(memory_space=pltpu.VMEM)
    return pl.pallas_call(
        turn_kernel,
        in_specs=[vmem] * 2,
        out_specs=[vmem] * 4,
        out_shape=[
            jax.ShapeDtypeStruct((NWIN * 128, 128), BF16),
            jax.ShapeDtypeStruct((NWIN * 128, 128), BF16),
            jax.ShapeDtypeStruct(((HALO + 1) * 128, 128), BF16),
            jax.ShapeDtypeStruct((HALO * 128, 128), BF16),
        ],
        compiler_params=pltpu.CompilerParams(vmem_limit_bytes=16 * MIB),
        cost_estimate=pl.CostEstimate(
            flops=2 * NWIN * 128 ** 3 * 2, bytes_accessed=8 * MIB, transcendentals=0
        ),
        name="turn",
    )(lines, jnp.asarray(perm, BF16))


def exchange_columns(left, right):
    across = lax.axis_size("tx")
    right_ward = [(i, i + 1) for i in range(across - 1)]
    left_ward = [(t, s) for s, t in right_ward]
    return lax.ppermute(right, "tx", right_ward), lax.ppermute(left, "tx", left_ward)


def exchange_rows(top, bottom, from_left, from_right):
    down = lax.axis_size("ty")
    down_ward = [(i, i + 1) for i in range(down - 1)]
    up_ward = [(t, s) for s, t in down_ward]
    m, h = HALO * 128, HALO * 16
    first = jnp.concatenate([top[:m], from_left[:h], from_right[:h]], axis=0)
    last = jnp.concatenate([bottom, from_left[-h:], from_right[-h:]], axis=0)
    return lax.ppermute(last, "ty", down_ward), lax.ppermute(first, "ty", up_ward)


def spread_matrix():
    out = np.zeros((PHASES + 2, GROUP_POINTS, GROUP * 48), np.float32)
    for index in range(PHASES + 2):
        p = (index - 1) % PHASES
        shift = -1 if index == 0 else (1 if index == PHASES + 1 else 0)
        for k in range(GROUP):
            for a in range(WIDE):
                s = a + shift
                row = k * WIDE + a
                if s < 0 or s >= WIDE:
                    continue
                if s < HALO:
                    out[index, row, GROUP * 16 + k * 16 + p * HALO + s] = 1.0
                elif s < HALO + SPOTS:
                    out[index, row, k * 16 + s - HALO] = 1.0
                else:
                    out[index, row, GROUP * 32 + k * 16 + p * HALO + s - HALO - SPOTS] = 1.0
    return out


def relu(x):
    return jnp.maximum(x, 0.0)


def level_one(x1, x2, one_ref, down2_ref, store):
    for cb in range(4):
        for version, x in enumerate((x1, x2)):
            taps = jnp.concatenate([x[2 * cb + k] for k in range(4)], axis=1)
            level = relu(dot(taps, one_ref[...])).astype(BF16)
            for half in range(2):
                down = relu(dot(level[:, half * 256:(half + 1) * 256], down2_ref[...]))
                store(2 * version + half, cb, down)


def lay(spread, first, second):
    return dot(spread, jnp.concatenate([jnp.concatenate(p, axis=0) for p in (first, second)], axis=1))


def interior_kernel(
    main_ref, lower_ref, fl_ref, fr_ref, spread_ref, one_ref, down2_ref, out_ref, side_ref, x1, x2
):
    low = lax.broadcasted_iota(jnp.int32, (16, 128), 1) < 64
    for s, side in enumerate((fl_ref, fr_ref)):
        for w in range(NWIN - 1):
            after = side[(w + 1) * 16:(w + 2) * 16].astype(F32)
            both = jnp.where(low, after, side[w * 16:(w + 1) * 16].astype(F32))
            side_ref[s, w * 16:(w + 1) * 16] = pltpu.roll(both, 64, 1).astype(BF16)

    def place(g, carry):
        row = pl.multiple_of(g * GROUP_POINTS, GROUP_POINTS)
        w = g * GROUP + GROUP - HALO
        edge = [pl.ds(pl.multiple_of((w + k) * 16, 16), 16) for k in range(GROUP)]
        for index in range(PHASES + 2):
            p = (index - 1) % PHASES
            own = [
                pl.ds(pl.multiple_of((w + k) * 128 + p * 16, 16), 16) for k in range(GROUP)
            ]
            first = [main_ref[o, :] for o in own]
            first += [ref[e, :] for ref in (fl_ref, fr_ref) for e in edge]
            second = [lower_ref[o, :] for o in own]
            second += [side_ref[s, e, :] for s in range(2) for e in edge]
            laid = lay(spread_ref[index], first, second).astype(BF16)
            x1[index, pl.ds(row, GROUP_POINTS), :] = laid[:, 0:128]
            x2[index, pl.ds(row, GROUP_POINTS), :] = laid[:, 128:256]
        return carry

    lax.fori_loop(0, TALL // GROUP - 2, place, 0)

    def store(rb, cb, down):
        out_ref[rb, cb] = down.astype(BF16)

    level_one(x1, x2, one_ref, down2_ref, store)


def interior(main, lower, from_left, from_right, spread, one, down2):
    vmem = pl.BlockSpec(memory_space=pltpu.VMEM)
    points = POINTS - 2 * GROUP_POINTS
    return pl.pallas_call(
        interior_kernel,
        in_specs=[vmem] * 7,
        out_specs=vmem,
        out_shape=jax.ShapeDtypeStruct((4, 4, points, 128), BF16),
        scratch_shapes=[
            pltpu.VMEM((2, NWIN * 16, 128), BF16),
            pltpu.VMEM((PHASES + 2, points, 128), BF16),
            pltpu.VMEM((PHASES + 2, points, 128), BF16),
        ],
        compiler_params=pltpu.CompilerParams(vmem_limit_bytes=32 * MIB),
        cost_estimate=pl.CostEstimate(
            flops=2 * points * 8 * (512 * 512 + 512 * 256),
            bytes_accessed=16 * MIB,
            transcendentals=0,
        ),
        name="interior",
    )(main, lower, from_left, from_right, spread, one, down2)


def encoder_kernel(
    inner_hbm, top_ref, bottom_ref, fl_ref, fr_ref, above_ref, below_ref, spread_ref, one_ref,
    down2_ref, two_ref, down3_hbm, three_hbm, down4_hbm, four_hbm,
    out_ref,
    inner_ref, ext1, ext2, x1, x2, d2, d3, d4, flat, down3_ref, three_ref, down4_ref, four_ref,
    sems,
):
    copies = [
        pltpu.make_async_copy(src, dst, sems.at[i])
        for i, (src, dst) in enumerate(
            (
                (down3_hbm, down3_ref),
                (three_hbm, three_ref),
                (down4_hbm, down4_ref),
                (four_hbm, four_ref),
                (inner_hbm, inner_ref),
            )
        )
    ]
    copies[4].start()
    for copy in copies[:4]:
        copy.start()

    m = HALO * 128
    for h in range(HALO):
        for source, i in ((above_ref, h), (below_ref, 3 * HALO + 1 + h)):
            ext1[i, 0:128] = source[h * 128:(h + 1) * 128]
            ext1[i, 128:144] = source[m + h * 16:m + h * 16 + 16]
            ext1[i, 144:160] = source[m + (HALO + h) * 16:m + (HALO + h) * 16 + 16]
    near = [(HALO + k, top_ref, k, k) for k in range(HALO + 1)]
    near += [(2 * HALO + 1 + k, bottom_ref, k, NWIN - HALO + k) for k in range(HALO)]
    for i, source, k, w in near:
        ext1[i, 0:128] = source[k * 128:(k + 1) * 128]
        ext1[i, 128:144] = fl_ref[w * 16:(w + 1) * 16]
        ext1[i, 144:160] = fr_ref[w * 16:(w + 1) * 16]

    low = lax.broadcasted_iota(jnp.int32, (160, 128), 1) < 64
    edges = (0, GROUP + 1)
    for base in edges:
        for k in range(GROUP):
            i = base + k
            after = min(i + 1, ext1.shape[0] - 1)
            both = jnp.where(low, ext1[after].astype(F32), ext1[i].astype(F32))
            ext2[i] = pltpu.roll(both, 64, 1).astype(BF16)

    for e, base in enumerate(edges):
        for index in range(PHASES + 2):
            p = (index - 1) % PHASES
            sides = []
            for ext in (ext1, ext2):
                pieces = [ext[base + k, p * 16:(p + 1) * 16] for k in range(GROUP)]
                pieces += [ext[base + k, 128:144] for k in range(GROUP)]
                pieces += [ext[base + k, 144:160] for k in range(GROUP)]
                sides.append(pieces)
            laid = lay(spread_ref[index], *sides).astype(BF16)
            x1[index, e * GROUP_POINTS:(e + 1) * GROUP_POINTS] = laid[:, 0:128]
            x2[index, e * GROUP_POINTS:(e + 1) * GROUP_POINTS] = laid[:, 128:256]

    across, below = lax.axis_size("tx"), lax.axis_size("ty")
    x, y = lax.axis_index("tx"), lax.axis_index("ty")
    least_w, most_w = jnp.where(y > 0, 0, HALO), jnp.where(y < below - 1, TALL, HALO + NWIN)
    least_a, most_a = jnp.where(x > 0, 0, HALO), jnp.where(x < across - 1, WIDE, HALO + SPOTS)
    point = lax.broadcasted_iota(jnp.int32, (POINTS, 128), 0)
    w = (point * (65536 // WIDE + 1)) >> 16
    a = point - w * WIDE
    inside = (w >= least_w) & (w < most_w) & (a >= least_a) & (a < most_a)
    mask = inside.astype(F32)
    mask2 = jnp.concatenate([mask, mask], axis=1)
    mask4 = jnp.concatenate([mask2, mask2], axis=1)

    def put(dst, i, j, value, last):
        rows = [(i + 1, 0)]
        if i == last:
            rows.append((0, WIDE))
        if i == 0:
            rows.append((last + 2, -WIDE))
        cols = [(j + 1, 0)]
        if j == last:
            cols.append((0, 1))
        if j == 0:
            cols.append((last + 2, -1))
        for r, row_shift in rows:
            for c, col_shift in cols:
                shift = (row_shift + col_shift) % POINTS
                moved = pltpu.roll(value, shift, 0) if shift else value
                dst[r, c] = moved.astype(BF16)

    copies[4].wait()

    def store(rb, cb, down):
        inner = inner_ref[rb, cb].astype(F32)
        down = jnp.concatenate([down[:GROUP_POINTS], inner, down[GROUP_POINTS:]], axis=0)
        if rb == 3:
            down = pltpu.roll(down, WIDE, 0)
        put(d2, (rb + 1) % 4, cb, down * mask, 3)

    level_one(x1, x2, one_ref, down2_ref, store)

    copies[0].wait()
    for rp in range(2):
        for j in range(2):
            total = None
            for v2 in range(2):
                taps = jnp.concatenate(
                    [d2[2 * rp + r, 2 * j + v2 + v] for r in range(4) for v in range(3)], axis=1
                )
                level = relu(dot(taps, two_ref[...])).astype(BF16)
                part = dot(level, down3_ref[v2])
                total = part if total is None else total + part
            put(d3, rp, j, relu(total) * mask2, 1)

    copies[1].wait()
    copies[2].wait()
    total = None
    for i in range(2):
        for j in range(2):
            taps = jnp.concatenate(
                [d3[i + u, j + v] for u in range(3) for v in range(3)], axis=1
            )
            level = relu(dot(taps, three_ref[...])).astype(BF16)
            part = dot(level, down4_ref[i * 2 + j])
            total = part if total is None else total + part
    put(d4, 0, 0, relu(total) * mask4, 0)

    copies[3].wait()
    first, count = HALO * WIDE, NWIN * WIDE
    taps = jnp.concatenate(
        [d4[u, v, first:first + count] for u in range(3) for v in range(3)], axis=1
    )
    flat[...] = relu(dot(taps, four_ref[...]))
    for w in range(NWIN):
        start = w * WIDE + HALO
        out_ref[w] = flat[start:start + SPOTS].astype(BF16)


def encoder(inner, edges, spread, one, down2, two, down3, three, down4, four):
    vmem = pl.BlockSpec(memory_space=pltpu.VMEM)
    hbm = pl.BlockSpec(memory_space=pl.ANY)
    rim = 2 * GROUP_POINTS
    return pl.pallas_call(
        encoder_kernel,
        in_specs=[hbm] + [vmem] * 10 + [hbm] * 4,
        out_specs=vmem,
        out_shape=jax.ShapeDtypeStruct((NWIN, SPOTS, four.shape[-1]), BF16),
        scratch_shapes=[
            pltpu.VMEM(inner.shape, BF16),
            pltpu.VMEM((2 * GROUP + 1, 160, 128), BF16),
            pltpu.VMEM((2 * GROUP + 1, 160, 128), BF16),
            pltpu.VMEM((PHASES + 2, rim, 128), BF16),
            pltpu.VMEM((PHASES + 2, rim, 128), BF16),
            pltpu.VMEM((6, 6, POINTS, 128), BF16),
            pltpu.VMEM((4, 4, POINTS, 256), BF16),
            pltpu.VMEM((3, 3, POINTS, 512), BF16),
            pltpu.VMEM((NWIN * WIDE, 512), F32),
            pltpu.VMEM(down3.shape, BF16),
            pltpu.VMEM(three.shape, BF16),
            pltpu.VMEM(down4.shape, BF16),
            pltpu.VMEM(four.shape, BF16),
            pltpu.SemaphoreType.DMA((5,)),
        ],
        compiler_params=pltpu.CompilerParams(vmem_limit_bytes=52 * MIB),
        name="encoder",
    )(inner, *edges, spread, one, down2, two, down3, three, down4, four)


def level_one_weights(kernel):
    kernel = jnp.pad(kernel, ((0, 0), (0, 0), (0, 16 - BANDS), (0, 0)))
    columns = []
    for rb in range(2):
        for i in range(2):
            for j in range(2):
                top = 1 + 2 * rb + i
                wide = jnp.pad(kernel, ((top, 5 - top), (j, 1 - j), (0, 0), (0, 0)))
                columns.append(wide.transpose(1, 0, 2, 3).reshape(4 * 8 * 16, -1))
    return jnp.concatenate(columns, axis=1)


def level_two_weights(kernel):
    none = ((0, 0),) * 3
    pair = [jnp.pad(kernel, ((i, 1 - i),) + none) for i in range(2)]
    return jnp.concatenate(pair, axis=3).reshape(12 * kernel.shape[2], -1)


def body(
    granule_blocks, row_weights, column_bank, destination, window_index, bank_index,
    kernel_one, reduce_two, kernel_two, reduce_three, kernel_three, reduce_four, kernel_four,
):
    axes = ("tx", "ty")
    tiles = lax.axis_size("tx") * lax.axis_size("ty")
    slots = resample(
        granule_blocks, row_weights, column_bank, destination, window_index, bank_index, tiles
    )
    received = lax.all_to_all(slots, axes, split_axis=0, concat_axis=0, tiled=True)
    gridded, lines, left, right = grid(received)
    from_left, from_right = exchange_columns(left, right)
    main, lower, top, bottom = turn(lines)
    above, below = exchange_rows(top, bottom, from_left, from_right)
    spread = jnp.asarray(spread_matrix(), BF16)
    one = level_one_weights(kernel_one)
    down2 = reduce_two.reshape(256, 128)
    inner = interior(main, lower, from_left, from_right, spread, one, down2)
    flat = encoder(
        inner, (top, bottom, from_left, from_right, above, below), spread, one, down2,
        level_two_weights(kernel_two),
        reduce_three.transpose(1, 0, 2, 3).reshape(2, 256, 256),
        kernel_three.reshape(9 * 256, 256),
        reduce_four.reshape(4, 256, 512),
        kernel_four.reshape(9 * 512, 512),
    )
    return gridded, flat.transpose(2, 0, 1)


def solution(mesh):
    both = P(("tx", "ty"))
    in_specs = (both, both, P(), both, both, both) + (P(),) * 7
    out_specs = (P(None, "ty", "tx"), P(None, "ty", "tx"))
    return jax.shard_map(body, mesh=mesh, in_specs=in_specs, out_specs=out_specs, check_vma=False)
```

```python
import functools

import jax
import jax.numpy as jnp
import numpy as np
from jax import lax
from jax.experimental import pallas as pl
from jax.experimental.pallas import tpu as pltpu
from jax.sharding import PartitionSpec as P

BF16 = jnp.bfloat16
F32 = jnp.float32
BANDS = 13
SRC_ROWS = 16
WIN_ROWS = 8
CAP = 2
NWIN = 32
TILE_COLS = 128
LINES = BANDS * WIN_ROWS
PACKED = CAP * LINES + WIN_ROWS
STEP_BLOCKS = 16
PIECES = 4
PHASES = 8
SPOTS = TILE_COLS // PHASES
HALO = 2
WIDE = SPOTS + 2 * HALO
TALL = NWIN + 2 * HALO
POINTS = WIDE * TALL
GROUP = 4
GROUP_POINTS = GROUP * WIDE
MARGIN = 24
MIB = 1024 * 1024


def dot(a, b):
    return jnp.dot(a, b, preferred_element_type=F32)


def dot_nt(a, b):
    return lax.dot_general(a, b, (((1,), (1,)), ((), ())), preferred_element_type=F32)


def resample_kernel(
    dest_ref, win_ref, choice_ref, weight_ref, raw_hbm, bank_ref, out_ref,
    raw_ref, rows_ref, held_ref, slot_win_ref, sems,
):
    tiles, blocks = held_ref.shape[0], dest_ref.shape[0]
    deep = BANDS * SRC_ROWS

    def fetch(group):
        part = pl.ds(group * STEP_BLOCKS, STEP_BLOCKS)
        return pltpu.make_async_copy(raw_hbm.at[part], raw_ref.at[part], sems.at[group])

    for group in range(blocks // STEP_BLOCKS):
        fetch(group).start()

    def clear(i, carry):
        held_ref[i] = 0
        for k in range(CAP):
            slot_win_ref[i * CAP + k] = -1
        return carry

    lax.fori_loop(0, tiles, clear, 0, unroll=8)

    turned = jnp.transpose(weight_ref[...].astype(F32)).astype(BF16)
    depth = lax.broadcasted_iota(jnp.int32, (WIN_ROWS * SRC_ROWS, 256), 0)
    lane = lax.broadcasted_iota(jnp.int32, (WIN_ROWS * SRC_ROWS, 256), 1)
    offset = depth - (lane & (SRC_ROWS - 1))
    for r in range(WIN_ROWS):
        wide = dot(turned, (offset == r * SRC_ROWS).astype(F32).astype(BF16))
        for h in range(2):
            rows_ref[h, pl.ds(r, blocks, stride=WIN_ROWS), :] = wide[:, h * 128:(h + 1) * 128]

    line = lax.broadcasted_iota(jnp.int32, (LINES, 256), 0)
    lane = lax.broadcasted_iota(jnp.int32, (LINES, 256), 1)
    own = (line >> 3) == (lane >> 4)
    spot = lax.broadcasted_iota(jnp.int32, (WIN_ROWS, TILE_COLS), 1)

    def work(group, carry):
        fetch(group).wait()
        rowed = []
        for j in range(STEP_BLOCKS):
            n = group * STEP_BLOCKS + j
            row = pl.multiple_of(n * WIN_ROWS, WIN_ROWS)
            rows = jnp.concatenate(
                [rows_ref[h, pl.ds(row, WIN_ROWS), :] for h in range(2)], axis=1
            )
            weights = jnp.where(own, jnp.concatenate([rows] * BANDS, axis=0), 0.0)
            rowed.append(dot(weights.astype(BF16)[:, 0:deep], raw_ref[n]).astype(BF16))
        done = []
        for j in range(STEP_BLOCKS):
            n = group * STEP_BLOCKS + j
            done.append(dot(rowed[j], bank_ref[choice_ref[n]]).astype(BF16))
        for j in range(STEP_BLOCKS):
            n = group * STEP_BLOCKS + j
            tile = dest_ref[n]
            rank = held_ref[tile]
            held_ref[tile] = rank + 1
            slot_win_ref[tile * CAP + rank] = win_ref[n]
            place = pl.ds(pl.multiple_of(rank * LINES, WIN_ROWS), LINES)
            out_ref[tile, place, :] = done[j]
        return carry

    lax.fori_loop(0, blocks // STEP_BLOCKS, work, 0)

    def number(i, carry):
        window = jnp.where(spot == 0, slot_win_ref[i * CAP], slot_win_ref[i * CAP + 1])
        out_ref[i, CAP * LINES:] = window.astype(F32).astype(BF16)
        return carry

    lax.fori_loop(0, tiles, number, 0, unroll=4)


def resample(granule_blocks, row_weights, column_bank, destination, window_index, bank_index, tiles):
    blocks = granule_blocks.shape[0]
    deep = BANDS * SRC_ROWS
    vmem = pl.BlockSpec(memory_space=pltpu.VMEM)
    smem = pl.BlockSpec(memory_space=pltpu.SMEM)
    return pl.pallas_call(
        resample_kernel,
        in_specs=[smem, smem, smem, vmem, pl.BlockSpec(memory_space=pl.ANY), vmem],
        out_specs=vmem,
        scratch_shapes=[
            pltpu.VMEM((blocks, deep, TILE_COLS), BF16),
            pltpu.VMEM((2, blocks * WIN_ROWS, 128), F32),
            pltpu.SMEM((tiles,), jnp.int32),
            pltpu.SMEM((tiles * CAP,), jnp.int32),
            pltpu.SemaphoreType.DMA((blocks // STEP_BLOCKS,)),
        ],
        out_shape=jax.ShapeDtypeStruct((tiles, PACKED, TILE_COLS), BF16),
        compiler_params=pltpu.CompilerParams(vmem_limit_bytes=60 * MIB),
        name="resample",
    )(
        destination, window_index, bank_index,
        row_weights.transpose(1, 2, 0).reshape(WIN_ROWS * SRC_ROWS, blocks),
        granule_blocks.reshape(blocks, deep, TILE_COLS),
        column_bank,
    )


def grid_kernel(
    got_hbm, perm_ref, grid_ref, lines_ref, left_ref, right_ref,
    got_ref, sum_ref, number_ref, win_ref, count_ref, sem, sems,
):
    tiles = got_ref.shape[0]
    size = tiles // PIECES
    last = pl.ds(CAP * LINES, WIN_ROWS)
    head = pltpu.make_async_copy(got_hbm.at[:, last], got_ref.at[:, last], sems.at[PIECES])
    head.start()

    def fetch(piece):
        part = pl.ds(piece * size, size), pl.ds(0, CAP * LINES)
        return pltpu.make_async_copy(got_hbm.at[part], got_ref.at[part], sems.at[piece])

    for piece in range(PIECES):
        fetch(piece).start()
    head.wait()
    numbers = got_ref[:, CAP * LINES:, :].astype(F32)
    number_ref[...] = jnp.max(numbers, axis=1).astype(jnp.int32)
    copy = pltpu.make_async_copy(number_ref, win_ref, sem)
    copy.start()

    def clear(w, carry):
        sum_ref[w] = jnp.zeros(sum_ref.shape[1:], F32)
        count_ref[w] = 0
        return carry

    lax.fori_loop(0, NWIN + 1, clear, 0)
    copy.wait()

    def add(t, carry):
        for k in range(CAP):
            w = win_ref[t, k]
            w = jnp.where(w < 0, NWIN, w)
            block = got_ref[t, k * LINES:(k + 1) * LINES].astype(F32)
            sum_ref[w, 0:LINES] = sum_ref[w, 0:LINES] + block
            count_ref[w] = count_ref[w] + 1
        return carry

    def add_piece(piece, carry):
        fetch(piece).wait()
        return lax.fori_loop(piece * size, (piece + 1) * size, add, carry)

    lax.fori_loop(0, PIECES, add_piece, 0)

    def finish(group, carry):
        first = group * GROUP
        means = []
        for k in range(GROUP):
            w = first + k
            divisor = jnp.maximum(count_ref[w], 1).astype(F32)
            mean = (sum_ref[w, 0:LINES] / divisor).astype(BF16).astype(F32)
            sum_ref[w, 0:LINES] = mean
            means.append(mean)
        row = pl.multiple_of(first * WIN_ROWS, GROUP * WIN_ROWS)
        for b in range(BANDS):
            part = jnp.concatenate([m[b * WIN_ROWS:(b + 1) * WIN_ROWS] for m in means], axis=0)
            grid_ref[b, pl.ds(row, GROUP * WIN_ROWS), :] = part.astype(BF16)
        for pair in range(GROUP // 2):
            lines = jnp.concatenate(
                [
                    sum_ref[first + pair * 2 + k, pl.ds(r, 16, stride=WIN_ROWS), :]
                    for k in range(2)
                    for r in range(WIN_ROWS)
                ],
                axis=0,
            ).astype(BF16)
            row = pl.multiple_of((first + pair * 2) * 128, 256)
            lines_ref[pl.ds(row, 256), :] = lines
            both = dot_nt(perm_ref[...], lines).astype(BF16)
            for k in range(2):
                w = first + pair * 2 + k
                turned = both[:, k * 128:(k + 1) * 128]
                left_ref[pl.ds(pl.multiple_of(w * 16, 16), 16), :] = turned[0:16]
                right_ref[pl.ds(pl.multiple_of(w * 16, 16), 16), :] = turned[16:32]
        return carry

    lax.fori_loop(0, NWIN // GROUP, finish, 0)


def grid(received):
    tiles = received.shape[0]
    perm = np.zeros((32, TILE_COLS), np.float32)
    for p in range(PHASES):
        for a in range(HALO):
            perm[p * HALO + a, a * PHASES + p] = 1.0
            perm[16 + p * HALO + a, (SPOTS - HALO + a) * PHASES + p] = 1.0
    vmem = pl.BlockSpec(memory_space=pltpu.VMEM)
    return pl.pallas_call(
        grid_kernel,
        in_specs=[pl.BlockSpec(memory_space=pl.ANY), vmem],
        out_specs=[vmem] * 4,
        out_shape=[
            jax.ShapeDtypeStruct((BANDS, NWIN * WIN_ROWS, TILE_COLS), BF16),
            jax.ShapeDtypeStruct((NWIN * 128, 128), BF16),
            jax.ShapeDtypeStruct((NWIN * 16, 128), BF16),
            jax.ShapeDtypeStruct((NWIN * 16, 128), BF16),
        ],
        scratch_shapes=[
            pltpu.VMEM(received.shape, BF16),
            pltpu.VMEM((NWIN + 1, 128, TILE_COLS), F32),
            pltpu.VMEM((tiles, TILE_COLS), jnp.int32),
            pltpu.SMEM((tiles, TILE_COLS), jnp.int32),
            pltpu.SMEM((NWIN + 1,), jnp.int32),
            pltpu.SemaphoreType.DMA,
            pltpu.SemaphoreType.DMA((PIECES + 1,)),
        ],
        compiler_params=pltpu.CompilerParams(vmem_limit_bytes=24 * MIB),
        name="grid",
    )(received, jnp.asarray(perm, BF16))


def turn_kernel(lines_ref, perm_ref, main_ref, lower_ref, top_ref, bottom_ref):
    def step(i, carry):
        for k in range(2):
            w = i * 2 + k
            start = pl.multiple_of(w * 128, 128)
            below = pl.multiple_of(jnp.minimum(w * 128 + 64, (NWIN - 1) * 128), 64)
            lines = jnp.concatenate(
                [lines_ref[pl.ds(start, 128), :], lines_ref[pl.ds(below, 128), :]], axis=0
            )
            both = dot_nt(perm_ref[...], lines).astype(BF16)
            main_ref[pl.ds(start, 128), :] = both[:, 0:128]
            lower_ref[pl.ds(start, 128), :] = both[:, 128:256]
        return carry

    lax.fori_loop(0, NWIN // 2, step, 0, unroll=2)
    top_ref[...] = main_ref[0:top_ref.shape[0]]
    bottom_ref[...] = main_ref[(NWIN - HALO) * 128:]


def turn(lines):
    perm = np.zeros((TILE_COLS, TILE_COLS), np.float32)
    for p in range(PHASES):
        for a in range(SPOTS):
            perm[p * SPOTS + a, a * PHASES + p] = 1.0
    vmem = pl.BlockSpec(memory_space=pltpu.VMEM)
    return pl.pallas_call(
        turn_kernel,
        in_specs=[vmem] * 2,
        out_specs=[vmem] * 4,
        out_shape=[
            jax.ShapeDtypeStruct((NWIN * 128, 128), BF16),
            jax.ShapeDtypeStruct((NWIN * 128, 128), BF16),
            jax.ShapeDtypeStruct(((HALO + 1) * 128, 128), BF16),
            jax.ShapeDtypeStruct((HALO * 128, 128), BF16),
        ],
        compiler_params=pltpu.CompilerParams(vmem_limit_bytes=16 * MIB),
        cost_estimate=pl.CostEstimate(
            flops=2 * NWIN * 128 ** 3 * 2, bytes_accessed=8 * MIB, transcendentals=0
        ),
        name="turn",
    )(lines, jnp.asarray(perm, BF16))


def exchange_columns(left, right):
    across = lax.axis_size("tx")
    right_ward = [(i, i + 1) for i in range(across - 1)]
    left_ward = [(t, s) for s, t in right_ward]
    return lax.ppermute(right, "tx", right_ward), lax.ppermute(left, "tx", left_ward)


def exchange_rows(top, bottom, from_left, from_right):
    down = lax.axis_size("ty")
    down_ward = [(i, i + 1) for i in range(down - 1)]
    up_ward = [(t, s) for s, t in down_ward]
    m, h = HALO * 128, HALO * 16
    first = jnp.concatenate([top[:m], from_left[:h], from_right[:h]], axis=0)
    last = jnp.concatenate([bottom, from_left[-h:], from_right[-h:]], axis=0)
    return lax.ppermute(last, "ty", down_ward), lax.ppermute(first, "ty", up_ward)


def spread_matrix():
    out = np.zeros((PHASES + 2, GROUP_POINTS, GROUP * 48), np.float32)
    for index in range(PHASES + 2):
        p = (index - 1) % PHASES
        shift = -1 if index == 0 else (1 if index == PHASES + 1 else 0)
        for k in range(GROUP):
            for a in range(WIDE):
                s = a + shift
                row = k * WIDE + a
                if s < 0 or s >= WIDE:
                    continue
                if s < HALO:
                    out[index, row, GROUP * 16 + k * 16 + p * HALO + s] = 1.0
                elif s < HALO + SPOTS:
                    out[index, row, k * 16 + s - HALO] = 1.0
                else:
                    out[index, row, GROUP * 32 + k * 16 + p * HALO + s - HALO - SPOTS] = 1.0
    return out


def relu(x):
    return jnp.maximum(x, 0.0)


def level_one(x1, x2, one_ref, down2_ref, store):
    for cb in range(4):
        for version, x in enumerate((x1, x2)):
            taps = jnp.concatenate([x[2 * cb + k] for k in range(4)], axis=1)
            level = relu(dot(taps, one_ref[...])).astype(BF16)
            for half in range(2):
                down = relu(dot(level[:, half * 256:(half + 1) * 256], down2_ref[...]))
                store(2 * version + half, cb, down)


def lay(spread, first, second):
    return dot(spread, jnp.concatenate([jnp.concatenate(p, axis=0) for p in (first, second)], axis=1))


def interior_kernel(
    main_ref, lower_ref, fl_ref, fr_ref, spread_ref, one_ref, down2_ref, out_ref, side_ref, x1, x2
):
    low = lax.broadcasted_iota(jnp.int32, (16, 128), 1) < 64
    for s, side in enumerate((fl_ref, fr_ref)):
        for w in range(NWIN - 1):
            after = side[(w + 1) * 16:(w + 2) * 16].astype(F32)
            both = jnp.where(low, after, side[w * 16:(w + 1) * 16].astype(F32))
            side_ref[s, w * 16:(w + 1) * 16] = pltpu.roll(both, 64, 1).astype(BF16)

    def place(g, carry):
        row = pl.multiple_of(g * GROUP_POINTS, GROUP_POINTS)
        w = g * GROUP + GROUP - HALO
        edge = [pl.ds(pl.multiple_of((w + k) * 16, 16), 16) for k in range(GROUP)]
        for index in range(PHASES + 2):
            p = (index - 1) % PHASES
            own = [
                pl.ds(pl.multiple_of((w + k) * 128 + p * 16, 16), 16) for k in range(GROUP)
            ]
            first = [main_ref[o, :] for o in own]
            first += [ref[e, :] for ref in (fl_ref, fr_ref) for e in edge]
            second = [lower_ref[o, :] for o in own]
            second += [side_ref[s, e, :] for s in range(2) for e in edge]
            laid = lay(spread_ref[index], first, second).astype(BF16)
            x1[index, pl.ds(row, GROUP_POINTS), :] = laid[:, 0:128]
            x2[index, pl.ds(row, GROUP_POINTS), :] = laid[:, 128:256]
        return carry

    lax.fori_loop(0, TALL // GROUP - 2, place, 0)

    def store(rb, cb, down):
        out_ref[rb, cb] = down.astype(BF16)

    level_one(x1, x2, one_ref, down2_ref, store)


def interior(main, lower, from_left, from_right, spread, one, down2):
    vmem = pl.BlockSpec(memory_space=pltpu.VMEM)
    points = POINTS - 2 * GROUP_POINTS
    return pl.pallas_call(
        interior_kernel,
        in_specs=[vmem] * 7,
        out_specs=vmem,
        out_shape=jax.ShapeDtypeStruct((4, 4, points, 128), BF16),
        scratch_shapes=[
            pltpu.VMEM((2, NWIN * 16, 128), BF16),
            pltpu.VMEM((PHASES + 2, points, 128), BF16),
            pltpu.VMEM((PHASES + 2, points, 128), BF16),
        ],
        compiler_params=pltpu.CompilerParams(vmem_limit_bytes=32 * MIB),
        cost_estimate=pl.CostEstimate(
            flops=2 * points * 8 * (512 * 512 + 512 * 256),
            bytes_accessed=16 * MIB,
            transcendentals=0,
        ),
        name="interior",
    )(main, lower, from_left, from_right, spread, one, down2)


def encoder_kernel(
    inner_hbm, top_ref, bottom_ref, fl_ref, fr_ref, above_ref, below_ref, spread_ref, one_ref,
    down2_ref, two_hbm, down3_hbm, three_hbm, down4_hbm, four_hbm,
    out_ref,
    inner_ref, ext1, ext2, x1, x2, d2, d3, d4, flat, stage,
    two_ref, down3_ref, three_ref, down4_ref, four_ref, sems,
):
    copies = [
        pltpu.make_async_copy(src, dst, sems.at[i])
        for i, (src, dst) in enumerate(
            (
                (down3_hbm, down3_ref),
                (three_hbm, three_ref),
                (down4_hbm, down4_ref),
                (four_hbm, four_ref),
                (inner_hbm, inner_ref),
                (two_hbm, two_ref),
            )
        )
    ]
    for i in (4, 5, 0, 1, 2, 3):
        copies[i].start()
    for side in range(2):
        for p in range(4):
            stage[side, p, 0:MARGIN] = jnp.zeros((MARGIN, 128), F32)
            stage[side, p, MARGIN + POINTS:] = jnp.zeros((MARGIN, 128), F32)

    m = HALO * 128
    for h in range(HALO):
        for source, i in ((above_ref, h), (below_ref, 3 * HALO + 1 + h)):
            ext1[i, 0:128] = source[h * 128:(h + 1) * 128]
            ext1[i, 128:144] = source[m + h * 16:m + h * 16 + 16]
            ext1[i, 144:160] = source[m + (HALO + h) * 16:m + (HALO + h) * 16 + 16]
    near = [(HALO + k, top_ref, k, k) for k in range(HALO + 1)]
    near += [(2 * HALO + 1 + k, bottom_ref, k, NWIN - HALO + k) for k in range(HALO)]
    for i, source, k, w in near:
        ext1[i, 0:128] = source[k * 128:(k + 1) * 128]
        ext1[i, 128:144] = fl_ref[w * 16:(w + 1) * 16]
        ext1[i, 144:160] = fr_ref[w * 16:(w + 1) * 16]

    low = lax.broadcasted_iota(jnp.int32, (160, 128), 1) < 64
    edges = (0, GROUP + 1)
    for base in edges:
        for k in range(GROUP):
            i = base + k
            after = min(i + 1, ext1.shape[0] - 1)
            both = jnp.where(low, ext1[after].astype(F32), ext1[i].astype(F32))
            ext2[i] = pltpu.roll(both, 64, 1).astype(BF16)

    for e, base in enumerate(edges):
        for index in range(PHASES + 2):
            p = (index - 1) % PHASES
            sides = []
            for ext in (ext1, ext2):
                pieces = [ext[base + k, p * 16:(p + 1) * 16] for k in range(GROUP)]
                pieces += [ext[base + k, 128:144] for k in range(GROUP)]
                pieces += [ext[base + k, 144:160] for k in range(GROUP)]
                sides.append(pieces)
            laid = lay(spread_ref[index], *sides).astype(BF16)
            x1[index, e * GROUP_POINTS:(e + 1) * GROUP_POINTS] = laid[:, 0:128]
            x2[index, e * GROUP_POINTS:(e + 1) * GROUP_POINTS] = laid[:, 128:256]

    across, below = lax.axis_size("tx"), lax.axis_size("ty")
    x, y = lax.axis_index("tx"), lax.axis_index("ty")
    least_w, most_w = jnp.where(y > 0, 0, HALO), jnp.where(y < below - 1, TALL, HALO + NWIN)
    least_a, most_a = jnp.where(x > 0, 0, HALO), jnp.where(x < across - 1, WIDE, HALO + SPOTS)
    point = lax.broadcasted_iota(jnp.int32, (POINTS, 128), 0)
    w = (point * (65536 // WIDE + 1)) >> 16
    a = point - w * WIDE
    inside = (w >= least_w) & (w < most_w) & (a >= least_a) & (a < most_a)
    mask = inside.astype(F32)
    mask2 = jnp.concatenate([mask, mask], axis=1)
    mask4 = jnp.concatenate([mask2, mask2], axis=1)

    def put(dst, i, j, value, last):
        rows = [(i + 1, 0)]
        if i == last:
            rows.append((0, WIDE))
        if i == 0:
            rows.append((last + 2, -WIDE))
        cols = [(j + 1, 0)]
        if j == last:
            cols.append((0, 1))
        if j == 0:
            cols.append((last + 2, -1))
        dst[i + 1, j + 1] = value.astype(BF16)
        side = (i + j) % 2
        for p in range(value.shape[1] // 128):
            lanes = slice(p * 128, (p + 1) * 128)
            stage[side, p, MARGIN:MARGIN + POINTS] = value[:, lanes]
            for r, row_shift in rows:
                for c, col_shift in cols:
                    shift = row_shift + col_shift
                    if shift:
                        moved = stage[side, p, MARGIN - shift:MARGIN - shift + POINTS]
                        dst[r, c, :, lanes] = moved.astype(BF16)

    copies[4].wait()

    def store(rb, cb, down):
        inner = inner_ref[rb, cb].astype(F32)
        down = jnp.concatenate([down[:GROUP_POINTS], inner, down[GROUP_POINTS:]], axis=0)
        if rb == 3:
            down = pltpu.roll(down, WIDE, 0)
        put(d2, (rb + 1) % 4, cb, down * mask, 3)

    level_one(x1, x2, one_ref, down2_ref, store)

    copies[5].wait()
    copies[0].wait()
    for rp in range(2):
        for j in range(2):
            total = None
            for v2 in range(2):
                taps = jnp.concatenate(
                    [d2[2 * rp + r, 2 * j + v2 + v] for r in range(4) for v in range(3)], axis=1
                )
                level = relu(dot(taps, two_ref[...])).astype(BF16)
                part = dot(level, down3_ref[v2])
                total = part if total is None else total + part
            put(d3, rp, j, relu(total) * mask2, 1)

    copies[1].wait()
    copies[2].wait()
    total = None
    for i in range(2):
        for j in range(2):
            taps = jnp.concatenate(
                [d3[i + u, j + v] for u in range(3) for v in range(3)], axis=1
            )
            level = relu(dot(taps, three_ref[...])).astype(BF16)
            part = dot(level, down4_ref[i * 2 + j])
            total = part if total is None else total + part
    put(d4, 0, 0, relu(total) * mask4, 0)

    copies[3].wait()
    first, count = HALO * WIDE, NWIN * WIDE
    taps = jnp.concatenate(
        [d4[u, v, first:first + count] for u in range(3) for v in range(3)], axis=1
    )
    flat[...] = relu(dot(taps, four_ref[...]))
    for w in range(NWIN):
        start = w * WIDE + HALO
        out_ref[w] = flat[start:start + SPOTS].astype(BF16)


def encoder(inner, edges, spread, one, down2, two, down3, three, down4, four):
    vmem = pl.BlockSpec(memory_space=pltpu.VMEM)
    hbm = pl.BlockSpec(memory_space=pl.ANY)
    rim = 2 * GROUP_POINTS
    return pl.pallas_call(
        encoder_kernel,
        in_specs=[hbm] + [vmem] * 9 + [hbm] * 5,
        out_specs=vmem,
        out_shape=jax.ShapeDtypeStruct((NWIN, SPOTS, four.shape[-1]), BF16),
        scratch_shapes=[
            pltpu.VMEM(inner.shape, BF16),
            pltpu.VMEM((2 * GROUP + 1, 160, 128), BF16),
            pltpu.VMEM((2 * GROUP + 1, 160, 128), BF16),
            pltpu.VMEM((PHASES + 2, rim, 128), BF16),
            pltpu.VMEM((PHASES + 2, rim, 128), BF16),
            pltpu.VMEM((6, 6, POINTS, 128), BF16),
            pltpu.VMEM((4, 4, POINTS, 256), BF16),
            pltpu.VMEM((3, 3, POINTS, 512), BF16),
            pltpu.VMEM((NWIN * WIDE, 512), F32),
            pltpu.VMEM((2, 4, POINTS + 2 * MARGIN, 128), F32),
            pltpu.VMEM(two.shape, BF16),
            pltpu.VMEM(down3.shape, BF16),
            pltpu.VMEM(three.shape, BF16),
            pltpu.VMEM(down4.shape, BF16),
            pltpu.VMEM(four.shape, BF16),
            pltpu.SemaphoreType.DMA((6,)),
        ],
        compiler_params=pltpu.CompilerParams(vmem_limit_bytes=44 * MIB),
        name="encoder",
    )(inner, *edges, spread, one, down2, two, down3, three, down4, four)


def level_one_weights(kernel):
    kernel = jnp.pad(kernel, ((0, 0), (0, 0), (0, 16 - BANDS), (0, 0)))
    columns = []
    for rb in range(2):
        for i in range(2):
            for j in range(2):
                top = 1 + 2 * rb + i
                wide = jnp.pad(kernel, ((top, 5 - top), (j, 1 - j), (0, 0), (0, 0)))
                columns.append(wide.transpose(1, 0, 2, 3).reshape(4 * 8 * 16, -1))
    return jnp.concatenate(columns, axis=1)


def level_two_weights(kernel):
    none = ((0, 0),) * 3
    pair = [jnp.pad(kernel, ((i, 1 - i),) + none) for i in range(2)]
    return jnp.concatenate(pair, axis=3).reshape(12 * kernel.shape[2], -1)


def body(
    granule_blocks, row_weights, column_bank, destination, window_index, bank_index,
    kernel_one, reduce_two, kernel_two, reduce_three, kernel_three, reduce_four, kernel_four,
):
    axes = ("tx", "ty")
    tiles = lax.axis_size("tx") * lax.axis_size("ty")
    slots = resample(
        granule_blocks, row_weights, column_bank, destination, window_index, bank_index, tiles
    )
    received = lax.all_to_all(slots, axes, split_axis=0, concat_axis=0, tiled=True)
    one = level_one_weights(kernel_one)
    two = level_two_weights(kernel_two)
    down3 = reduce_three.transpose(1, 0, 2, 3).reshape(2, 256, 256)
    received, one, two, down3 = lax.optimization_barrier((received, one, two, down3))
    gridded, lines, left, right = grid(received)
    from_left, from_right = exchange_columns(left, right)
    main, lower, top, bottom = turn(lines)
    above, below = exchange_rows(top, bottom, from_left, from_right)
    spread = jnp.asarray(spread_matrix(), BF16)
    down2 = reduce_two.reshape(256, 128)
    inner = interior(main, lower, from_left, from_right, spread, one, down2)
    flat = encoder(
        inner, (top, bottom, from_left, from_right, above, below), spread, one, down2,
        two, down3,
        kernel_three.reshape(9 * 256, 256),
        reduce_four.reshape(4, 256, 512),
        kernel_four.reshape(9 * 512, 512),
    )
    return gridded, flat.transpose(2, 0, 1)


def solution(mesh):
    both = P(("tx", "ty"))
    in_specs = (both, both, P(), both, both, both) + (P(),) * 7
    out_specs = (P(None, "ty", "tx"), P(None, "ty", "tx"))
    return jax.shard_map(body, mesh=mesh, in_specs=in_specs, out_specs=out_specs, check_vma=False)
```

```python
import functools

import jax
import jax.numpy as jnp
import numpy as np
from jax import lax
from jax.experimental import pallas as pl
from jax.experimental.pallas import tpu as pltpu
from jax.sharding import PartitionSpec as P

BF16 = jnp.bfloat16
F32 = jnp.float32
BANDS = 13
SRC_ROWS = 16
WIN_ROWS = 8
CAP = 2
NWIN = 32
TILE_COLS = 128
LINES = BANDS * WIN_ROWS
PACKED = CAP * LINES + WIN_ROWS
STEP_BLOCKS = 16
PIECES = 4
PHASES = 8
SPOTS = TILE_COLS // PHASES
HALO = 2
WIDE = SPOTS + 2 * HALO
TALL = NWIN + 2 * HALO
POINTS = WIDE * TALL
GROUP = 4
GROUP_POINTS = GROUP * WIDE
MARGIN = 24
MIB = 1024 * 1024


def dot(a, b):
    return jnp.dot(a, b, preferred_element_type=F32)


def dot_nt(a, b):
    return lax.dot_general(a, b, (((1,), (1,)), ((), ())), preferred_element_type=F32)


def resample_kernel(
    dest_ref, win_ref, choice_ref, weight_ref, raw_hbm, bank_ref, out_ref,
    raw_ref, rows_ref, held_ref, slot_win_ref, sems,
):
    tiles, blocks = held_ref.shape[0], dest_ref.shape[0]
    deep = BANDS * SRC_ROWS

    def fetch(group):
        part = pl.ds(group * STEP_BLOCKS, STEP_BLOCKS)
        return pltpu.make_async_copy(raw_hbm.at[part], raw_ref.at[part], sems.at[group])

    for group in range(blocks // STEP_BLOCKS):
        fetch(group).start()

    def clear(i, carry):
        held_ref[i] = 0
        for k in range(CAP):
            slot_win_ref[i * CAP + k] = -1
        return carry

    lax.fori_loop(0, tiles, clear, 0, unroll=8)

    turned = jnp.transpose(weight_ref[...].astype(F32)).astype(BF16)
    depth = lax.broadcasted_iota(jnp.int32, (WIN_ROWS * SRC_ROWS, 256), 0)
    lane = lax.broadcasted_iota(jnp.int32, (WIN_ROWS * SRC_ROWS, 256), 1)
    offset = depth - (lane & (SRC_ROWS - 1))
    for r in range(WIN_ROWS):
        wide = dot(turned, (offset == r * SRC_ROWS).astype(F32).astype(BF16))
        for h in range(2):
            rows_ref[h, pl.ds(r, blocks, stride=WIN_ROWS), :] = wide[:, h * 128:(h + 1) * 128]

    line = lax.broadcasted_iota(jnp.int32, (LINES, 256), 0)
    lane = lax.broadcasted_iota(jnp.int32, (LINES, 256), 1)
    own = (line >> 3) == (lane >> 4)
    spot = lax.broadcasted_iota(jnp.int32, (WIN_ROWS, TILE_COLS), 1)

    def work(group, carry):
        fetch(group).wait()
        rowed = []
        for j in range(STEP_BLOCKS):
            n = group * STEP_BLOCKS + j
            row = pl.multiple_of(n * WIN_ROWS, WIN_ROWS)
            rows = jnp.concatenate(
                [rows_ref[h, pl.ds(row, WIN_ROWS), :] for h in range(2)], axis=1
            )
            weights = jnp.where(own, jnp.concatenate([rows] * BANDS, axis=0), 0.0)
            rowed.append(dot(weights.astype(BF16)[:, 0:deep], raw_ref[n]).astype(BF16))
        done = []
        for j in range(STEP_BLOCKS):
            n = group * STEP_BLOCKS + j
            done.append(dot(rowed[j], bank_ref[choice_ref[n]]).astype(BF16))
        for j in range(STEP_BLOCKS):
            n = group * STEP_BLOCKS + j
            tile = dest_ref[n]
            rank = held_ref[tile]
            held_ref[tile] = rank + 1
            slot_win_ref[tile * CAP + rank] = win_ref[n]
            place = pl.ds(pl.multiple_of(rank * LINES, WIN_ROWS), LINES)
            out_ref[tile, place, :] = done[j]
        return carry

    lax.fori_loop(0, blocks // STEP_BLOCKS, work, 0)

    def number(i, carry):
        window = jnp.where(spot == 0, slot_win_ref[i * CAP], slot_win_ref[i * CAP + 1])
        out_ref[i, CAP * LINES:] = window.astype(F32).astype(BF16)
        return carry

    lax.fori_loop(0, tiles, number, 0, unroll=4)


def resample(granule_blocks, row_weights, column_bank, destination, window_index, bank_index, tiles):
    blocks = granule_blocks.shape[0]
    deep = BANDS * SRC_ROWS
    vmem = pl.BlockSpec(memory_space=pltpu.VMEM)
    smem = pl.BlockSpec(memory_space=pltpu.SMEM)
    return pl.pallas_call(
        resample_kernel,
        in_specs=[smem, smem, smem, vmem, pl.BlockSpec(memory_space=pl.ANY), vmem],
        out_specs=vmem,
        scratch_shapes=[
            pltpu.VMEM((blocks, deep, TILE_COLS), BF16),
            pltpu.VMEM((2, blocks * WIN_ROWS, 128), F32),
            pltpu.SMEM((tiles,), jnp.int32),
            pltpu.SMEM((tiles * CAP,), jnp.int32),
            pltpu.SemaphoreType.DMA((blocks // STEP_BLOCKS,)),
        ],
        out_shape=jax.ShapeDtypeStruct((tiles, PACKED, TILE_COLS), BF16),
        compiler_params=pltpu.CompilerParams(vmem_limit_bytes=60 * MIB),
        name="resample",
    )(
        destination, window_index, bank_index,
        row_weights.transpose(1, 2, 0).reshape(WIN_ROWS * SRC_ROWS, blocks),
        granule_blocks.reshape(blocks, deep, TILE_COLS),
        column_bank,
    )


def grid_kernel(
    got_hbm, perm_ref, grid_ref, lines_ref, left_ref, right_ref,
    got_ref, sum_ref, number_ref, win_ref, count_ref, sem, sems,
):
    tiles = got_ref.shape[0]
    size = tiles // PIECES
    last = pl.ds(CAP * LINES, WIN_ROWS)
    head = pltpu.make_async_copy(got_hbm.at[:, last], got_ref.at[:, last], sems.at[PIECES])
    head.start()

    def fetch(piece):
        part = pl.ds(piece * size, size), pl.ds(0, CAP * LINES)
        return pltpu.make_async_copy(got_hbm.at[part], got_ref.at[part], sems.at[piece])

    for piece in range(PIECES):
        fetch(piece).start()
    head.wait()
    numbers = got_ref[:, CAP * LINES:, :].astype(F32)
    number_ref[...] = jnp.max(numbers, axis=1).astype(jnp.int32)
    copy = pltpu.make_async_copy(number_ref, win_ref, sem)
    copy.start()

    def clear(w, carry):
        sum_ref[w] = jnp.zeros(sum_ref.shape[1:], F32)
        count_ref[w] = 0
        return carry

    lax.fori_loop(0, NWIN + 1, clear, 0)
    copy.wait()

    def add(t, carry):
        for k in range(CAP):
            w = win_ref[t, k]
            w = jnp.where(w < 0, NWIN, w)
            block = got_ref[t, k * LINES:(k + 1) * LINES].astype(F32)
            sum_ref[w, 0:LINES] = sum_ref[w, 0:LINES] + block
            count_ref[w] = count_ref[w] + 1
        return carry

    def add_piece(piece, carry):
        fetch(piece).wait()
        return lax.fori_loop(piece * size, (piece + 1) * size, add, carry)

    lax.fori_loop(0, PIECES, add_piece, 0)

    def finish(group, carry):
        first = group * GROUP
        means = []
        for k in range(GROUP):
            w = first + k
            divisor = jnp.maximum(count_ref[w], 1).astype(F32)
            mean = (sum_ref[w, 0:LINES] / divisor).astype(BF16).astype(F32)
            sum_ref[w, 0:LINES] = mean
            means.append(mean)
        row = pl.multiple_of(first * WIN_ROWS, GROUP * WIN_ROWS)
        for b in range(BANDS):
            part = jnp.concatenate([m[b * WIN_ROWS:(b + 1) * WIN_ROWS] for m in means], axis=0)
            grid_ref[b, pl.ds(row, GROUP * WIN_ROWS), :] = part.astype(BF16)
        for pair in range(GROUP // 2):
            lines = jnp.concatenate(
                [
                    sum_ref[first + pair * 2 + k, pl.ds(r, 16, stride=WIN_ROWS), :]
                    for k in range(2)
                    for r in range(WIN_ROWS)
                ],
                axis=0,
            ).astype(BF16)
            row = pl.multiple_of((first + pair * 2) * 128, 256)
            lines_ref[pl.ds(row, 256), :] = lines
            both = dot_nt(perm_ref[...], lines).astype(BF16)
            for k in range(2):
                w = first + pair * 2 + k
                turned = both[:, k * 128:(k + 1) * 128]
                left_ref[pl.ds(pl.multiple_of(w * 16, 16), 16), :] = turned[0:16]
                right_ref[pl.ds(pl.multiple_of(w * 16, 16), 16), :] = turned[16:32]
        return carry

    lax.fori_loop(0, NWIN // GROUP, finish, 0)


def grid(received):
    tiles = received.shape[0]
    perm = np.zeros((32, TILE_COLS), np.float32)
    for p in range(PHASES):
        for a in range(HALO):
            perm[p * HALO + a, a * PHASES + p] = 1.0
            perm[16 + p * HALO + a, (SPOTS - HALO + a) * PHASES + p] = 1.0
    vmem = pl.BlockSpec(memory_space=pltpu.VMEM)
    return pl.pallas_call(
        grid_kernel,
        in_specs=[pl.BlockSpec(memory_space=pl.ANY), vmem],
        out_specs=[vmem] * 4,
        out_shape=[
            jax.ShapeDtypeStruct((BANDS, NWIN * WIN_ROWS, TILE_COLS), BF16),
            jax.ShapeDtypeStruct((NWIN * 128, 128), BF16),
            jax.ShapeDtypeStruct((NWIN * 16, 128), BF16),
            jax.ShapeDtypeStruct((NWIN * 16, 128), BF16),
        ],
        scratch_shapes=[
            pltpu.VMEM(received.shape, BF16),
            pltpu.VMEM((NWIN + 1, 128, TILE_COLS), F32),
            pltpu.VMEM((tiles, TILE_COLS), jnp.int32),
            pltpu.SMEM((tiles, TILE_COLS), jnp.int32),
            pltpu.SMEM((NWIN + 1,), jnp.int32),
            pltpu.SemaphoreType.DMA,
            pltpu.SemaphoreType.DMA((PIECES + 1,)),
        ],
        compiler_params=pltpu.CompilerParams(vmem_limit_bytes=24 * MIB),
        name="grid",
    )(received, jnp.asarray(perm, BF16))


def turn_kernel(lines_ref, perm_ref, main_ref, lower_ref, top_ref, bottom_ref):
    def step(i, carry):
        for k in range(2):
            w = i * 2 + k
            start = pl.multiple_of(w * 128, 128)
            below = pl.multiple_of(jnp.minimum(w * 128 + 64, (NWIN - 1) * 128), 64)
            lines = jnp.concatenate(
                [lines_ref[pl.ds(start, 128), :], lines_ref[pl.ds(below, 128), :]], axis=0
            )
            both = dot_nt(perm_ref[...], lines).astype(BF16)
            main_ref[pl.ds(start, 128), :] = both[:, 0:128]
            lower_ref[pl.ds(start, 128), :] = both[:, 128:256]
        return carry

    lax.fori_loop(0, NWIN // 2, step, 0, unroll=2)
    top_ref[...] = main_ref[0:top_ref.shape[0]]
    bottom_ref[...] = main_ref[(NWIN - HALO) * 128:]


def turn(lines):
    perm = np.zeros((TILE_COLS, TILE_COLS), np.float32)
    for p in range(PHASES):
        for a in range(SPOTS):
            perm[p * SPOTS + a, a * PHASES + p] = 1.0
    vmem = pl.BlockSpec(memory_space=pltpu.VMEM)
    return pl.pallas_call(
        turn_kernel,
        in_specs=[vmem] * 2,
        out_specs=[vmem] * 4,
        out_shape=[
            jax.ShapeDtypeStruct((NWIN * 128, 128), BF16),
            jax.ShapeDtypeStruct((NWIN * 128, 128), BF16),
            jax.ShapeDtypeStruct(((HALO + 1) * 128, 128), BF16),
            jax.ShapeDtypeStruct((HALO * 128, 128), BF16),
        ],
        compiler_params=pltpu.CompilerParams(vmem_limit_bytes=16 * MIB),
        cost_estimate=pl.CostEstimate(
            flops=2 * NWIN * 128 ** 3 * 2, bytes_accessed=8 * MIB, transcendentals=0
        ),
        name="turn",
    )(lines, jnp.asarray(perm, BF16))


def exchange_columns(left, right):
    across = lax.axis_size("tx")
    right_ward = [(i, i + 1) for i in range(across - 1)]
    left_ward = [(t, s) for s, t in right_ward]
    return lax.ppermute(right, "tx", right_ward), lax.ppermute(left, "tx", left_ward)


def exchange_rows(top, bottom, from_left, from_right):
    down = lax.axis_size("ty")
    down_ward = [(i, i + 1) for i in range(down - 1)]
    up_ward = [(t, s) for s, t in down_ward]
    m, h = HALO * 128, HALO * 16
    first = jnp.concatenate([top[:m], from_left[:h], from_right[:h]], axis=0)
    last = jnp.concatenate([bottom, from_left[-h:], from_right[-h:]], axis=0)
    return lax.ppermute(last, "ty", down_ward), lax.ppermute(first, "ty", up_ward)


def spread_matrix():
    out = np.zeros((PHASES + 2, GROUP_POINTS, GROUP * 48), np.float32)
    for index in range(PHASES + 2):
        p = (index - 1) % PHASES
        shift = -1 if index == 0 else (1 if index == PHASES + 1 else 0)
        for k in range(GROUP):
            for a in range(WIDE):
                s = a + shift
                row = k * WIDE + a
                if s < 0 or s >= WIDE:
                    continue
                if s < HALO:
                    out[index, row, GROUP * 16 + k * 16 + p * HALO + s] = 1.0
                elif s < HALO + SPOTS:
                    out[index, row, k * 16 + s - HALO] = 1.0
                else:
                    out[index, row, GROUP * 32 + k * 16 + p * HALO + s - HALO - SPOTS] = 1.0
    return out


def relu(x):
    return jnp.maximum(x, 0.0)


def level_one(x1, x2, one_ref, down2_ref, store):
    for cb in range(4):
        for version, x in enumerate((x1, x2)):
            taps = jnp.concatenate([x[2 * cb + k] for k in range(4)], axis=1)
            level = relu(dot(taps, one_ref[...])).astype(BF16)
            for half in range(2):
                down = relu(dot(level[:, half * 256:(half + 1) * 256], down2_ref[...]))
                store(2 * version + half, cb, down)


def lay(spread, first, second):
    return dot(spread, jnp.concatenate([jnp.concatenate(p, axis=0) for p in (first, second)], axis=1))


def interior_kernel(
    main_ref, lower_ref, fl_ref, fr_ref, spread_ref, one_ref, down2_ref, out_ref, side_ref, x1, x2
):
    low = lax.broadcasted_iota(jnp.int32, (16, 128), 1) < 64
    for s, side in enumerate((fl_ref, fr_ref)):
        for w in range(NWIN - 1):
            after = side[(w + 1) * 16:(w + 2) * 16].astype(F32)
            both = jnp.where(low, after, side[w * 16:(w + 1) * 16].astype(F32))
            side_ref[s, w * 16:(w + 1) * 16] = pltpu.roll(both, 64, 1).astype(BF16)

    def place(g, carry):
        row = pl.multiple_of(g * GROUP_POINTS, GROUP_POINTS)
        w = g * GROUP + GROUP - HALO
        edge = [pl.ds(pl.multiple_of((w + k) * 16, 16), 16) for k in range(GROUP)]
        for index in range(PHASES + 2):
            p = (index - 1) % PHASES
            own = [
                pl.ds(pl.multiple_of((w + k) * 128 + p * 16, 16), 16) for k in range(GROUP)
            ]
            first = [main_ref[o, :] for o in own]
            first += [ref[e, :] for ref in (fl_ref, fr_ref) for e in edge]
            second = [lower_ref[o, :] for o in own]
            second += [side_ref[s, e, :] for s in range(2) for e in edge]
            laid = lay(spread_ref[index], first, second).astype(BF16)
            x1[index, pl.ds(row, GROUP_POINTS), :] = laid[:, 0:128]
            x2[index, pl.ds(row, GROUP_POINTS), :] = laid[:, 128:256]
        return carry

    lax.fori_loop(0, TALL // GROUP - 2, place, 0)

    def store(rb, cb, down):
        out_ref[rb, cb] = down.astype(BF16)

    level_one(x1, x2, one_ref, down2_ref, store)


def interior(main, lower, from_left, from_right, spread, one, down2):
    vmem = pl.BlockSpec(memory_space=pltpu.VMEM)
    points = POINTS - 2 * GROUP_POINTS
    return pl.pallas_call(
        interior_kernel,
        in_specs=[vmem] * 7,
        out_specs=vmem,
        out_shape=jax.ShapeDtypeStruct((4, 4, points, 128), BF16),
        scratch_shapes=[
            pltpu.VMEM((2, NWIN * 16, 128), BF16),
            pltpu.VMEM((PHASES + 2, points, 128), BF16),
            pltpu.VMEM((PHASES + 2, points, 128), BF16),
        ],
        compiler_params=pltpu.CompilerParams(vmem_limit_bytes=32 * MIB),
        cost_estimate=pl.CostEstimate(
            flops=2 * points * 8 * (512 * 512 + 512 * 256),
            bytes_accessed=16 * MIB,
            transcendentals=0,
        ),
        name="interior",
    )(main, lower, from_left, from_right, spread, one, down2)


def encoder_kernel(
    inner_hbm, top_ref, bottom_ref, fl_ref, fr_ref, above_ref, below_ref, spread_ref, one_ref,
    down2_ref, two_hbm, down3_hbm, three_hbm, down4_hbm, four_hbm,
    out_ref,
    inner_ref, ext1, ext2, x1, x2, d2, d3, d4, flat, stage,
    two_ref, down3_ref, three_ref, down4_ref, four_ref, sems,
):
    copies = [
        pltpu.make_async_copy(src, dst, sems.at[i])
        for i, (src, dst) in enumerate(
            (
                (down3_hbm, down3_ref),
                (three_hbm, three_ref),
                (down4_hbm, down4_ref),
                (four_hbm, four_ref),
                (inner_hbm, inner_ref),
                (two_hbm, two_ref),
            )
        )
    ]
    for i in (4, 5, 0, 1, 2, 3):
        copies[i].start()
    for side in range(2):
        for p in range(4):
            stage[side, p, 0:MARGIN] = jnp.zeros((MARGIN, 128), F32)
            stage[side, p, MARGIN + POINTS:] = jnp.zeros((MARGIN, 128), F32)

    m = HALO * 128
    for h in range(HALO):
        for source, i in ((above_ref, h), (below_ref, 3 * HALO + 1 + h)):
            ext1[i, 0:128] = source[h * 128:(h + 1) * 128]
            ext1[i, 128:144] = source[m + h * 16:m + h * 16 + 16]
            ext1[i, 144:160] = source[m + (HALO + h) * 16:m + (HALO + h) * 16 + 16]
    near = [(HALO + k, top_ref, k, k) for k in range(HALO + 1)]
    near += [(2 * HALO + 1 + k, bottom_ref, k, NWIN - HALO + k) for k in range(HALO)]
    for i, source, k, w in near:
        ext1[i, 0:128] = source[k * 128:(k + 1) * 128]
        ext1[i, 128:144] = fl_ref[w * 16:(w + 1) * 16]
        ext1[i, 144:160] = fr_ref[w * 16:(w + 1) * 16]

    low = lax.broadcasted_iota(jnp.int32, (160, 128), 1) < 64
    edges = (0, GROUP + 1)
    for base in edges:
        for k in range(GROUP):
            i = base + k
            after = min(i + 1, ext1.shape[0] - 1)
            both = jnp.where(low, ext1[after].astype(F32), ext1[i].astype(F32))
            ext2[i] = pltpu.roll(both, 64, 1).astype(BF16)

    for e, base in enumerate(edges):
        for index in range(PHASES + 2):
            p = (index - 1) % PHASES
            sides = []
            for ext in (ext1, ext2):
                pieces = [ext[base + k, p * 16:(p + 1) * 16] for k in range(GROUP)]
                pieces += [ext[base + k, 128:144] for k in range(GROUP)]
                pieces += [ext[base + k, 144:160] for k in range(GROUP)]
                sides.append(pieces)
            laid = lay(spread_ref[index], *sides).astype(BF16)
            x1[index, e * GROUP_POINTS:(e + 1) * GROUP_POINTS] = laid[:, 0:128]
            x2[index, e * GROUP_POINTS:(e + 1) * GROUP_POINTS] = laid[:, 128:256]

    across, below = lax.axis_size("tx"), lax.axis_size("ty")
    x, y = lax.axis_index("tx"), lax.axis_index("ty")
    least_w, most_w = jnp.where(y > 0, 0, HALO), jnp.where(y < below - 1, TALL, HALO + NWIN)
    least_a, most_a = jnp.where(x > 0, 0, HALO), jnp.where(x < across - 1, WIDE, HALO + SPOTS)
    point = lax.broadcasted_iota(jnp.int32, (POINTS, 128), 0)
    w = (point * (65536 // WIDE + 1)) >> 16
    a = point - w * WIDE
    inside = (w >= least_w) & (w < most_w) & (a >= least_a) & (a < most_a)
    mask = inside.astype(F32)
    mask2 = jnp.concatenate([mask, mask], axis=1)
    mask4 = jnp.concatenate([mask2, mask2], axis=1)

    def put(dst, i, j, value, last):
        rows = [(i + 1, 0)]
        if i == last:
            rows.append((0, WIDE))
        if i == 0:
            rows.append((last + 2, -WIDE))
        cols = [(j + 1, 0)]
        if j == last:
            cols.append((0, 1))
        if j == 0:
            cols.append((last + 2, -1))
        dst[i + 1, j + 1] = value.astype(BF16)
        side = (i + j) % 2
        for p in range(value.shape[1] // 128):
            lanes = slice(p * 128, (p + 1) * 128)
            stage[side, p, MARGIN:MARGIN + POINTS] = value[:, lanes]
            for r, row_shift in rows:
                for c, col_shift in cols:
                    shift = row_shift + col_shift
                    if shift:
                        moved = stage[side, p, MARGIN - shift:MARGIN - shift + POINTS]
                        dst[r, c, :, lanes] = moved.astype(BF16)

    copies[4].wait()

    def store(rb, cb, down):
        inner = inner_ref[rb, cb].astype(F32)
        down = jnp.concatenate([down[:GROUP_POINTS], inner, down[GROUP_POINTS:]], axis=0)
        if rb == 3:
            down = pltpu.roll(down, WIDE, 0)
        put(d2, (rb + 1) % 4, cb, down * mask, 3)

    level_one(x1, x2, one_ref, down2_ref, store)

    copies[5].wait()
    copies[0].wait()
    for rp in range(2):
        for j in range(2):
            taps = jnp.concatenate(
                [d2[2 * rp + r, 2 * j + c] for r in range(4) for c in range(4)], axis=1
            )
            level = relu(dot(taps, two_ref[...])).astype(BF16)
            put(d3, rp, j, relu(dot(level, down3_ref[...])) * mask2, 1)

    copies[1].wait()
    copies[2].wait()
    total = None
    for i in range(2):
        taps = jnp.concatenate([d3[i + u, c] for u in range(3) for c in range(4)], axis=1)
        level = relu(dot(taps, three_ref[...])).astype(BF16)
        part = dot(level, down4_ref[i])
        total = part if total is None else total + part
    put(d4, 0, 0, relu(total) * mask4, 0)

    copies[3].wait()
    first, count = HALO * WIDE, NWIN * WIDE
    taps = jnp.concatenate(
        [d4[u, v, first:first + count] for u in range(3) for v in range(3)], axis=1
    )
    flat[...] = relu(dot(taps, four_ref[...]))
    for w in range(NWIN):
        start = w * WIDE + HALO
        out_ref[w] = flat[start:start + SPOTS].astype(BF16)


def encoder(inner, edges, spread, one, down2, two, down3, three, down4, four):
    vmem = pl.BlockSpec(memory_space=pltpu.VMEM)
    hbm = pl.BlockSpec(memory_space=pl.ANY)
    rim = 2 * GROUP_POINTS
    return pl.pallas_call(
        encoder_kernel,
        in_specs=[hbm] + [vmem] * 9 + [hbm] * 5,
        out_specs=vmem,
        out_shape=jax.ShapeDtypeStruct((NWIN, SPOTS, four.shape[-1]), BF16),
        scratch_shapes=[
            pltpu.VMEM(inner.shape, BF16),
            pltpu.VMEM((2 * GROUP + 1, 160, 128), BF16),
            pltpu.VMEM((2 * GROUP + 1, 160, 128), BF16),
            pltpu.VMEM((PHASES + 2, rim, 128), BF16),
            pltpu.VMEM((PHASES + 2, rim, 128), BF16),
            pltpu.VMEM((6, 6, POINTS, 128), BF16),
            pltpu.VMEM((4, 4, POINTS, 256), BF16),
            pltpu.VMEM((3, 3, POINTS, 512), BF16),
            pltpu.VMEM((NWIN * WIDE, 512), F32),
            pltpu.VMEM((2, 4, POINTS + 2 * MARGIN, 128), F32),
            pltpu.VMEM(two.shape, BF16),
            pltpu.VMEM(down3.shape, BF16),
            pltpu.VMEM(three.shape, BF16),
            pltpu.VMEM(down4.shape, BF16),
            pltpu.VMEM(four.shape, BF16),
            pltpu.SemaphoreType.DMA((6,)),
        ],
        compiler_params=pltpu.CompilerParams(vmem_limit_bytes=44 * MIB),
        name="encoder",
    )(inner, *edges, spread, one, down2, two, down3, three, down4, four)


def level_one_weights(kernel):
    kernel = jnp.pad(kernel, ((0, 0), (0, 0), (0, 16 - BANDS), (0, 0)))
    columns = []
    for rb in range(2):
        for i in range(2):
            for j in range(2):
                top = 1 + 2 * rb + i
                wide = jnp.pad(kernel, ((top, 5 - top), (j, 1 - j), (0, 0), (0, 0)))
                columns.append(wide.transpose(1, 0, 2, 3).reshape(4 * 8 * 16, -1))
    return jnp.concatenate(columns, axis=1)


def block_weights(kernel, rows, cols):
    none = ((0, 0), (0, 0))
    parts = [
        jnp.pad(kernel, ((i, rows - 1 - i), (j, cols - 1 - j)) + none)
        for j in range(cols)
        for i in range(rows)
    ]
    return jnp.concatenate(parts, axis=3).reshape(-1, rows * cols * kernel.shape[3])


def body(
    granule_blocks, row_weights, column_bank, destination, window_index, bank_index,
    kernel_one, reduce_two, kernel_two, reduce_three, kernel_three, reduce_four, kernel_four,
):
    axes = ("tx", "ty")
    tiles = lax.axis_size("tx") * lax.axis_size("ty")
    slots = resample(
        granule_blocks, row_weights, column_bank, destination, window_index, bank_index, tiles
    )
    received = lax.all_to_all(slots, axes, split_axis=0, concat_axis=0, tiled=True)
    one = level_one_weights(kernel_one)
    two = block_weights(kernel_two, 2, 2)
    three = block_weights(kernel_three, 1, 2)
    down3 = reduce_three.transpose(1, 0, 2, 3).reshape(512, 256)
    received, one, two, three, down3 = lax.optimization_barrier((received, one, two, three, down3))
    gridded, lines, left, right = grid(received)
    from_left, from_right = exchange_columns(left, right)
    main, lower, top, bottom = turn(lines)
    above, below = exchange_rows(top, bottom, from_left, from_right)
    spread = jnp.asarray(spread_matrix(), BF16)
    down2 = reduce_two.reshape(256, 128)
    inner = interior(main, lower, from_left, from_right, spread, one, down2)
    flat = encoder(
        inner, (top, bottom, from_left, from_right, above, below), spread, one, down2,
        two, down3, three,
        reduce_four.reshape(2, 512, 512),
        kernel_four.reshape(9 * 512, 512),
    )
    return gridded, flat.transpose(2, 0, 1)


def solution(mesh):
    both = P(("tx", "ty"))
    in_specs = (both, both, P(), both, both, both) + (P(),) * 7
    out_specs = (P(None, "ty", "tx"), P(None, "ty", "tx"))
    return jax.shard_map(body, mesh=mesh, in_specs=in_specs, out_specs=out_specs, check_vma=False)
```

```python
import functools

import jax
import jax.numpy as jnp
import numpy as np
from jax import lax
from jax.experimental import pallas as pl
from jax.experimental.pallas import tpu as pltpu
from jax.sharding import PartitionSpec as P

BF16 = jnp.bfloat16
F32 = jnp.float32
BANDS = 13
SRC_ROWS = 16
WIN_ROWS = 8
CAP = 2
NWIN = 32
TILE_COLS = 128
LINES = BANDS * WIN_ROWS
PACKED = CAP * LINES + WIN_ROWS
STEP_BLOCKS = 16
PIECES = 4
PHASES = 8
SPOTS = TILE_COLS // PHASES
HALO = 2
WIDE = SPOTS + 2 * HALO
TALL = NWIN + 2 * HALO
POINTS = WIDE * TALL
GROUP = 4
GROUP_POINTS = GROUP * WIDE
MARGIN = 24
PART = 240
LAST_PART = 256
MIB = 1024 * 1024


def dot(a, b):
    return jnp.dot(a, b, preferred_element_type=F32)


def dot_nt(a, b):
    return lax.dot_general(a, b, (((1,), (1,)), ((), ())), preferred_element_type=F32)


def resample_kernel(
    dest_ref, win_ref, choice_ref, weight_ref, raw_hbm, bank_ref, out_ref,
    raw_ref, rows_ref, held_ref, slot_win_ref, sems,
):
    tiles, blocks = held_ref.shape[0], dest_ref.shape[0]
    deep = BANDS * SRC_ROWS

    def fetch(group):
        part = pl.ds(group * STEP_BLOCKS, STEP_BLOCKS)
        return pltpu.make_async_copy(raw_hbm.at[part], raw_ref.at[part], sems.at[group])

    for group in range(blocks // STEP_BLOCKS):
        fetch(group).start()

    def clear(i, carry):
        held_ref[i] = 0
        for k in range(CAP):
            slot_win_ref[i * CAP + k] = -1
        return carry

    lax.fori_loop(0, tiles, clear, 0, unroll=8)

    turned = jnp.transpose(weight_ref[...].astype(F32)).astype(BF16)
    depth = lax.broadcasted_iota(jnp.int32, (WIN_ROWS * SRC_ROWS, 256), 0)
    lane = lax.broadcasted_iota(jnp.int32, (WIN_ROWS * SRC_ROWS, 256), 1)
    offset = depth - (lane & (SRC_ROWS - 1))
    for r in range(WIN_ROWS):
        wide = dot(turned, (offset == r * SRC_ROWS).astype(F32).astype(BF16))
        for h in range(2):
            rows_ref[h, pl.ds(r, blocks, stride=WIN_ROWS), :] = wide[:, h * 128:(h + 1) * 128]

    line = lax.broadcasted_iota(jnp.int32, (LINES, 256), 0)
    lane = lax.broadcasted_iota(jnp.int32, (LINES, 256), 1)
    own = (line >> 3) == (lane >> 4)
    spot = lax.broadcasted_iota(jnp.int32, (WIN_ROWS, TILE_COLS), 1)

    def work(group, carry):
        fetch(group).wait()
        rowed = []
        for j in range(STEP_BLOCKS):
            n = group * STEP_BLOCKS + j
            row = pl.multiple_of(n * WIN_ROWS, WIN_ROWS)
            rows = jnp.concatenate(
                [rows_ref[h, pl.ds(row, WIN_ROWS), :] for h in range(2)], axis=1
            )
            weights = jnp.where(own, jnp.concatenate([rows] * BANDS, axis=0), 0.0)
            rowed.append(dot(weights.astype(BF16)[:, 0:deep], raw_ref[n]).astype(BF16))
        done = []
        for j in range(STEP_BLOCKS):
            n = group * STEP_BLOCKS + j
            done.append(dot(rowed[j], bank_ref[choice_ref[n]]).astype(BF16))
        for j in range(STEP_BLOCKS):
            n = group * STEP_BLOCKS + j
            tile = dest_ref[n]
            rank = held_ref[tile]
            held_ref[tile] = rank + 1
            slot_win_ref[tile * CAP + rank] = win_ref[n]
            place = pl.ds(pl.multiple_of(rank * LINES, WIN_ROWS), LINES)
            out_ref[tile, place, :] = done[j]
        return carry

    lax.fori_loop(0, blocks // STEP_BLOCKS, work, 0)

    def number(i, carry):
        window = jnp.where(spot == 0, slot_win_ref[i * CAP], slot_win_ref[i * CAP + 1])
        out_ref[i, CAP * LINES:] = window.astype(F32).astype(BF16)
        return carry

    lax.fori_loop(0, tiles, number, 0, unroll=4)


def resample(granule_blocks, row_weights, column_bank, destination, window_index, bank_index, tiles):
    blocks = granule_blocks.shape[0]
    deep = BANDS * SRC_ROWS
    vmem = pl.BlockSpec(memory_space=pltpu.VMEM)
    smem = pl.BlockSpec(memory_space=pltpu.SMEM)
    return pl.pallas_call(
        resample_kernel,
        in_specs=[smem, smem, smem, vmem, pl.BlockSpec(memory_space=pl.ANY), vmem],
        out_specs=vmem,
        scratch_shapes=[
            pltpu.VMEM((blocks, deep, TILE_COLS), BF16),
            pltpu.VMEM((2, blocks * WIN_ROWS, 128), F32),
            pltpu.SMEM((tiles,), jnp.int32),
            pltpu.SMEM((tiles * CAP,), jnp.int32),
            pltpu.SemaphoreType.DMA((blocks // STEP_BLOCKS,)),
        ],
        out_shape=jax.ShapeDtypeStruct((tiles, PACKED, TILE_COLS), BF16),
        compiler_params=pltpu.CompilerParams(vmem_limit_bytes=60 * MIB),
        name="resample",
    )(
        destination, window_index, bank_index,
        row_weights.transpose(1, 2, 0).reshape(WIN_ROWS * SRC_ROWS, blocks),
        granule_blocks.reshape(blocks, deep, TILE_COLS),
        column_bank,
    )


def grid_kernel(
    got_hbm, perm_ref, grid_ref, lines_ref, left_ref, right_ref,
    got_ref, sum_ref, number_ref, win_ref, count_ref, sem, sems,
):
    tiles = got_ref.shape[0]
    size = tiles // PIECES
    last = pl.ds(CAP * LINES, WIN_ROWS)
    head = pltpu.make_async_copy(got_hbm.at[:, last], got_ref.at[:, last], sems.at[PIECES])
    head.start()

    def fetch(piece):
        part = pl.ds(piece * size, size), pl.ds(0, CAP * LINES)
        return pltpu.make_async_copy(got_hbm.at[part], got_ref.at[part], sems.at[piece])

    for piece in range(PIECES):
        fetch(piece).start()
    head.wait()
    numbers = got_ref[:, CAP * LINES:, :].astype(F32)
    number_ref[...] = jnp.max(numbers, axis=1).astype(jnp.int32)
    copy = pltpu.make_async_copy(number_ref, win_ref, sem)
    copy.start()

    def clear(w, carry):
        sum_ref[w] = jnp.zeros(sum_ref.shape[1:], F32)
        count_ref[w] = 0
        return carry

    lax.fori_loop(0, NWIN + 1, clear, 0)
    copy.wait()

    def add(t, carry):
        for k in range(CAP):
            w = win_ref[t, k]
            w = jnp.where(w < 0, NWIN, w)
            block = got_ref[t, k * LINES:(k + 1) * LINES].astype(F32)
            sum_ref[w, 0:LINES] = sum_ref[w, 0:LINES] + block
            count_ref[w] = count_ref[w] + 1
        return carry

    def add_piece(piece, carry):
        fetch(piece).wait()
        return lax.fori_loop(piece * size, (piece + 1) * size, add, carry)

    lax.fori_loop(0, PIECES, add_piece, 0)

    def finish(group, carry):
        first = group * GROUP
        means = []
        for k in range(GROUP):
            w = first + k
            divisor = jnp.maximum(count_ref[w], 1).astype(F32)
            mean = (sum_ref[w, 0:LINES] / divisor).astype(BF16).astype(F32)
            sum_ref[w, 0:LINES] = mean
            means.append(mean)
        row = pl.multiple_of(first * WIN_ROWS, GROUP * WIN_ROWS)
        for b in range(BANDS):
            part = jnp.concatenate([m[b * WIN_ROWS:(b + 1) * WIN_ROWS] for m in means], axis=0)
            grid_ref[b, pl.ds(row, GROUP * WIN_ROWS), :] = part.astype(BF16)
        for pair in range(GROUP // 2):
            lines = jnp.concatenate(
                [
                    sum_ref[first + pair * 2 + k, pl.ds(r, 16, stride=WIN_ROWS), :]
                    for k in range(2)
                    for r in range(WIN_ROWS)
                ],
                axis=0,
            ).astype(BF16)
            row = pl.multiple_of((first + pair * 2) * 128, 256)
            lines_ref[pl.ds(row, 256), :] = lines
            both = dot_nt(perm_ref[...], lines).astype(BF16)
            for k in range(2):
                w = first + pair * 2 + k
                turned = both[:, k * 128:(k + 1) * 128]
                left_ref[pl.ds(pl.multiple_of(w * 16, 16), 16), :] = turned[0:16]
                right_ref[pl.ds(pl.multiple_of(w * 16, 16), 16), :] = turned[16:32]
        return carry

    lax.fori_loop(0, NWIN // GROUP, finish, 0)


def grid(received):
    tiles = received.shape[0]
    perm = np.zeros((32, TILE_COLS), np.float32)
    for p in range(PHASES):
        for a in range(HALO):
            perm[p * HALO + a, a * PHASES + p] = 1.0
            perm[16 + p * HALO + a, (SPOTS - HALO + a) * PHASES + p] = 1.0
    vmem = pl.BlockSpec(memory_space=pltpu.VMEM)
    return pl.pallas_call(
        grid_kernel,
        in_specs=[pl.BlockSpec(memory_space=pl.ANY), vmem],
        out_specs=[vmem] * 4,
        out_shape=[
            jax.ShapeDtypeStruct((BANDS, NWIN * WIN_ROWS, TILE_COLS), BF16),
            jax.ShapeDtypeStruct((NWIN * 128, 128), BF16),
            jax.ShapeDtypeStruct((NWIN * 16, 128), BF16),
            jax.ShapeDtypeStruct((NWIN * 16, 128), BF16),
        ],
        scratch_shapes=[
            pltpu.VMEM(received.shape, BF16),
            pltpu.VMEM((NWIN + 1, 128, TILE_COLS), F32),
            pltpu.VMEM((tiles, TILE_COLS), jnp.int32),
            pltpu.SMEM((tiles, TILE_COLS), jnp.int32),
            pltpu.SMEM((NWIN + 1,), jnp.int32),
            pltpu.SemaphoreType.DMA,
            pltpu.SemaphoreType.DMA((PIECES + 1,)),
        ],
        compiler_params=pltpu.CompilerParams(vmem_limit_bytes=24 * MIB),
        name="grid",
    )(received, jnp.asarray(perm, BF16))


def turn_kernel(lines_ref, perm_ref, main_ref, lower_ref, top_ref, bottom_ref):
    def step(i, carry):
        for k in range(2):
            w = i * 2 + k
            start = pl.multiple_of(w * 128, 128)
            below = pl.multiple_of(jnp.minimum(w * 128 + 64, (NWIN - 1) * 128), 64)
            lines = jnp.concatenate(
                [lines_ref[pl.ds(start, 128), :], lines_ref[pl.ds(below, 128), :]], axis=0
            )
            both = dot_nt(perm_ref[...], lines).astype(BF16)
            main_ref[pl.ds(start, 128), :] = both[:, 0:128]
            lower_ref[pl.ds(start, 128), :] = both[:, 128:256]
        return carry

    lax.fori_loop(0, NWIN // 2, step, 0, unroll=2)
    top_ref[...] = main_ref[0:top_ref.shape[0]]
    bottom_ref[...] = main_ref[(NWIN - HALO) * 128:]


def turn(lines):
    perm = np.zeros((TILE_COLS, TILE_COLS), np.float32)
    for p in range(PHASES):
        for a in range(SPOTS):
            perm[p * SPOTS + a, a * PHASES + p] = 1.0
    vmem = pl.BlockSpec(memory_space=pltpu.VMEM)
    return pl.pallas_call(
        turn_kernel,
        in_specs=[vmem] * 2,
        out_specs=[vmem] * 4,
        out_shape=[
            jax.ShapeDtypeStruct((NWIN * 128, 128), BF16),
            jax.ShapeDtypeStruct((NWIN * 128, 128), BF16),
            jax.ShapeDtypeStruct(((HALO + 1) * 128, 128), BF16),
            jax.ShapeDtypeStruct((HALO * 128, 128), BF16),
        ],
        compiler_params=pltpu.CompilerParams(vmem_limit_bytes=16 * MIB),
        cost_estimate=pl.CostEstimate(
            flops=2 * NWIN * 128 ** 3 * 2, bytes_accessed=8 * MIB, transcendentals=0
        ),
        name="turn",
    )(lines, jnp.asarray(perm, BF16))


def exchange_columns(left, right):
    across = lax.axis_size("tx")
    right_ward = [(i, i + 1) for i in range(across - 1)]
    left_ward = [(t, s) for s, t in right_ward]
    return lax.ppermute(right, "tx", right_ward), lax.ppermute(left, "tx", left_ward)


def exchange_rows(top, bottom, from_left, from_right):
    down = lax.axis_size("ty")
    down_ward = [(i, i + 1) for i in range(down - 1)]
    up_ward = [(t, s) for s, t in down_ward]
    m, h = HALO * 128, HALO * 16
    first = jnp.concatenate([top[:m], from_left[:h], from_right[:h]], axis=0)
    last = jnp.concatenate([bottom, from_left[-h:], from_right[-h:]], axis=0)
    return lax.ppermute(last, "ty", down_ward), lax.ppermute(first, "ty", up_ward)


def spread_matrix():
    out = np.zeros((PHASES + 2, GROUP_POINTS, GROUP * 48), np.float32)
    for index in range(PHASES + 2):
        p = (index - 1) % PHASES
        shift = -1 if index == 0 else (1 if index == PHASES + 1 else 0)
        for k in range(GROUP):
            for a in range(WIDE):
                s = a + shift
                row = k * WIDE + a
                if s < 0 or s >= WIDE:
                    continue
                if s < HALO:
                    out[index, row, GROUP * 16 + k * 16 + p * HALO + s] = 1.0
                elif s < HALO + SPOTS:
                    out[index, row, k * 16 + s - HALO] = 1.0
                else:
                    out[index, row, GROUP * 32 + k * 16 + p * HALO + s - HALO - SPOTS] = 1.0
    return out


def relu(x):
    return jnp.maximum(x, 0.0)


def level_one(x1, x2, one_ref, down2_ref, store):
    for cb in range(4):
        for version, x in enumerate((x1, x2)):
            taps = jnp.concatenate([x[2 * cb + k] for k in range(4)], axis=1)
            level = relu(dot(taps, one_ref[...])).astype(BF16)
            for half in range(2):
                down = relu(dot(level[:, half * 256:(half + 1) * 256], down2_ref[...]))
                store(2 * version + half, cb, down)


def lay(spread, first, second):
    return dot(spread, jnp.concatenate([jnp.concatenate(p, axis=0) for p in (first, second)], axis=1))


def interior_kernel(
    main_ref, lower_ref, fl_ref, fr_ref, spread_ref, one_ref, down2_ref, out_ref, side_ref, x1, x2
):
    low = lax.broadcasted_iota(jnp.int32, (16, 128), 1) < 64
    for s, side in enumerate((fl_ref, fr_ref)):
        for w in range(NWIN - 1):
            after = side[(w + 1) * 16:(w + 2) * 16].astype(F32)
            both = jnp.where(low, after, side[w * 16:(w + 1) * 16].astype(F32))
            side_ref[s, w * 16:(w + 1) * 16] = pltpu.roll(both, 64, 1).astype(BF16)

    def place(g, carry):
        row = pl.multiple_of(g * GROUP_POINTS, GROUP_POINTS)
        w = g * GROUP + GROUP - HALO
        edge = [pl.ds(pl.multiple_of((w + k) * 16, 16), 16) for k in range(GROUP)]
        for index in range(PHASES + 2):
            p = (index - 1) % PHASES
            own = [
                pl.ds(pl.multiple_of((w + k) * 128 + p * 16, 16), 16) for k in range(GROUP)
            ]
            first = [main_ref[o, :] for o in own]
            first += [ref[e, :] for ref in (fl_ref, fr_ref) for e in edge]
            second = [lower_ref[o, :] for o in own]
            second += [side_ref[s, e, :] for s in range(2) for e in edge]
            laid = lay(spread_ref[index], first, second).astype(BF16)
            x1[index, pl.ds(row, GROUP_POINTS), :] = laid[:, 0:128]
            x2[index, pl.ds(row, GROUP_POINTS), :] = laid[:, 128:256]
        return carry

    lax.fori_loop(0, TALL // GROUP - 2, place, 0)

    def store(rb, cb, down):
        out_ref[rb, cb] = down.astype(BF16)

    level_one(x1, x2, one_ref, down2_ref, store)


def interior(main, lower, from_left, from_right, spread, one, down2):
    vmem = pl.BlockSpec(memory_space=pltpu.VMEM)
    points = POINTS - 2 * GROUP_POINTS
    return pl.pallas_call(
        interior_kernel,
        in_specs=[vmem] * 7,
        out_specs=vmem,
        out_shape=jax.ShapeDtypeStruct((4, 4, points, 128), BF16),
        scratch_shapes=[
            pltpu.VMEM((2, NWIN * 16, 128), BF16),
            pltpu.VMEM((PHASES + 2, points, 128), BF16),
            pltpu.VMEM((PHASES + 2, points, 128), BF16),
        ],
        compiler_params=pltpu.CompilerParams(vmem_limit_bytes=32 * MIB),
        cost_estimate=pl.CostEstimate(
            flops=2 * points * 8 * (512 * 512 + 512 * 256),
            bytes_accessed=16 * MIB,
            transcendentals=0,
        ),
        name="interior",
    )(main, lower, from_left, from_right, spread, one, down2)


def encoder_kernel(
    inner_hbm, top_ref, bottom_ref, fl_ref, fr_ref, above_ref, below_ref, spread_ref, one_ref,
    down2_ref, two_hbm, down3_hbm, three_hbm, down4_hbm, four_hbm,
    out_ref,
    inner_ref, ext1, ext2, x1, x2, d2, d3, d4, stage,
    two_ref, down3_ref, three_ref, down4_ref, four_ref, sems,
):
    copies = [
        pltpu.make_async_copy(src, dst, sems.at[i])
        for i, (src, dst) in enumerate(
            (
                (down3_hbm, down3_ref),
                (three_hbm, three_ref),
                (down4_hbm, down4_ref),
                (four_hbm, four_ref),
                (inner_hbm, inner_ref),
                (two_hbm, two_ref),
            )
        )
    ]
    for i in (4, 5, 0, 1, 2, 3):
        copies[i].start()
    for side in range(2):
        for p in range(4):
            stage[side, p, 0:MARGIN] = jnp.zeros((MARGIN, 128), F32)
            stage[side, p, MARGIN + POINTS:] = jnp.zeros((MARGIN, 128), F32)

    m = HALO * 128
    for h in range(HALO):
        for source, i in ((above_ref, h), (below_ref, 3 * HALO + 1 + h)):
            ext1[i, 0:128] = source[h * 128:(h + 1) * 128]
            ext1[i, 128:144] = source[m + h * 16:m + h * 16 + 16]
            ext1[i, 144:160] = source[m + (HALO + h) * 16:m + (HALO + h) * 16 + 16]
    near = [(HALO + k, top_ref, k, k) for k in range(HALO + 1)]
    near += [(2 * HALO + 1 + k, bottom_ref, k, NWIN - HALO + k) for k in range(HALO)]
    for i, source, k, w in near:
        ext1[i, 0:128] = source[k * 128:(k + 1) * 128]
        ext1[i, 128:144] = fl_ref[w * 16:(w + 1) * 16]
        ext1[i, 144:160] = fr_ref[w * 16:(w + 1) * 16]

    low = lax.broadcasted_iota(jnp.int32, (160, 128), 1) < 64
    edges = (0, GROUP + 1)
    for base in edges:
        for k in range(GROUP):
            i = base + k
            after = min(i + 1, ext1.shape[0] - 1)
            both = jnp.where(low, ext1[after].astype(F32), ext1[i].astype(F32))
            ext2[i] = pltpu.roll(both, 64, 1).astype(BF16)

    for e, base in enumerate(edges):
        for index in range(PHASES + 2):
            p = (index - 1) % PHASES
            sides = []
            for ext in (ext1, ext2):
                pieces = [ext[base + k, p * 16:(p + 1) * 16] for k in range(GROUP)]
                pieces += [ext[base + k, 128:144] for k in range(GROUP)]
                pieces += [ext[base + k, 144:160] for k in range(GROUP)]
                sides.append(pieces)
            laid = lay(spread_ref[index], *sides).astype(BF16)
            x1[index, e * GROUP_POINTS:(e + 1) * GROUP_POINTS] = laid[:, 0:128]
            x2[index, e * GROUP_POINTS:(e + 1) * GROUP_POINTS] = laid[:, 128:256]

    across, below = lax.axis_size("tx"), lax.axis_size("ty")
    x, y = lax.axis_index("tx"), lax.axis_index("ty")
    least_w, most_w = jnp.where(y > 0, 0, HALO), jnp.where(y < below - 1, TALL, HALO + NWIN)
    least_a, most_a = jnp.where(x > 0, 0, HALO), jnp.where(x < across - 1, WIDE, HALO + SPOTS)
    point = lax.broadcasted_iota(jnp.int32, (POINTS, 128), 0)
    w = (point * (65536 // WIDE + 1)) >> 16
    a = point - w * WIDE
    inside = (w >= least_w) & (w < most_w) & (a >= least_a) & (a < most_a)
    mask = inside.astype(F32)
    mask2 = jnp.concatenate([mask, mask], axis=1)
    mask4 = jnp.concatenate([mask2, mask2], axis=1)

    def put(dst, i, j, value, last):
        rows = [(i + 1, 0)]
        if i == last:
            rows.append((0, WIDE))
        if i == 0:
            rows.append((last + 2, -WIDE))
        cols = [(j + 1, 0)]
        if j == last:
            cols.append((0, 1))
        if j == 0:
            cols.append((last + 2, -1))
        dst[i + 1, j + 1] = value.astype(BF16)
        side = (i + j) % 2
        for p in range(value.shape[1] // 128):
            lanes = slice(p * 128, (p + 1) * 128)
            stage[side, p, MARGIN:MARGIN + POINTS] = value[:, lanes]
            for r, row_shift in rows:
                for c, col_shift in cols:
                    shift = row_shift + col_shift
                    if shift:
                        moved = stage[side, p, MARGIN - shift:MARGIN - shift + POINTS]
                        dst[r, c, :, lanes] = moved.astype(BF16)

    copies[4].wait()

    def store(rb, cb, down):
        inner = inner_ref[rb, cb].astype(F32)
        down = jnp.concatenate([down[:GROUP_POINTS], inner, down[GROUP_POINTS:]], axis=0)
        if rb == 3:
            down = pltpu.roll(down, WIDE, 0)
        put(d2, (rb + 1) % 4, cb, down * mask, 3)

    level_one(x1, x2, one_ref, down2_ref, store)

    copies[5].wait()
    copies[0].wait()
    parts = [slice(m, m + PART) for m in range(0, POINTS, PART)]
    for rp in range(2):
        for j in range(2):
            totals = []
            for m in parts:
                total = None
                for v2 in range(2):
                    taps = jnp.concatenate(
                        [d2[2 * rp + r, 2 * j + v2 + v, m] for r in range(4) for v in range(3)],
                        axis=1,
                    )
                    level = relu(dot(taps, two_ref[...])).astype(BF16)
                    part = dot(level, down3_ref[v2])
                    total = part if total is None else total + part
                totals.append(relu(total))
            put(d3, rp, j, jnp.concatenate(totals, axis=0) * mask2, 1)

    copies[1].wait()
    copies[2].wait()
    totals = []
    for m in parts:
        total = None
        for i in range(2):
            for j in range(2):
                taps = jnp.concatenate(
                    [d3[i + u, j + v, m] for u in range(3) for v in range(3)], axis=1
                )
                level = relu(dot(taps, three_ref[...])).astype(BF16)
                part = dot(level, down4_ref[i * 2 + j])
                total = part if total is None else total + part
        totals.append(relu(total))
    value = jnp.concatenate(totals, axis=0) * mask4

    for p in range(4):
        lanes = slice(p * 128, (p + 1) * 128)
        stage[0, p, MARGIN:MARGIN + POINTS] = value[:, lanes]
        for w in range(NWIN):
            for u in range(3):
                for v in range(3):
                    start = MARGIN + (w + HALO + u - 1) * WIDE + HALO + v - 1
                    tap = stage[0, p, start:start + SPOTS]
                    d4[u, v, w * SPOTS:(w + 1) * SPOTS, lanes] = tap.astype(BF16)

    copies[3].wait()
    for m in range(0, NWIN * SPOTS, LAST_PART):
        part = slice(m, m + LAST_PART)
        taps = jnp.concatenate([d4[u, v, part] for u in range(3) for v in range(3)], axis=1)
        out_ref[part] = relu(dot(taps, four_ref[...])).astype(BF16)


def encoder(inner, edges, spread, one, down2, two, down3, three, down4, four):
    vmem = pl.BlockSpec(memory_space=pltpu.VMEM)
    hbm = pl.BlockSpec(memory_space=pl.ANY)
    rim = 2 * GROUP_POINTS
    return pl.pallas_call(
        encoder_kernel,
        in_specs=[hbm] + [vmem] * 9 + [hbm] * 5,
        out_specs=vmem,
        out_shape=jax.ShapeDtypeStruct((NWIN * SPOTS, four.shape[-1]), BF16),
        scratch_shapes=[
            pltpu.VMEM(inner.shape, BF16),
            pltpu.VMEM((2 * GROUP + 1, 160, 128), BF16),
            pltpu.VMEM((2 * GROUP + 1, 160, 128), BF16),
            pltpu.VMEM((PHASES + 2, rim, 128), BF16),
            pltpu.VMEM((PHASES + 2, rim, 128), BF16),
            pltpu.VMEM((6, 6, POINTS, 128), BF16),
            pltpu.VMEM((4, 4, POINTS, 256), BF16),
            pltpu.VMEM((3, 3, NWIN * SPOTS, 512), BF16),
            pltpu.VMEM((2, 4, POINTS + 2 * MARGIN, 128), F32),
            pltpu.VMEM(two.shape, BF16),
            pltpu.VMEM(down3.shape, BF16),
            pltpu.VMEM(three.shape, BF16),
            pltpu.VMEM(down4.shape, BF16),
            pltpu.VMEM(four.shape, BF16),
            pltpu.SemaphoreType.DMA((6,)),
        ],
        compiler_params=pltpu.CompilerParams(vmem_limit_bytes=44 * MIB),
        name="encoder",
    )(inner, *edges, spread, one, down2, two, down3, three, down4, four)


def level_one_weights(kernel):
    kernel = jnp.pad(kernel, ((0, 0), (0, 0), (0, 16 - BANDS), (0, 0)))
    columns = []
    for rb in range(2):
        for i in range(2):
            for j in range(2):
                top = 1 + 2 * rb + i
                wide = jnp.pad(kernel, ((top, 5 - top), (j, 1 - j), (0, 0), (0, 0)))
                columns.append(wide.transpose(1, 0, 2, 3).reshape(4 * 8 * 16, -1))
    return jnp.concatenate(columns, axis=1)


def level_two_weights(kernel):
    none = ((0, 0),) * 3
    pair = [jnp.pad(kernel, ((i, 1 - i),) + none) for i in range(2)]
    return jnp.concatenate(pair, axis=3).reshape(12 * kernel.shape[2], -1)


def body(
    granule_blocks, row_weights, column_bank, destination, window_index, bank_index,
    kernel_one, reduce_two, kernel_two, reduce_three, kernel_three, reduce_four, kernel_four,
):
    axes = ("tx", "ty")
    tiles = lax.axis_size("tx") * lax.axis_size("ty")
    slots = resample(
        granule_blocks, row_weights, column_bank, destination, window_index, bank_index, tiles
    )
    received = lax.all_to_all(slots, axes, split_axis=0, concat_axis=0, tiled=True)
    one = level_one_weights(kernel_one)
    two = level_two_weights(kernel_two)
    down3 = reduce_three.transpose(1, 0, 2, 3).reshape(2, 256, 256)
    received, one, two, down3 = lax.optimization_barrier((received, one, two, down3))
    gridded, lines, left, right = grid(received)
    from_left, from_right = exchange_columns(left, right)
    main, lower, top, bottom = turn(lines)
    above, below = exchange_rows(top, bottom, from_left, from_right)
    spread = jnp.asarray(spread_matrix(), BF16)
    down2 = reduce_two.reshape(256, 128)
    inner = interior(main, lower, from_left, from_right, spread, one, down2)
    flat = encoder(
        inner, (top, bottom, from_left, from_right, above, below), spread, one, down2,
        two, down3,
        kernel_three.reshape(9 * 256, 256),
        reduce_four.reshape(4, 256, 512),
        kernel_four.reshape(9 * 512, 512),
    )
    return gridded, flat.reshape(NWIN, SPOTS, -1).transpose(2, 0, 1)


def solution(mesh):
    both = P(("tx", "ty"))
    in_specs = (both, both, P(), both, both, both) + (P(),) * 7
    out_specs = (P(None, "ty", "tx"), P(None, "ty", "tx"))
    return jax.shard_map(body, mesh=mesh, in_specs=in_specs, out_specs=out_specs, check_vma=False)
```

```python
import functools

import jax
import jax.numpy as jnp
import numpy as np
from jax import lax
from jax.experimental import pallas as pl
from jax.experimental.pallas import tpu as pltpu
from jax.sharding import PartitionSpec as P

BF16 = jnp.bfloat16
F32 = jnp.float32
BANDS = 13
SRC_ROWS = 16
WIN_ROWS = 8
CAP = 2
NWIN = 32
TILE_COLS = 128
LINES = BANDS * WIN_ROWS
PACKED = CAP * LINES + WIN_ROWS
STEP_BLOCKS = 16
PIECES = 4
PHASES = 8
SPOTS = TILE_COLS // PHASES
HALO = 2
WIDE = SPOTS + 2 * HALO
TALL = NWIN + 2 * HALO
POINTS = WIDE * TALL
GROUP = 4
GROUP_POINTS = GROUP * WIDE
MARGIN = 24
MIB = 1024 * 1024


def dot(a, b):
    return jnp.dot(a, b, preferred_element_type=F32)


def dot_nt(a, b):
    return lax.dot_general(a, b, (((1,), (1,)), ((), ())), preferred_element_type=F32)


def resample_kernel(
    dest_ref, win_ref, choice_ref, weight_ref, raw_hbm, bank_ref, out_ref,
    raw_ref, rows_ref, held_ref, slot_win_ref, sems,
):
    tiles, blocks = held_ref.shape[0], dest_ref.shape[0]
    deep = BANDS * SRC_ROWS

    def fetch(group):
        part = pl.ds(group * STEP_BLOCKS, STEP_BLOCKS)
        return pltpu.make_async_copy(raw_hbm.at[part], raw_ref.at[part], sems.at[group])

    for group in range(blocks // STEP_BLOCKS):
        fetch(group).start()

    def clear(i, carry):
        held_ref[i] = 0
        for k in range(CAP):
            slot_win_ref[i * CAP + k] = -1
        return carry

    lax.fori_loop(0, tiles, clear, 0, unroll=8)

    turned = jnp.transpose(weight_ref[...].astype(F32)).astype(BF16)
    depth = lax.broadcasted_iota(jnp.int32, (WIN_ROWS * SRC_ROWS, 256), 0)
    lane = lax.broadcasted_iota(jnp.int32, (WIN_ROWS * SRC_ROWS, 256), 1)
    offset = depth - (lane & (SRC_ROWS - 1))
    for r in range(WIN_ROWS):
        wide = dot(turned, (offset == r * SRC_ROWS).astype(F32).astype(BF16))
        for h in range(2):
            rows_ref[h, pl.ds(r, blocks, stride=WIN_ROWS), :] = wide[:, h * 128:(h + 1) * 128]

    line = lax.broadcasted_iota(jnp.int32, (LINES, 256), 0)
    lane = lax.broadcasted_iota(jnp.int32, (LINES, 256), 1)
    own = (line >> 3) == (lane >> 4)
    spot = lax.broadcasted_iota(jnp.int32, (WIN_ROWS, TILE_COLS), 1)

    def work(group, carry):
        fetch(group).wait()
        rowed = []
        for j in range(STEP_BLOCKS):
            n = group * STEP_BLOCKS + j
            row = pl.multiple_of(n * WIN_ROWS, WIN_ROWS)
            rows = jnp.concatenate(
                [rows_ref[h, pl.ds(row, WIN_ROWS), :] for h in range(2)], axis=1
            )
            weights = jnp.where(own, jnp.concatenate([rows] * BANDS, axis=0), 0.0)
            rowed.append(dot(weights.astype(BF16)[:, 0:deep], raw_ref[n]).astype(BF16))
        done = []
        for j in range(STEP_BLOCKS):
            n = group * STEP_BLOCKS + j
            done.append(dot(rowed[j], bank_ref[choice_ref[n]]).astype(BF16))
        for j in range(STEP_BLOCKS):
            n = group * STEP_BLOCKS + j
            tile = dest_ref[n]
            rank = held_ref[tile]
            held_ref[tile] = rank + 1
            slot_win_ref[tile * CAP + rank] = win_ref[n]
            place = pl.ds(pl.multiple_of(rank * LINES, WIN_ROWS), LINES)
            out_ref[tile, place, :] = done[j]
        return carry

    lax.fori_loop(0, blocks // STEP_BLOCKS, work, 0)

    def number(i, carry):
        window = jnp.where(spot == 0, slot_win_ref[i * CAP], slot_win_ref[i * CAP + 1])
        out_ref[i, CAP * LINES:] = window.astype(F32).astype(BF16)
        return carry

    lax.fori_loop(0, tiles, number, 0, unroll=4)


def resample(granule_blocks, row_weights, column_bank, destination, window_index, bank_index, tiles):
    blocks = granule_blocks.shape[0]
    deep = BANDS * SRC_ROWS
    vmem = pl.BlockSpec(memory_space=pltpu.VMEM)
    smem = pl.BlockSpec(memory_space=pltpu.SMEM)
    return pl.pallas_call(
        resample_kernel,
        in_specs=[smem, smem, smem, vmem, pl.BlockSpec(memory_space=pl.ANY), vmem],
        out_specs=vmem,
        scratch_shapes=[
            pltpu.VMEM((blocks, deep, TILE_COLS), BF16),
            pltpu.VMEM((2, blocks * WIN_ROWS, 128), F32),
            pltpu.SMEM((tiles,), jnp.int32),
            pltpu.SMEM((tiles * CAP,), jnp.int32),
            pltpu.SemaphoreType.DMA((blocks // STEP_BLOCKS,)),
        ],
        out_shape=jax.ShapeDtypeStruct((tiles, PACKED, TILE_COLS), BF16),
        compiler_params=pltpu.CompilerParams(vmem_limit_bytes=60 * MIB),
        name="resample",
    )(
        destination, window_index, bank_index,
        row_weights.transpose(1, 2, 0).reshape(WIN_ROWS * SRC_ROWS, blocks),
        granule_blocks.reshape(blocks, deep, TILE_COLS),
        column_bank,
    )


def grid_kernel(
    got_hbm, perm_ref, grid_ref, lines_ref, left_ref, right_ref,
    got_ref, sum_ref, number_ref, win_ref, count_ref, sem, sems,
):
    tiles = got_ref.shape[0]
    size = tiles // PIECES
    last = pl.ds(CAP * LINES, WIN_ROWS)
    head = pltpu.make_async_copy(got_hbm.at[:, last], got_ref.at[:, last], sems.at[PIECES])
    head.start()

    def fetch(piece):
        part = pl.ds(piece * size, size), pl.ds(0, CAP * LINES)
        return pltpu.make_async_copy(got_hbm.at[part], got_ref.at[part], sems.at[piece])

    for piece in range(PIECES):
        fetch(piece).start()
    head.wait()
    numbers = got_ref[:, CAP * LINES:, :].astype(F32)
    number_ref[...] = jnp.max(numbers, axis=1).astype(jnp.int32)
    copy = pltpu.make_async_copy(number_ref, win_ref, sem)
    copy.start()

    def clear(w, carry):
        sum_ref[w] = jnp.zeros(sum_ref.shape[1:], F32)
        count_ref[w] = 0
        return carry

    lax.fori_loop(0, NWIN + 1, clear, 0)
    copy.wait()

    def add(t, carry):
        for k in range(CAP):
            w = win_ref[t, k]
            w = jnp.where(w < 0, NWIN, w)
            block = got_ref[t, k * LINES:(k + 1) * LINES].astype(F32)
            sum_ref[w, 0:LINES] = sum_ref[w, 0:LINES] + block
            count_ref[w] = count_ref[w] + 1
        return carry

    def add_piece(piece, carry):
        fetch(piece).wait()
        return lax.fori_loop(piece * size, (piece + 1) * size, add, carry)

    lax.fori_loop(0, PIECES, add_piece, 0)

    def finish(group, carry):
        first = group * GROUP
        means = []
        for k in range(GROUP):
            w = first + k
            divisor = jnp.maximum(count_ref[w], 1).astype(F32)
            mean = (sum_ref[w, 0:LINES] / divisor).astype(BF16).astype(F32)
            sum_ref[w, 0:LINES] = mean
            means.append(mean)
        row = pl.multiple_of(first * WIN_ROWS, GROUP * WIN_ROWS)
        for b in range(BANDS):
            part = jnp.concatenate([m[b * WIN_ROWS:(b + 1) * WIN_ROWS] for m in means], axis=0)
            grid_ref[b, pl.ds(row, GROUP * WIN_ROWS), :] = part.astype(BF16)
        for pair in range(GROUP // 2):
            lines = jnp.concatenate(
                [
                    sum_ref[first + pair * 2 + k, pl.ds(r, 16, stride=WIN_ROWS), :]
                    for k in range(2)
                    for r in range(WIN_ROWS)
                ],
                axis=0,
            ).astype(BF16)
            row = pl.multiple_of((first + pair * 2) * 128, 256)
            lines_ref[pl.ds(row, 256), :] = lines
            both = dot_nt(perm_ref[...], lines).astype(BF16)
            for k in range(2):
                w = first + pair * 2 + k
                turned = both[:, k * 128:(k + 1) * 128]
                left_ref[pl.ds(pl.multiple_of(w * 16, 16), 16), :] = turned[0:16]
                right_ref[pl.ds(pl.multiple_of(w * 16, 16), 16), :] = turned[16:32]
        return carry

    lax.fori_loop(0, NWIN // GROUP, finish, 0)


def grid(received):
    tiles = received.shape[0]
    perm = np.zeros((32, TILE_COLS), np.float32)
    for p in range(PHASES):
        for a in range(HALO):
            perm[p * HALO + a, a * PHASES + p] = 1.0
            perm[16 + p * HALO + a, (SPOTS - HALO + a) * PHASES + p] = 1.0
    vmem = pl.BlockSpec(memory_space=pltpu.VMEM)
    return pl.pallas_call(
        grid_kernel,
        in_specs=[pl.BlockSpec(memory_space=pl.ANY), vmem],
        out_specs=[vmem] * 4,
        out_shape=[
            jax.ShapeDtypeStruct((BANDS, NWIN * WIN_ROWS, TILE_COLS), BF16),
            jax.ShapeDtypeStruct((NWIN * 128, 128), BF16),
            jax.ShapeDtypeStruct((NWIN * 16, 128), BF16),
            jax.ShapeDtypeStruct((NWIN * 16, 128), BF16),
        ],
        scratch_shapes=[
            pltpu.VMEM(received.shape, BF16),
            pltpu.VMEM((NWIN + 1, 128, TILE_COLS), F32),
            pltpu.VMEM((tiles, TILE_COLS), jnp.int32),
            pltpu.SMEM((tiles, TILE_COLS), jnp.int32),
            pltpu.SMEM((NWIN + 1,), jnp.int32),
            pltpu.SemaphoreType.DMA,
            pltpu.SemaphoreType.DMA((PIECES + 1,)),
        ],
        compiler_params=pltpu.CompilerParams(vmem_limit_bytes=24 * MIB),
        name="grid",
    )(received, jnp.asarray(perm, BF16))


def turn_kernel(lines_ref, perm_ref, main_ref, lower_ref, top_ref, bottom_ref):
    def step(i, carry):
        for k in range(2):
            w = i * 2 + k
            start = pl.multiple_of(w * 128, 128)
            below = pl.multiple_of(jnp.minimum(w * 128 + 64, (NWIN - 1) * 128), 64)
            lines = jnp.concatenate(
                [lines_ref[pl.ds(start, 128), :], lines_ref[pl.ds(below, 128), :]], axis=0
            )
            both = dot_nt(perm_ref[...], lines).astype(BF16)
            main_ref[pl.ds(start, 128), :] = both[:, 0:128]
            lower_ref[pl.ds(start, 128), :] = both[:, 128:256]
        return carry

    lax.fori_loop(0, NWIN // 2, step, 0, unroll=2)
    top_ref[...] = main_ref[0:top_ref.shape[0]]
    bottom_ref[...] = main_ref[(NWIN - HALO) * 128:]


def turn(lines):
    perm = np.zeros((TILE_COLS, TILE_COLS), np.float32)
    for p in range(PHASES):
        for a in range(SPOTS):
            perm[p * SPOTS + a, a * PHASES + p] = 1.0
    vmem = pl.BlockSpec(memory_space=pltpu.VMEM)
    return pl.pallas_call(
        turn_kernel,
        in_specs=[vmem] * 2,
        out_specs=[vmem] * 4,
        out_shape=[
            jax.ShapeDtypeStruct((NWIN * 128, 128), BF16),
            jax.ShapeDtypeStruct((NWIN * 128, 128), BF16),
            jax.ShapeDtypeStruct(((HALO + 1) * 128, 128), BF16),
            jax.ShapeDtypeStruct((HALO * 128, 128), BF16),
        ],
        compiler_params=pltpu.CompilerParams(vmem_limit_bytes=16 * MIB),
        cost_estimate=pl.CostEstimate(
            flops=2 * NWIN * 128 ** 3 * 2, bytes_accessed=8 * MIB, transcendentals=0
        ),
        name="turn",
    )(lines, jnp.asarray(perm, BF16))


def exchange_columns(left, right):
    across = lax.axis_size("tx")
    right_ward = [(i, i + 1) for i in range(across - 1)]
    left_ward = [(t, s) for s, t in right_ward]
    return lax.ppermute(right, "tx", right_ward), lax.ppermute(left, "tx", left_ward)


def exchange_rows(top, bottom, from_left, from_right):
    down = lax.axis_size("ty")
    down_ward = [(i, i + 1) for i in range(down - 1)]
    up_ward = [(t, s) for s, t in down_ward]
    m, h = HALO * 128, HALO * 16
    first = jnp.concatenate([top[:m], from_left[:h], from_right[:h]], axis=0)
    last = jnp.concatenate([bottom, from_left[-h:], from_right[-h:]], axis=0)
    return lax.ppermute(last, "ty", down_ward), lax.ppermute(first, "ty", up_ward)


def spread_matrix():
    out = np.zeros((PHASES + 2, GROUP_POINTS, GROUP * 48), np.float32)
    for index in range(PHASES + 2):
        p = (index - 1) % PHASES
        shift = -1 if index == 0 else (1 if index == PHASES + 1 else 0)
        for k in range(GROUP):
            for a in range(WIDE):
                s = a + shift
                row = k * WIDE + a
                if s < 0 or s >= WIDE:
                    continue
                if s < HALO:
                    out[index, row, GROUP * 16 + k * 16 + p * HALO + s] = 1.0
                elif s < HALO + SPOTS:
                    out[index, row, k * 16 + s - HALO] = 1.0
                else:
                    out[index, row, GROUP * 32 + k * 16 + p * HALO + s - HALO - SPOTS] = 1.0
    return out


def relu(x):
    return jnp.maximum(x, 0.0)


def level_one(x1, x2, one_ref, down2_ref, store):
    for cb in range(4):
        for version, x in enumerate((x1, x2)):
            taps = jnp.concatenate([x[2 * cb + k] for k in range(4)], axis=1)
            level = relu(dot(taps, one_ref[...])).astype(BF16)
            for half in range(2):
                down = relu(dot(level[:, half * 256:(half + 1) * 256], down2_ref[...]))
                store(2 * version + half, cb, down)


def lay(spread, first, second):
    return dot(spread, jnp.concatenate([jnp.concatenate(p, axis=0) for p in (first, second)], axis=1))


def interior_kernel(
    main_ref, lower_ref, fl_ref, fr_ref, spread_ref, one_ref, down2_ref, out_ref, side_ref, x1, x2
):
    low = lax.broadcasted_iota(jnp.int32, (16, 128), 1) < 64
    for s, side in enumerate((fl_ref, fr_ref)):
        for w in range(NWIN - 1):
            after = side[(w + 1) * 16:(w + 2) * 16].astype(F32)
            both = jnp.where(low, after, side[w * 16:(w + 1) * 16].astype(F32))
            side_ref[s, w * 16:(w + 1) * 16] = pltpu.roll(both, 64, 1).astype(BF16)

    def place(g, carry):
        row = pl.multiple_of(g * GROUP_POINTS, GROUP_POINTS)
        w = g * GROUP + GROUP - HALO
        edge = [pl.ds(pl.multiple_of((w + k) * 16, 16), 16) for k in range(GROUP)]
        for index in range(PHASES + 2):
            p = (index - 1) % PHASES
            own = [
                pl.ds(pl.multiple_of((w + k) * 128 + p * 16, 16), 16) for k in range(GROUP)
            ]
            first = [main_ref[o, :] for o in own]
            first += [ref[e, :] for ref in (fl_ref, fr_ref) for e in edge]
            second = [lower_ref[o, :] for o in own]
            second += [side_ref[s, e, :] for s in range(2) for e in edge]
            laid = lay(spread_ref[index], first, second).astype(BF16)
            x1[index, pl.ds(row, GROUP_POINTS), :] = laid[:, 0:128]
            x2[index, pl.ds(row, GROUP_POINTS), :] = laid[:, 128:256]
        return carry

    lax.fori_loop(0, TALL // GROUP - 2, place, 0)

    def store(rb, cb, down):
        out_ref[rb, cb] = down.astype(BF16)

    level_one(x1, x2, one_ref, down2_ref, store)


def interior(main, lower, from_left, from_right, spread, one, down2):
    vmem = pl.BlockSpec(memory_space=pltpu.VMEM)
    points = POINTS - 2 * GROUP_POINTS
    return pl.pallas_call(
        interior_kernel,
        in_specs=[vmem] * 7,
        out_specs=vmem,
        out_shape=jax.ShapeDtypeStruct((4, 4, points, 128), BF16),
        scratch_shapes=[
            pltpu.VMEM((2, NWIN * 16, 128), BF16),
            pltpu.VMEM((PHASES + 2, points, 128), BF16),
            pltpu.VMEM((PHASES + 2, points, 128), BF16),
        ],
        compiler_params=pltpu.CompilerParams(vmem_limit_bytes=32 * MIB),
        cost_estimate=pl.CostEstimate(
            flops=2 * points * 8 * (512 * 512 + 512 * 256),
            bytes_accessed=16 * MIB,
            transcendentals=0,
        ),
        name="interior",
    )(main, lower, from_left, from_right, spread, one, down2)


def encoder_kernel(
    inner_hbm, top_ref, bottom_ref, fl_ref, fr_ref, above_ref, below_ref, spread_ref, one_ref,
    down2_ref, two_hbm, down3_hbm, three_hbm, down4_hbm, four_hbm,
    out_ref,
    inner_ref, ext1, ext2, x1, x2, d2, d3, d4, stage,
    two_ref, down3_ref, three_ref, down4_ref, four_ref, sems,
):
    copies = [
        pltpu.make_async_copy(src, dst, sems.at[i])
        for i, (src, dst) in enumerate(
            (
                (down3_hbm, down3_ref),
                (three_hbm, three_ref),
                (down4_hbm, down4_ref),
                (four_hbm, four_ref),
                (inner_hbm, inner_ref),
                (two_hbm, two_ref),
            )
        )
    ]
    for i in (4, 5, 0, 1, 2, 3):
        copies[i].start()
    for side in range(2):
        for p in range(4):
            stage[side, p, 0:MARGIN] = jnp.zeros((MARGIN, 128), F32)
            stage[side, p, MARGIN + POINTS:] = jnp.zeros((MARGIN, 128), F32)

    m = HALO * 128
    for h in range(HALO):
        for source, i in ((above_ref, h), (below_ref, 3 * HALO + 1 + h)):
            ext1[i, 0:128] = source[h * 128:(h + 1) * 128]
            ext1[i, 128:144] = source[m + h * 16:m + h * 16 + 16]
            ext1[i, 144:160] = source[m + (HALO + h) * 16:m + (HALO + h) * 16 + 16]
    near = [(HALO + k, top_ref, k, k) for k in range(HALO + 1)]
    near += [(2 * HALO + 1 + k, bottom_ref, k, NWIN - HALO + k) for k in range(HALO)]
    for i, source, k, w in near:
        ext1[i, 0:128] = source[k * 128:(k + 1) * 128]
        ext1[i, 128:144] = fl_ref[w * 16:(w + 1) * 16]
        ext1[i, 144:160] = fr_ref[w * 16:(w + 1) * 16]

    low = lax.broadcasted_iota(jnp.int32, (160, 128), 1) < 64
    edges = (0, GROUP + 1)
    for base in edges:
        for k in range(GROUP):
            i = base + k
            after = min(i + 1, ext1.shape[0] - 1)
            both = jnp.where(low, ext1[after].astype(F32), ext1[i].astype(F32))
            ext2[i] = pltpu.roll(both, 64, 1).astype(BF16)

    for e, base in enumerate(edges):
        for index in range(PHASES + 2):
            p = (index - 1) % PHASES
            sides = []
            for ext in (ext1, ext2):
                pieces = [ext[base + k, p * 16:(p + 1) * 16] for k in range(GROUP)]
                pieces += [ext[base + k, 128:144] for k in range(GROUP)]
                pieces += [ext[base + k, 144:160] for k in range(GROUP)]
                sides.append(pieces)
            laid = lay(spread_ref[index], *sides).astype(BF16)
            x1[index, e * GROUP_POINTS:(e + 1) * GROUP_POINTS] = laid[:, 0:128]
            x2[index, e * GROUP_POINTS:(e + 1) * GROUP_POINTS] = laid[:, 128:256]

    across, below = lax.axis_size("tx"), lax.axis_size("ty")
    x, y = lax.axis_index("tx"), lax.axis_index("ty")
    least_w, most_w = jnp.where(y > 0, 0, HALO), jnp.where(y < below - 1, TALL, HALO + NWIN)
    least_a, most_a = jnp.where(x > 0, 0, HALO), jnp.where(x < across - 1, WIDE, HALO + SPOTS)
    point = lax.broadcasted_iota(jnp.int32, (POINTS, 128), 0)
    w = (point * (65536 // WIDE + 1)) >> 16
    a = point - w * WIDE
    inside = (w >= least_w) & (w < most_w) & (a >= least_a) & (a < most_a)
    mask = inside.astype(F32)
    mask2 = jnp.concatenate([mask, mask], axis=1)
    mask4 = jnp.concatenate([mask2, mask2], axis=1)

    def put(dst, i, j, value, last):
        rows = [(i + 1, 0)]
        if i == last:
            rows.append((0, WIDE))
        if i == 0:
            rows.append((last + 2, -WIDE))
        cols = [(j + 1, 0)]
        if j == last:
            cols.append((0, 1))
        if j == 0:
            cols.append((last + 2, -1))
        dst[i + 1, j + 1] = value.astype(BF16)
        side = (i + j) % 2
        for p in range(value.shape[1] // 128):
            lanes = slice(p * 128, (p + 1) * 128)
            stage[side, p, MARGIN:MARGIN + POINTS] = value[:, lanes]
            for r, row_shift in rows:
                for c, col_shift in cols:
                    shift = row_shift + col_shift
                    if shift:
                        moved = stage[side, p, MARGIN - shift:MARGIN - shift + POINTS]
                        dst[r, c, :, lanes] = moved.astype(BF16)

    copies[4].wait()

    def store(rb, cb, down):
        inner = inner_ref[rb, cb].astype(F32)
        down = jnp.concatenate([down[:GROUP_POINTS], inner, down[GROUP_POINTS:]], axis=0)
        if rb == 3:
            down = pltpu.roll(down, WIDE, 0)
        put(d2, (rb + 1) % 4, cb, down * mask, 3)

    level_one(x1, x2, one_ref, down2_ref, store)

    copies[5].wait()
    copies[0].wait()
    for rp in range(2):
        for j in range(2):
            taps = [
                jnp.concatenate(
                    [d2[2 * rp + r, 2 * j + v2 + v] for r in range(4) for v in range(3)], axis=1
                )
                for v2 in range(2)
            ]
            level = relu(dot(jnp.concatenate(taps, axis=0), two_ref[...])).astype(BF16)
            total = dot(level[:POINTS], down3_ref[0]) + dot(level[POINTS:], down3_ref[1])
            put(d3, rp, j, relu(total) * mask2, 1)

    copies[1].wait()
    copies[2].wait()
    total = None
    for i in range(2):
        taps = [
            jnp.concatenate([d3[i + u, j + v] for u in range(3) for v in range(3)], axis=1)
            for j in range(2)
        ]
        level = relu(dot(jnp.concatenate(taps, axis=0), three_ref[...])).astype(BF16)
        for j in range(2):
            part = dot(level[j * POINTS:(j + 1) * POINTS], down4_ref[i * 2 + j])
            total = part if total is None else total + part
    value = relu(total) * mask4

    for p in range(4):
        lanes = slice(p * 128, (p + 1) * 128)
        stage[0, p, MARGIN:MARGIN + POINTS] = value[:, lanes]
        for w in range(NWIN):
            for u in range(3):
                for v in range(3):
                    start = MARGIN + (w + HALO + u - 1) * WIDE + HALO + v - 1
                    tap = stage[0, p, start:start + SPOTS]
                    d4[u, v, w * SPOTS:(w + 1) * SPOTS, lanes] = tap.astype(BF16)

    copies[3].wait()
    taps = jnp.concatenate([d4[u, v] for u in range(3) for v in range(3)], axis=1)
    out_ref[...] = relu(dot(taps, four_ref[...])).astype(BF16)


def encoder(inner, edges, spread, one, down2, two, down3, three, down4, four):
    vmem = pl.BlockSpec(memory_space=pltpu.VMEM)
    hbm = pl.BlockSpec(memory_space=pl.ANY)
    rim = 2 * GROUP_POINTS
    return pl.pallas_call(
        encoder_kernel,
        in_specs=[hbm] + [vmem] * 9 + [hbm] * 5,
        out_specs=vmem,
        out_shape=jax.ShapeDtypeStruct((NWIN * SPOTS, four.shape[-1]), BF16),
        scratch_shapes=[
            pltpu.VMEM(inner.shape, BF16),
            pltpu.VMEM((2 * GROUP + 1, 160, 128), BF16),
            pltpu.VMEM((2 * GROUP + 1, 160, 128), BF16),
            pltpu.VMEM((PHASES + 2, rim, 128), BF16),
            pltpu.VMEM((PHASES + 2, rim, 128), BF16),
            pltpu.VMEM((6, 6, POINTS, 128), BF16),
            pltpu.VMEM((4, 4, POINTS, 256), BF16),
            pltpu.VMEM((3, 3, NWIN * SPOTS, 512), BF16),
            pltpu.VMEM((2, 4, POINTS + 2 * MARGIN, 128), F32),
            pltpu.VMEM(two.shape, BF16),
            pltpu.VMEM(down3.shape, BF16),
            pltpu.VMEM(three.shape, BF16),
            pltpu.VMEM(down4.shape, BF16),
            pltpu.VMEM(four.shape, BF16),
            pltpu.SemaphoreType.DMA((6,)),
        ],
        compiler_params=pltpu.CompilerParams(vmem_limit_bytes=44 * MIB),
        name="encoder",
    )(inner, *edges, spread, one, down2, two, down3, three, down4, four)


def level_one_weights(kernel):
    kernel = jnp.pad(kernel, ((0, 0), (0, 0), (0, 16 - BANDS), (0, 0)))
    columns = []
    for rb in range(2):
        for i in range(2):
            for j in range(2):
                top = 1 + 2 * rb + i
                wide = jnp.pad(kernel, ((top, 5 - top), (j, 1 - j), (0, 0), (0, 0)))
                columns.append(wide.transpose(1, 0, 2, 3).reshape(4 * 8 * 16, -1))
    return jnp.concatenate(columns, axis=1)


def level_two_weights(kernel):
    none = ((0, 0),) * 3
    pair = [jnp.pad(kernel, ((i, 1 - i),) + none) for i in range(2)]
    return jnp.concatenate(pair, axis=3).reshape(12 * kernel.shape[2], -1)


def body(
    granule_blocks, row_weights, column_bank, destination, window_index, bank_index,
    kernel_one, reduce_two, kernel_two, reduce_three, kernel_three, reduce_four, kernel_four,
):
    axes = ("tx", "ty")
    tiles = lax.axis_size("tx") * lax.axis_size("ty")
    slots = resample(
        granule_blocks, row_weights, column_bank, destination, window_index, bank_index, tiles
    )
    received = lax.all_to_all(slots, axes, split_axis=0, concat_axis=0, tiled=True)
    one = level_one_weights(kernel_one)
    two = level_two_weights(kernel_two)
    down3 = reduce_three.transpose(1, 0, 2, 3).reshape(2, 256, 256)
    received, one, two, down3 = lax.optimization_barrier((received, one, two, down3))
    gridded, lines, left, right = grid(received)
    from_left, from_right = exchange_columns(left, right)
    main, lower, top, bottom = turn(lines)
    above, below = exchange_rows(top, bottom, from_left, from_right)
    spread = jnp.asarray(spread_matrix(), BF16)
    down2 = reduce_two.reshape(256, 128)
    inner = interior(main, lower, from_left, from_right, spread, one, down2)
    flat = encoder(
        inner, (top, bottom, from_left, from_right, above, below), spread, one, down2,
        two, down3,
        kernel_three.reshape(9 * 256, 256),
        reduce_four.reshape(4, 256, 512),
        kernel_four.reshape(9 * 512, 512),
    )
    return gridded, flat.reshape(NWIN, SPOTS, -1).transpose(2, 0, 1)


def solution(mesh):
    both = P(("tx", "ty"))
    in_specs = (both, both, P(), both, both, both) + (P(),) * 7
    out_specs = (P(None, "ty", "tx"), P(None, "ty", "tx"))
    return jax.shard_map(body, mesh=mesh, in_specs=in_specs, out_specs=out_specs, check_vma=False)
```

```python
import functools

import jax
import jax.numpy as jnp
import numpy as np
from jax import lax
from jax.experimental import pallas as pl
from jax.experimental.pallas import tpu as pltpu
from jax.sharding import PartitionSpec as P

BF16 = jnp.bfloat16
F32 = jnp.float32
BANDS = 13
SRC_ROWS = 16
WIN_ROWS = 8
CAP = 2
NWIN = 32
TILE_COLS = 128
LINES = BANDS * WIN_ROWS
PACKED = CAP * LINES + WIN_ROWS
STEP_BLOCKS = 16
PIECES = 4
PHASES = 8
SPOTS = TILE_COLS // PHASES
HALO = 2
WIDE = SPOTS + 2 * HALO
TALL = NWIN + 2 * HALO
POINTS = WIDE * TALL
GROUP = 4
GROUP_POINTS = GROUP * WIDE
MARGIN = 24
MIB = 1024 * 1024


def dot(a, b):
    return jnp.dot(a, b, preferred_element_type=F32)


def dot_nt(a, b):
    return lax.dot_general(a, b, (((1,), (1,)), ((), ())), preferred_element_type=F32)


def resample_kernel(
    dest_ref, win_ref, choice_ref, weight_ref, raw_hbm, bank_ref, out_ref,
    raw_ref, rows_ref, held_ref, slot_win_ref, sems,
):
    tiles, blocks = held_ref.shape[0], dest_ref.shape[0]
    deep = BANDS * SRC_ROWS

    def fetch(group):
        part = pl.ds(group * STEP_BLOCKS, STEP_BLOCKS)
        return pltpu.make_async_copy(raw_hbm.at[part], raw_ref.at[part], sems.at[group])

    for group in range(blocks // STEP_BLOCKS):
        fetch(group).start()

    def clear(i, carry):
        held_ref[i] = 0
        for k in range(CAP):
            slot_win_ref[i * CAP + k] = -1
        return carry

    lax.fori_loop(0, tiles, clear, 0, unroll=8)

    turned = jnp.transpose(weight_ref[...].astype(F32)).astype(BF16)
    depth = lax.broadcasted_iota(jnp.int32, (WIN_ROWS * SRC_ROWS, 256), 0)
    lane = lax.broadcasted_iota(jnp.int32, (WIN_ROWS * SRC_ROWS, 256), 1)
    offset = depth - (lane & (SRC_ROWS - 1))
    for r in range(WIN_ROWS):
        wide = dot(turned, (offset == r * SRC_ROWS).astype(F32).astype(BF16))
        for h in range(2):
            rows_ref[h, pl.ds(r, blocks, stride=WIN_ROWS), :] = wide[:, h * 128:(h + 1) * 128]

    line = lax.broadcasted_iota(jnp.int32, (LINES, 256), 0)
    lane = lax.broadcasted_iota(jnp.int32, (LINES, 256), 1)
    own = (line >> 3) == (lane >> 4)
    spot = lax.broadcasted_iota(jnp.int32, (WIN_ROWS, TILE_COLS), 1)

    def work(group, carry):
        fetch(group).wait()
        rowed = []
        for j in range(STEP_BLOCKS):
            n = group * STEP_BLOCKS + j
            row = pl.multiple_of(n * WIN_ROWS, WIN_ROWS)
            rows = jnp.concatenate(
                [rows_ref[h, pl.ds(row, WIN_ROWS), :] for h in range(2)], axis=1
            )
            weights = jnp.where(own, jnp.concatenate([rows] * BANDS, axis=0), 0.0)
            rowed.append(dot(weights.astype(BF16)[:, 0:deep], raw_ref[n]).astype(BF16))
        done = []
        for j in range(STEP_BLOCKS):
            n = group * STEP_BLOCKS + j
            done.append(dot(rowed[j], bank_ref[choice_ref[n]]).astype(BF16))
        for j in range(STEP_BLOCKS):
            n = group * STEP_BLOCKS + j
            tile = dest_ref[n]
            rank = held_ref[tile]
            held_ref[tile] = rank + 1
            slot_win_ref[tile * CAP + rank] = win_ref[n]
            place = pl.ds(pl.multiple_of(rank * LINES, WIN_ROWS), LINES)
            out_ref[tile, place, :] = done[j]
        return carry

    lax.fori_loop(0, blocks // STEP_BLOCKS, work, 0)

    def number(i, carry):
        window = jnp.where(spot == 0, slot_win_ref[i * CAP], slot_win_ref[i * CAP + 1])
        out_ref[i, CAP * LINES:] = window.astype(F32).astype(BF16)
        return carry

    lax.fori_loop(0, tiles, number, 0, unroll=4)


def resample(granule_blocks, row_weights, column_bank, destination, window_index, bank_index, tiles):
    blocks = granule_blocks.shape[0]
    deep = BANDS * SRC_ROWS
    vmem = pl.BlockSpec(memory_space=pltpu.VMEM)
    smem = pl.BlockSpec(memory_space=pltpu.SMEM)
    return pl.pallas_call(
        resample_kernel,
        in_specs=[smem, smem, smem, vmem, pl.BlockSpec(memory_space=pl.ANY), vmem],
        out_specs=vmem,
        scratch_shapes=[
            pltpu.VMEM((blocks, deep, TILE_COLS), BF16),
            pltpu.VMEM((2, blocks * WIN_ROWS, 128), F32),
            pltpu.SMEM((tiles,), jnp.int32),
            pltpu.SMEM((tiles * CAP,), jnp.int32),
            pltpu.SemaphoreType.DMA((blocks // STEP_BLOCKS,)),
        ],
        out_shape=jax.ShapeDtypeStruct((tiles, PACKED, TILE_COLS), BF16),
        compiler_params=pltpu.CompilerParams(vmem_limit_bytes=60 * MIB),
        name="resample",
    )(
        destination, window_index, bank_index,
        row_weights.transpose(1, 2, 0).reshape(WIN_ROWS * SRC_ROWS, blocks),
        granule_blocks.reshape(blocks, deep, TILE_COLS),
        column_bank,
    )


def grid_kernel(
    got_hbm, perm_ref, grid_ref, lines_ref, left_ref, right_ref,
    got_ref, sum_ref, number_ref, win_ref, count_ref, sem, sems,
):
    tiles = got_ref.shape[0]
    size = tiles // PIECES
    last = pl.ds(CAP * LINES, WIN_ROWS)
    head = pltpu.make_async_copy(got_hbm.at[:, last], got_ref.at[:, last], sems.at[PIECES])
    head.start()

    def fetch(piece):
        part = pl.ds(piece * size, size), pl.ds(0, CAP * LINES)
        return pltpu.make_async_copy(got_hbm.at[part], got_ref.at[part], sems.at[piece])

    for piece in range(PIECES):
        fetch(piece).start()
    head.wait()
    numbers = got_ref[:, CAP * LINES:, :].astype(F32)
    number_ref[...] = jnp.max(numbers, axis=1).astype(jnp.int32)
    copy = pltpu.make_async_copy(number_ref, win_ref, sem)
    copy.start()

    def clear(w, carry):
        sum_ref[w] = jnp.zeros(sum_ref.shape[1:], F32)
        count_ref[w] = 0
        return carry

    lax.fori_loop(0, NWIN + 1, clear, 0)
    copy.wait()

    def add(t, carry):
        for k in range(CAP):
            w = win_ref[t, k]
            w = jnp.where(w < 0, NWIN, w)
            block = got_ref[t, k * LINES:(k + 1) * LINES].astype(F32)
            sum_ref[w, 0:LINES] = sum_ref[w, 0:LINES] + block
            count_ref[w] = count_ref[w] + 1
        return carry

    def add_piece(piece, carry):
        fetch(piece).wait()
        return lax.fori_loop(piece * size, (piece + 1) * size, add, carry)

    lax.fori_loop(0, PIECES, add_piece, 0)

    def finish(group, carry):
        first = group * GROUP
        means = []
        for k in range(GROUP):
            w = first + k
            divisor = jnp.maximum(count_ref[w], 1).astype(F32)
            mean = (sum_ref[w, 0:LINES] / divisor).astype(BF16).astype(F32)
            sum_ref[w, 0:LINES] = mean
            means.append(mean)
        row = pl.multiple_of(first * WIN_ROWS, GROUP * WIN_ROWS)
        for b in range(BANDS):
            part = jnp.concatenate([m[b * WIN_ROWS:(b + 1) * WIN_ROWS] for m in means], axis=0)
            grid_ref[b, pl.ds(row, GROUP * WIN_ROWS), :] = part.astype(BF16)
        for pair in range(GROUP // 2):
            lines = jnp.concatenate(
                [
                    sum_ref[first + pair * 2 + k, pl.ds(r, 16, stride=WIN_ROWS), :]
                    for k in range(2)
                    for r in range(WIN_ROWS)
                ],
                axis=0,
            ).astype(BF16)
            row = pl.multiple_of((first + pair * 2) * 128, 256)
            lines_ref[pl.ds(row, 256), :] = lines
            both = dot_nt(perm_ref[...], lines).astype(BF16)
            for k in range(2):
                w = first + pair * 2 + k
                turned = both[:, k * 128:(k + 1) * 128]
                left_ref[pl.ds(pl.multiple_of(w * 16, 16), 16), :] = turned[0:16]
                right_ref[pl.ds(pl.multiple_of(w * 16, 16), 16), :] = turned[16:32]
        return carry

    lax.fori_loop(0, NWIN // GROUP, finish, 0)


def grid(received):
    tiles = received.shape[0]
    perm = np.zeros((32, TILE_COLS), np.float32)
    for p in range(PHASES):
        for a in range(HALO):
            perm[p * HALO + a, a * PHASES + p] = 1.0
            perm[16 + p * HALO + a, (SPOTS - HALO + a) * PHASES + p] = 1.0
    vmem = pl.BlockSpec(memory_space=pltpu.VMEM)
    return pl.pallas_call(
        grid_kernel,
        in_specs=[pl.BlockSpec(memory_space=pl.ANY), vmem],
        out_specs=[vmem] * 4,
        out_shape=[
            jax.ShapeDtypeStruct((BANDS, NWIN * WIN_ROWS, TILE_COLS), BF16),
            jax.ShapeDtypeStruct((NWIN * 128, 128), BF16),
            jax.ShapeDtypeStruct((NWIN * 16, 128), BF16),
            jax.ShapeDtypeStruct((NWIN * 16, 128), BF16),
        ],
        scratch_shapes=[
            pltpu.VMEM(received.shape, BF16),
            pltpu.VMEM((NWIN + 1, 128, TILE_COLS), F32),
            pltpu.VMEM((tiles, TILE_COLS), jnp.int32),
            pltpu.SMEM((tiles, TILE_COLS), jnp.int32),
            pltpu.SMEM((NWIN + 1,), jnp.int32),
            pltpu.SemaphoreType.DMA,
            pltpu.SemaphoreType.DMA((PIECES + 1,)),
        ],
        compiler_params=pltpu.CompilerParams(vmem_limit_bytes=24 * MIB),
        name="grid",
    )(received, jnp.asarray(perm, BF16))


def turn_kernel(lines_ref, perm_ref, main_ref, lower_ref, top_ref, bottom_ref):
    def step(i, carry):
        for k in range(2):
            w = i * 2 + k
            start = pl.multiple_of(w * 128, 128)
            below = pl.multiple_of(jnp.minimum(w * 128 + 64, (NWIN - 1) * 128), 64)
            lines = jnp.concatenate(
                [lines_ref[pl.ds(start, 128), :], lines_ref[pl.ds(below, 128), :]], axis=0
            )
            both = dot_nt(perm_ref[...], lines).astype(BF16)
            main_ref[pl.ds(start, 128), :] = both[:, 0:128]
            lower_ref[pl.ds(start, 128), :] = both[:, 128:256]
        return carry

    lax.fori_loop(0, NWIN // 2, step, 0, unroll=2)
    top_ref[...] = main_ref[0:top_ref.shape[0]]
    bottom_ref[...] = main_ref[(NWIN - HALO) * 128:]


def turn(lines):
    perm = np.zeros((TILE_COLS, TILE_COLS), np.float32)
    for p in range(PHASES):
        for a in range(SPOTS):
            perm[p * SPOTS + a, a * PHASES + p] = 1.0
    vmem = pl.BlockSpec(memory_space=pltpu.VMEM)
    return pl.pallas_call(
        turn_kernel,
        in_specs=[vmem] * 2,
        out_specs=[vmem] * 4,
        out_shape=[
            jax.ShapeDtypeStruct((NWIN * 128, 128), BF16),
            jax.ShapeDtypeStruct((NWIN * 128, 128), BF16),
            jax.ShapeDtypeStruct(((HALO + 1) * 128, 128), BF16),
            jax.ShapeDtypeStruct((HALO * 128, 128), BF16),
        ],
        compiler_params=pltpu.CompilerParams(vmem_limit_bytes=16 * MIB),
        cost_estimate=pl.CostEstimate(
            flops=2 * NWIN * 128 ** 3 * 2, bytes_accessed=8 * MIB, transcendentals=0
        ),
        name="turn",
    )(lines, jnp.asarray(perm, BF16))


def exchange_columns(left, right):
    across = lax.axis_size("tx")
    right_ward = [(i, i + 1) for i in range(across - 1)]
    left_ward = [(t, s) for s, t in right_ward]
    return lax.ppermute(right, "tx", right_ward), lax.ppermute(left, "tx", left_ward)


def exchange_rows(top, bottom, from_left, from_right):
    down = lax.axis_size("ty")
    down_ward = [(i, i + 1) for i in range(down - 1)]
    up_ward = [(t, s) for s, t in down_ward]
    m, h = HALO * 128, HALO * 16
    first = jnp.concatenate([top[:m], from_left[:h], from_right[:h]], axis=0)
    last = jnp.concatenate([bottom, from_left[-h:], from_right[-h:]], axis=0)
    return lax.ppermute(last, "ty", down_ward), lax.ppermute(first, "ty", up_ward)


def spread_matrix():
    out = np.zeros((PHASES + 2, GROUP_POINTS, GROUP * 48), np.float32)
    for index in range(PHASES + 2):
        p = (index - 1) % PHASES
        shift = -1 if index == 0 else (1 if index == PHASES + 1 else 0)
        for k in range(GROUP):
            for a in range(WIDE):
                s = a + shift
                row = k * WIDE + a
                if s < 0 or s >= WIDE:
                    continue
                if s < HALO:
                    out[index, row, GROUP * 16 + k * 16 + p * HALO + s] = 1.0
                elif s < HALO + SPOTS:
                    out[index, row, k * 16 + s - HALO] = 1.0
                else:
                    out[index, row, GROUP * 32 + k * 16 + p * HALO + s - HALO - SPOTS] = 1.0
    return out


def relu(x):
    return jnp.maximum(x, 0.0)


def summed(taps, weights_ref, depth):
    total = None
    for k, tap in enumerate(taps):
        part = dot(tap(), weights_ref[k * depth:(k + 1) * depth])
        total = part if total is None else total + part
    return total


def level_one(x1, x2, one_ref, down2_ref, store):
    for cb in range(4):
        for version, x in enumerate((x1, x2)):
            taps = jnp.concatenate([x[2 * cb + k] for k in range(4)], axis=1)
            level = relu(dot(taps, one_ref[...])).astype(BF16)
            for half in range(2):
                down = relu(dot(level[:, half * 256:(half + 1) * 256], down2_ref[...]))
                store(2 * version + half, cb, down)


def lay(spread, first, second):
    return dot(spread, jnp.concatenate([jnp.concatenate(p, axis=0) for p in (first, second)], axis=1))


def interior_kernel(
    main_ref, lower_ref, fl_ref, fr_ref, spread_ref, one_ref, down2_ref, out_ref, side_ref, x1, x2
):
    low = lax.broadcasted_iota(jnp.int32, (16, 128), 1) < 64
    for s, side in enumerate((fl_ref, fr_ref)):
        for w in range(NWIN - 1):
            after = side[(w + 1) * 16:(w + 2) * 16].astype(F32)
            both = jnp.where(low, after, side[w * 16:(w + 1) * 16].astype(F32))
            side_ref[s, w * 16:(w + 1) * 16] = pltpu.roll(both, 64, 1).astype(BF16)

    def place(g, carry):
        row = pl.multiple_of(g * GROUP_POINTS, GROUP_POINTS)
        w = g * GROUP + GROUP - HALO
        edge = [pl.ds(pl.multiple_of((w + k) * 16, 16), 16) for k in range(GROUP)]
        for index in range(PHASES + 2):
            p = (index - 1) % PHASES
            own = [
                pl.ds(pl.multiple_of((w + k) * 128 + p * 16, 16), 16) for k in range(GROUP)
            ]
            first = [main_ref[o, :] for o in own]
            first += [ref[e, :] for ref in (fl_ref, fr_ref) for e in edge]
            second = [lower_ref[o, :] for o in own]
            second += [side_ref[s, e, :] for s in range(2) for e in edge]
            laid = lay(spread_ref[index], first, second).astype(BF16)
            x1[index, pl.ds(row, GROUP_POINTS), :] = laid[:, 0:128]
            x2[index, pl.ds(row, GROUP_POINTS), :] = laid[:, 128:256]
        return carry

    lax.fori_loop(0, TALL // GROUP - 2, place, 0)

    def store(rb, cb, down):
        out_ref[rb, cb] = down.astype(BF16)

    level_one(x1, x2, one_ref, down2_ref, store)


def interior(main, lower, from_left, from_right, spread, one, down2):
    vmem = pl.BlockSpec(memory_space=pltpu.VMEM)
    points = POINTS - 2 * GROUP_POINTS
    return pl.pallas_call(
        interior_kernel,
        in_specs=[vmem] * 7,
        out_specs=vmem,
        out_shape=jax.ShapeDtypeStruct((4, 4, points, 128), BF16),
        scratch_shapes=[
            pltpu.VMEM((2, NWIN * 16, 128), BF16),
            pltpu.VMEM((PHASES + 2, points, 128), BF16),
            pltpu.VMEM((PHASES + 2, points, 128), BF16),
        ],
        compiler_params=pltpu.CompilerParams(vmem_limit_bytes=32 * MIB),
        cost_estimate=pl.CostEstimate(
            flops=2 * points * 8 * (512 * 512 + 512 * 256),
            bytes_accessed=16 * MIB,
            transcendentals=0,
        ),
        name="interior",
    )(main, lower, from_left, from_right, spread, one, down2)


def encoder_kernel(
    inner_hbm, top_ref, bottom_ref, fl_ref, fr_ref, above_ref, below_ref, spread_ref, one_ref,
    down2_ref, two_hbm, down3_hbm, three_hbm, down4_hbm, four_hbm,
    out_ref,
    inner_ref, ext1, ext2, x1, x2, d2, d3, d4, stage,
    two_ref, down3_ref, three_ref, down4_ref, four_ref, sems,
):
    copies = [
        pltpu.make_async_copy(src, dst, sems.at[i])
        for i, (src, dst) in enumerate(
            (
                (down3_hbm, down3_ref),
                (three_hbm, three_ref),
                (down4_hbm, down4_ref),
                (four_hbm, four_ref),
                (inner_hbm, inner_ref),
                (two_hbm, two_ref),
            )
        )
    ]
    for i in (4, 5, 0, 1, 2, 3):
        copies[i].start()
    for side in range(2):
        for p in range(4):
            stage[side, p, 0:MARGIN] = jnp.zeros((MARGIN, 128), F32)
            stage[side, p, MARGIN + POINTS:] = jnp.zeros((MARGIN, 128), F32)

    m = HALO * 128
    for h in range(HALO):
        for source, i in ((above_ref, h), (below_ref, 3 * HALO + 1 + h)):
            ext1[i, 0:128] = source[h * 128:(h + 1) * 128]
            ext1[i, 128:144] = source[m + h * 16:m + h * 16 + 16]
            ext1[i, 144:160] = source[m + (HALO + h) * 16:m + (HALO + h) * 16 + 16]
    near = [(HALO + k, top_ref, k, k) for k in range(HALO + 1)]
    near += [(2 * HALO + 1 + k, bottom_ref, k, NWIN - HALO + k) for k in range(HALO)]
    for i, source, k, w in near:
        ext1[i, 0:128] = source[k * 128:(k + 1) * 128]
        ext1[i, 128:144] = fl_ref[w * 16:(w + 1) * 16]
        ext1[i, 144:160] = fr_ref[w * 16:(w + 1) * 16]

    low = lax.broadcasted_iota(jnp.int32, (160, 128), 1) < 64
    edges = (0, GROUP + 1)
    for base in edges:
        for k in range(GROUP):
            i = base + k
            after = min(i + 1, ext1.shape[0] - 1)
            both = jnp.where(low, ext1[after].astype(F32), ext1[i].astype(F32))
            ext2[i] = pltpu.roll(both, 64, 1).astype(BF16)

    for e, base in enumerate(edges):
        for index in range(PHASES + 2):
            p = (index - 1) % PHASES
            sides = []
            for ext in (ext1, ext2):
                pieces = [ext[base + k, p * 16:(p + 1) * 16] for k in range(GROUP)]
                pieces += [ext[base + k, 128:144] for k in range(GROUP)]
                pieces += [ext[base + k, 144:160] for k in range(GROUP)]
                sides.append(pieces)
            laid = lay(spread_ref[index], *sides).astype(BF16)
            x1[index, e * GROUP_POINTS:(e + 1) * GROUP_POINTS] = laid[:, 0:128]
            x2[index, e * GROUP_POINTS:(e + 1) * GROUP_POINTS] = laid[:, 128:256]

    across, below = lax.axis_size("tx"), lax.axis_size("ty")
    x, y = lax.axis_index("tx"), lax.axis_index("ty")
    least_w, most_w = jnp.where(y > 0, 0, HALO), jnp.where(y < below - 1, TALL, HALO + NWIN)
    least_a, most_a = jnp.where(x > 0, 0, HALO), jnp.where(x < across - 1, WIDE, HALO + SPOTS)
    point = lax.broadcasted_iota(jnp.int32, (POINTS, 128), 0)
    w = (point * (65536 // WIDE + 1)) >> 16
    a = point - w * WIDE
    inside = (w >= least_w) & (w < most_w) & (a >= least_a) & (a < most_a)
    mask = inside.astype(F32)
    mask2 = jnp.concatenate([mask, mask], axis=1)
    mask4 = jnp.concatenate([mask2, mask2], axis=1)

    def put(dst, i, j, value, last):
        rows = [(i + 1, 0)]
        if i == last:
            rows.append((0, WIDE))
        if i == 0:
            rows.append((last + 2, -WIDE))
        cols = [(j + 1, 0)]
        if j == last:
            cols.append((0, 1))
        if j == 0:
            cols.append((last + 2, -1))
        dst[i + 1, j + 1] = value.astype(BF16)
        side = (i + j) % 2
        for p in range(value.shape[1] // 128):
            lanes = slice(p * 128, (p + 1) * 128)
            stage[side, p, MARGIN:MARGIN + POINTS] = value[:, lanes]
            for r, row_shift in rows:
                for c, col_shift in cols:
                    shift = row_shift + col_shift
                    if shift:
                        moved = stage[side, p, MARGIN - shift:MARGIN - shift + POINTS]
                        dst[r, c, :, lanes] = moved.astype(BF16)

    copies[4].wait()

    def store(rb, cb, down):
        inner = inner_ref[rb, cb].astype(F32)
        down = jnp.concatenate([down[:GROUP_POINTS], inner, down[GROUP_POINTS:]], axis=0)
        if rb == 3:
            down = pltpu.roll(down, WIDE, 0)
        put(d2, (rb + 1) % 4, cb, down * mask, 3)

    level_one(x1, x2, one_ref, down2_ref, store)

    copies[5].wait()
    copies[0].wait()
    for rp in range(2):
        for j in range(2):
            total = None
            for v2 in range(2):
                spots = [(2 * rp + r, 2 * j + v2 + v) for r in range(4) for v in range(3)]
                pairs = [
                    lambda k=k: jnp.concatenate([d2[spots[2 * k]], d2[spots[2 * k + 1]]], axis=1)
                    for k in range(6)
                ]
                level = relu(summed(pairs, two_ref, 256)).astype(BF16)
                part = dot(level, down3_ref[v2])
                total = part if total is None else total + part
            put(d3, rp, j, relu(total) * mask2, 1)

    copies[1].wait()
    copies[2].wait()
    total = None
    for i in range(2):
        for j in range(2):
            taps = [lambda u=u, v=v: d3[i + u, j + v] for u in range(3) for v in range(3)]
            level = relu(summed(taps, three_ref, 256)).astype(BF16)
            part = dot(level, down4_ref[i * 2 + j])
            total = part if total is None else total + part
    value = relu(total) * mask4

    for p in range(4):
        lanes = slice(p * 128, (p + 1) * 128)
        stage[0, p, MARGIN:MARGIN + POINTS] = value[:, lanes]
        for w in range(NWIN):
            for u in range(3):
                for v in range(3):
                    start = MARGIN + (w + HALO + u - 1) * WIDE + HALO + v - 1
                    tap = stage[0, p, start:start + SPOTS]
                    d4[u, v, w * SPOTS:(w + 1) * SPOTS, lanes] = tap.astype(BF16)

    copies[3].wait()
    taps = [lambda u=u, v=v: d4[u, v] for u in range(3) for v in range(3)]
    out_ref[...] = relu(summed(taps, four_ref, 512)).astype(BF16)


def encoder(inner, edges, spread, one, down2, two, down3, three, down4, four):
    vmem = pl.BlockSpec(memory_space=pltpu.VMEM)
    hbm = pl.BlockSpec(memory_space=pl.ANY)
    rim = 2 * GROUP_POINTS
    return pl.pallas_call(
        encoder_kernel,
        in_specs=[hbm] + [vmem] * 9 + [hbm] * 5,
        out_specs=vmem,
        out_shape=jax.ShapeDtypeStruct((NWIN * SPOTS, four.shape[-1]), BF16),
        scratch_shapes=[
            pltpu.VMEM(inner.shape, BF16),
            pltpu.VMEM((2 * GROUP + 1, 160, 128), BF16),
            pltpu.VMEM((2 * GROUP + 1, 160, 128), BF16),
            pltpu.VMEM((PHASES + 2, rim, 128), BF16),
            pltpu.VMEM((PHASES + 2, rim, 128), BF16),
            pltpu.VMEM((6, 6, POINTS, 128), BF16),
            pltpu.VMEM((4, 4, POINTS, 256), BF16),
            pltpu.VMEM((3, 3, NWIN * SPOTS, 512), BF16),
            pltpu.VMEM((2, 4, POINTS + 2 * MARGIN, 128), F32),
            pltpu.VMEM(two.shape, BF16),
            pltpu.VMEM(down3.shape, BF16),
            pltpu.VMEM(three.shape, BF16),
            pltpu.VMEM(down4.shape, BF16),
            pltpu.VMEM(four.shape, BF16),
            pltpu.SemaphoreType.DMA((6,)),
        ],
        compiler_params=pltpu.CompilerParams(vmem_limit_bytes=44 * MIB),
        name="encoder",
    )(inner, *edges, spread, one, down2, two, down3, three, down4, four)


def level_one_weights(kernel):
    kernel = jnp.pad(kernel, ((0, 0), (0, 0), (0, 16 - BANDS), (0, 0)))
    columns = []
    for rb in range(2):
        for i in range(2):
            for j in range(2):
                top = 1 + 2 * rb + i
                wide = jnp.pad(kernel, ((top, 5 - top), (j, 1 - j), (0, 0), (0, 0)))
                columns.append(wide.transpose(1, 0, 2, 3).reshape(4 * 8 * 16, -1))
    return jnp.concatenate(columns, axis=1)


def level_two_weights(kernel):
    none = ((0, 0),) * 3
    pair = [jnp.pad(kernel, ((i, 1 - i),) + none) for i in range(2)]
    return jnp.concatenate(pair, axis=3).reshape(12 * kernel.shape[2], -1)


def body(
    granule_blocks, row_weights, column_bank, destination, window_index, bank_index,
    kernel_one, reduce_two, kernel_two, reduce_three, kernel_three, reduce_four, kernel_four,
):
    axes = ("tx", "ty")
    tiles = lax.axis_size("tx") * lax.axis_size("ty")
    slots = resample(
        granule_blocks, row_weights, column_bank, destination, window_index, bank_index, tiles
    )
    received = lax.all_to_all(slots, axes, split_axis=0, concat_axis=0, tiled=True)
    one = level_one_weights(kernel_one)
    two = level_two_weights(kernel_two)
    down3 = reduce_three.transpose(1, 0, 2, 3).reshape(2, 256, 256)
    received, one, two, down3 = lax.optimization_barrier((received, one, two, down3))
    gridded, lines, left, right = grid(received)
    from_left, from_right = exchange_columns(left, right)
    main, lower, top, bottom = turn(lines)
    above, below = exchange_rows(top, bottom, from_left, from_right)
    spread = jnp.asarray(spread_matrix(), BF16)
    down2 = reduce_two.reshape(256, 128)
    inner = interior(main, lower, from_left, from_right, spread, one, down2)
    flat = encoder(
        inner, (top, bottom, from_left, from_right, above, below), spread, one, down2,
        two, down3,
        kernel_three.reshape(9 * 256, 256),
        reduce_four.reshape(4, 256, 512),
        kernel_four.reshape(9 * 512, 512),
    )
    return gridded, flat.reshape(NWIN, SPOTS, -1).transpose(2, 0, 1)


def solution(mesh):
    both = P(("tx", "ty"))
    in_specs = (both, both, P(), both, both, both) + (P(),) * 7
    out_specs = (P(None, "ty", "tx"), P(None, "ty", "tx"))
    return jax.shard_map(body, mesh=mesh, in_specs=in_specs, out_specs=out_specs, check_vma=False)
```

```python
import functools

import jax
import jax.numpy as jnp
import numpy as np
from jax import lax
from jax.experimental import pallas as pl
from jax.experimental.pallas import tpu as pltpu
from jax.sharding import PartitionSpec as P

BF16 = jnp.bfloat16
F32 = jnp.float32
BANDS = 13
SRC_ROWS = 16
WIN_ROWS = 8
CAP = 2
NWIN = 32
TILE_COLS = 128
LINES = BANDS * WIN_ROWS
PACKED = CAP * LINES + WIN_ROWS
STEP_BLOCKS = 16
PIECES = 4
PHASES = 8
SPOTS = TILE_COLS // PHASES
HALO = 2
WIDE = SPOTS + 2 * HALO
TALL = NWIN + 2 * HALO
POINTS = WIDE * TALL
GROUP = 4
GROUP_POINTS = GROUP * WIDE
MARGIN = 24
MIB = 1024 * 1024


def dot(a, b):
    return jnp.dot(a, b, preferred_element_type=F32)


def dot_nt(a, b):
    return lax.dot_general(a, b, (((1,), (1,)), ((), ())), preferred_element_type=F32)


def resample_kernel(
    dest_ref, win_ref, choice_ref, weight_ref, raw_hbm, bank_ref, out_ref,
    raw_ref, rows_ref, held_ref, slot_win_ref, sems,
):
    tiles, blocks = held_ref.shape[0], dest_ref.shape[0]
    deep = BANDS * SRC_ROWS

    def fetch(group):
        part = pl.ds(group * STEP_BLOCKS, STEP_BLOCKS)
        return pltpu.make_async_copy(raw_hbm.at[part], raw_ref.at[part], sems.at[group])

    for group in range(blocks // STEP_BLOCKS):
        fetch(group).start()

    def clear(i, carry):
        held_ref[i] = 0
        for k in range(CAP):
            slot_win_ref[i * CAP + k] = -1
        return carry

    lax.fori_loop(0, tiles, clear, 0, unroll=8)

    turned = jnp.transpose(weight_ref[...].astype(F32)).astype(BF16)
    depth = lax.broadcasted_iota(jnp.int32, (WIN_ROWS * SRC_ROWS, 256), 0)
    lane = lax.broadcasted_iota(jnp.int32, (WIN_ROWS * SRC_ROWS, 256), 1)
    offset = depth - (lane & (SRC_ROWS - 1))
    for r in range(WIN_ROWS):
        wide = dot(turned, (offset == r * SRC_ROWS).astype(F32).astype(BF16))
        for h in range(2):
            rows_ref[h, pl.ds(r, blocks, stride=WIN_ROWS), :] = wide[:, h * 128:(h + 1) * 128]

    line = lax.broadcasted_iota(jnp.int32, (LINES, 256), 0)
    lane = lax.broadcasted_iota(jnp.int32, (LINES, 256), 1)
    own = (line >> 3) == (lane >> 4)
    spot = lax.broadcasted_iota(jnp.int32, (WIN_ROWS, TILE_COLS), 1)

    def work(group, carry):
        fetch(group).wait()
        rowed = []
        for j in range(STEP_BLOCKS):
            n = group * STEP_BLOCKS + j
            row = pl.multiple_of(n * WIN_ROWS, WIN_ROWS)
            rows = jnp.concatenate(
                [rows_ref[h, pl.ds(row, WIN_ROWS), :] for h in range(2)], axis=1
            )
            weights = jnp.where(own, jnp.concatenate([rows] * BANDS, axis=0), 0.0)
            rowed.append(dot(weights.astype(BF16)[:, 0:deep], raw_ref[n]).astype(BF16))
        done = []
        for j in range(STEP_BLOCKS):
            n = group * STEP_BLOCKS + j
            done.append(dot(rowed[j], bank_ref[choice_ref[n]]).astype(BF16))
        for j in range(STEP_BLOCKS):
            n = group * STEP_BLOCKS + j
            tile = dest_ref[n]
            rank = held_ref[tile]
            held_ref[tile] = rank + 1
            slot_win_ref[tile * CAP + rank] = win_ref[n]
            place = pl.ds(pl.multiple_of(rank * LINES, WIN_ROWS), LINES)
            out_ref[tile, place, :] = done[j]
        return carry

    lax.fori_loop(0, blocks // STEP_BLOCKS, work, 0)

    def number(i, carry):
        window = jnp.where(spot == 0, slot_win_ref[i * CAP], slot_win_ref[i * CAP + 1])
        out_ref[i, CAP * LINES:] = window.astype(F32).astype(BF16)
        return carry

    lax.fori_loop(0, tiles, number, 0, unroll=4)


def resample(granule_blocks, row_weights, column_bank, destination, window_index, bank_index, tiles):
    blocks = granule_blocks.shape[0]
    deep = BANDS * SRC_ROWS
    vmem = pl.BlockSpec(memory_space=pltpu.VMEM)
    smem = pl.BlockSpec(memory_space=pltpu.SMEM)
    return pl.pallas_call(
        resample_kernel,
        in_specs=[smem, smem, smem, vmem, pl.BlockSpec(memory_space=pl.ANY), vmem],
        out_specs=vmem,
        scratch_shapes=[
            pltpu.VMEM((blocks, deep, TILE_COLS), BF16),
            pltpu.VMEM((2, blocks * WIN_ROWS, 128), F32),
            pltpu.SMEM((tiles,), jnp.int32),
            pltpu.SMEM((tiles * CAP,), jnp.int32),
            pltpu.SemaphoreType.DMA((blocks // STEP_BLOCKS,)),
        ],
        out_shape=jax.ShapeDtypeStruct((tiles, PACKED, TILE_COLS), BF16),
        compiler_params=pltpu.CompilerParams(vmem_limit_bytes=60 * MIB),
        name="resample",
    )(
        destination, window_index, bank_index,
        row_weights.transpose(1, 2, 0).reshape(WIN_ROWS * SRC_ROWS, blocks),
        granule_blocks.reshape(blocks, deep, TILE_COLS),
        column_bank,
    )


def grid_kernel(
    got_hbm, perm_ref, grid_ref, lines_ref, left_ref, right_ref,
    got_ref, sum_ref, number_ref, win_ref, count_ref, sem, sems,
):
    tiles = got_ref.shape[0]
    size = tiles // PIECES
    last = pl.ds(CAP * LINES, WIN_ROWS)
    head = pltpu.make_async_copy(got_hbm.at[:, last], got_ref.at[:, last], sems.at[PIECES])
    head.start()

    def fetch(piece):
        part = pl.ds(piece * size, size), pl.ds(0, CAP * LINES)
        return pltpu.make_async_copy(got_hbm.at[part], got_ref.at[part], sems.at[piece])

    for piece in range(PIECES):
        fetch(piece).start()
    head.wait()
    numbers = got_ref[:, CAP * LINES:, :].astype(F32)
    number_ref[...] = jnp.max(numbers, axis=1).astype(jnp.int32)
    copy = pltpu.make_async_copy(number_ref, win_ref, sem)
    copy.start()

    def clear(w, carry):
        sum_ref[w] = jnp.zeros(sum_ref.shape[1:], F32)
        count_ref[w] = 0
        return carry

    lax.fori_loop(0, NWIN + 1, clear, 0)
    copy.wait()

    def add(t, carry):
        for k in range(CAP):
            w = win_ref[t, k]
            w = jnp.where(w < 0, NWIN, w)
            block = got_ref[t, k * LINES:(k + 1) * LINES].astype(F32)
            sum_ref[w, 0:LINES] = sum_ref[w, 0:LINES] + block
            count_ref[w] = count_ref[w] + 1
        return carry

    def add_piece(piece, carry):
        fetch(piece).wait()
        return lax.fori_loop(piece * size, (piece + 1) * size, add, carry)

    lax.fori_loop(0, PIECES, add_piece, 0)

    def finish(group, carry):
        first = group * GROUP
        means = []
        for k in range(GROUP):
            w = first + k
            divisor = jnp.maximum(count_ref[w], 1).astype(F32)
            mean = (sum_ref[w, 0:LINES] / divisor).astype(BF16).astype(F32)
            sum_ref[w, 0:LINES] = mean
            means.append(mean)
        row = pl.multiple_of(first * WIN_ROWS, GROUP * WIN_ROWS)
        for b in range(BANDS):
            part = jnp.concatenate([m[b * WIN_ROWS:(b + 1) * WIN_ROWS] for m in means], axis=0)
            grid_ref[b, pl.ds(row, GROUP * WIN_ROWS), :] = part.astype(BF16)
        for pair in range(GROUP // 2):
            lines = jnp.concatenate(
                [
                    sum_ref[first + pair * 2 + k, pl.ds(r, 16, stride=WIN_ROWS), :]
                    for k in range(2)
                    for r in range(WIN_ROWS)
                ],
                axis=0,
            ).astype(BF16)
            row = pl.multiple_of((first + pair * 2) * 128, 256)
            lines_ref[pl.ds(row, 256), :] = lines
            both = dot_nt(perm_ref[...], lines).astype(BF16)
            for k in range(2):
                w = first + pair * 2 + k
                turned = both[:, k * 128:(k + 1) * 128]
                left_ref[pl.ds(pl.multiple_of(w * 16, 16), 16), :] = turned[0:16]
                right_ref[pl.ds(pl.multiple_of(w * 16, 16), 16), :] = turned[16:32]
        return carry

    lax.fori_loop(0, NWIN // GROUP, finish, 0)


def grid(received):
    tiles = received.shape[0]
    perm = np.zeros((32, TILE_COLS), np.float32)
    for p in range(PHASES):
        for a in range(HALO):
            perm[p * HALO + a, a * PHASES + p] = 1.0
            perm[16 + p * HALO + a, (SPOTS - HALO + a) * PHASES + p] = 1.0
    vmem = pl.BlockSpec(memory_space=pltpu.VMEM)
    return pl.pallas_call(
        grid_kernel,
        in_specs=[pl.BlockSpec(memory_space=pl.ANY), vmem],
        out_specs=[vmem] * 4,
        out_shape=[
            jax.ShapeDtypeStruct((BANDS, NWIN * WIN_ROWS, TILE_COLS), BF16),
            jax.ShapeDtypeStruct((NWIN * 128, 128), BF16),
            jax.ShapeDtypeStruct((NWIN * 16, 128), BF16),
            jax.ShapeDtypeStruct((NWIN * 16, 128), BF16),
        ],
        scratch_shapes=[
            pltpu.VMEM(received.shape, BF16),
            pltpu.VMEM((NWIN + 1, 128, TILE_COLS), F32),
            pltpu.VMEM((tiles, TILE_COLS), jnp.int32),
            pltpu.SMEM((tiles, TILE_COLS), jnp.int32),
            pltpu.SMEM((NWIN + 1,), jnp.int32),
            pltpu.SemaphoreType.DMA,
            pltpu.SemaphoreType.DMA((PIECES + 1,)),
        ],
        compiler_params=pltpu.CompilerParams(vmem_limit_bytes=24 * MIB),
        name="grid",
    )(received, jnp.asarray(perm, BF16))


def turn_kernel(lines_ref, perm_ref, main_ref, lower_ref, top_ref, bottom_ref):
    def step(i, carry):
        for k in range(2):
            w = i * 2 + k
            start = pl.multiple_of(w * 128, 128)
            below = pl.multiple_of(jnp.minimum(w * 128 + 64, (NWIN - 1) * 128), 64)
            lines = jnp.concatenate(
                [lines_ref[pl.ds(start, 128), :], lines_ref[pl.ds(below, 128), :]], axis=0
            )
            both = dot_nt(perm_ref[...], lines).astype(BF16)
            main_ref[pl.ds(start, 128), :] = both[:, 0:128]
            lower_ref[pl.ds(start, 128), :] = both[:, 128:256]
        return carry

    lax.fori_loop(0, NWIN // 2, step, 0, unroll=2)
    top_ref[...] = main_ref[0:top_ref.shape[0]]
    bottom_ref[...] = main_ref[(NWIN - HALO) * 128:]


def turn(lines):
    perm = np.zeros((TILE_COLS, TILE_COLS), np.float32)
    for p in range(PHASES):
        for a in range(SPOTS):
            perm[p * SPOTS + a, a * PHASES + p] = 1.0
    vmem = pl.BlockSpec(memory_space=pltpu.VMEM)
    return pl.pallas_call(
        turn_kernel,
        in_specs=[vmem] * 2,
        out_specs=[vmem] * 4,
        out_shape=[
            jax.ShapeDtypeStruct((NWIN * 128, 128), BF16),
            jax.ShapeDtypeStruct((NWIN * 128, 128), BF16),
            jax.ShapeDtypeStruct(((HALO + 1) * 128, 128), BF16),
            jax.ShapeDtypeStruct((HALO * 128, 128), BF16),
        ],
        compiler_params=pltpu.CompilerParams(vmem_limit_bytes=16 * MIB),
        cost_estimate=pl.CostEstimate(
            flops=2 * NWIN * 128 ** 3 * 2, bytes_accessed=8 * MIB, transcendentals=0
        ),
        name="turn",
    )(lines, jnp.asarray(perm, BF16))


def exchange_columns(left, right):
    across = lax.axis_size("tx")
    right_ward = [(i, i + 1) for i in range(across - 1)]
    left_ward = [(t, s) for s, t in right_ward]
    return lax.ppermute(right, "tx", right_ward), lax.ppermute(left, "tx", left_ward)


def exchange_rows(top, bottom, from_left, from_right):
    down = lax.axis_size("ty")
    down_ward = [(i, i + 1) for i in range(down - 1)]
    up_ward = [(t, s) for s, t in down_ward]
    m, h = HALO * 128, HALO * 16
    first = jnp.concatenate([top[:m], from_left[:h], from_right[:h]], axis=0)
    last = jnp.concatenate([bottom, from_left[-h:], from_right[-h:]], axis=0)
    return lax.ppermute(last, "ty", down_ward), lax.ppermute(first, "ty", up_ward)


def spread_matrix():
    out = np.zeros((PHASES + 2, GROUP_POINTS, GROUP * 48), np.float32)
    for index in range(PHASES + 2):
        p = (index - 1) % PHASES
        shift = -1 if index == 0 else (1 if index == PHASES + 1 else 0)
        for k in range(GROUP):
            for a in range(WIDE):
                s = a + shift
                row = k * WIDE + a
                if s < 0 or s >= WIDE:
                    continue
                if s < HALO:
                    out[index, row, GROUP * 16 + k * 16 + p * HALO + s] = 1.0
                elif s < HALO + SPOTS:
                    out[index, row, k * 16 + s - HALO] = 1.0
                else:
                    out[index, row, GROUP * 32 + k * 16 + p * HALO + s - HALO - SPOTS] = 1.0
    return out


def relu(x):
    return jnp.maximum(x, 0.0)


def summed(taps, weights_ref, depth):
    total = None
    for k, tap in enumerate(taps):
        part = dot(tap(), weights_ref[k * depth:(k + 1) * depth])
        total = part if total is None else total + part
    return total


def level_one(x1, x2, one_ref, down2_ref, store):
    for cb in range(4):
        for version, x in enumerate((x1, x2)):
            taps = jnp.concatenate([x[2 * cb + k] for k in range(4)], axis=1)
            level = relu(dot(taps, one_ref[...])).astype(BF16)
            for half in range(2):
                down = relu(dot(level[:, half * 256:(half + 1) * 256], down2_ref[...]))
                store(2 * version + half, cb, down)


def lay(spread, first, second):
    return dot(spread, jnp.concatenate([jnp.concatenate(p, axis=0) for p in (first, second)], axis=1))


def interior_kernel(
    main_ref, lower_ref, fl_ref, fr_ref, spread_ref, one_ref, down2_ref, out_ref, side_ref, x1, x2
):
    low = lax.broadcasted_iota(jnp.int32, (16, 128), 1) < 64
    for s, side in enumerate((fl_ref, fr_ref)):
        for w in range(NWIN - 1):
            after = side[(w + 1) * 16:(w + 2) * 16].astype(F32)
            both = jnp.where(low, after, side[w * 16:(w + 1) * 16].astype(F32))
            side_ref[s, w * 16:(w + 1) * 16] = pltpu.roll(both, 64, 1).astype(BF16)

    def place(g, carry):
        row = pl.multiple_of(g * GROUP_POINTS, GROUP_POINTS)
        w = g * GROUP + GROUP - HALO
        edge = [pl.ds(pl.multiple_of((w + k) * 16, 16), 16) for k in range(GROUP)]
        for index in range(PHASES + 2):
            p = (index - 1) % PHASES
            own = [
                pl.ds(pl.multiple_of((w + k) * 128 + p * 16, 16), 16) for k in range(GROUP)
            ]
            first = [main_ref[o, :] for o in own]
            first += [ref[e, :] for ref in (fl_ref, fr_ref) for e in edge]
            second = [lower_ref[o, :] for o in own]
            second += [side_ref[s, e, :] for s in range(2) for e in edge]
            laid = lay(spread_ref[index], first, second).astype(BF16)
            x1[index, pl.ds(row, GROUP_POINTS), :] = laid[:, 0:128]
            x2[index, pl.ds(row, GROUP_POINTS), :] = laid[:, 128:256]
        return carry

    lax.fori_loop(0, TALL // GROUP - 2, place, 0)

    def store(rb, cb, down):
        out_ref[rb, cb] = down.astype(BF16)

    level_one(x1, x2, one_ref, down2_ref, store)


def interior(main, lower, from_left, from_right, spread, one, down2):
    vmem = pl.BlockSpec(memory_space=pltpu.VMEM)
    points = POINTS - 2 * GROUP_POINTS
    return pl.pallas_call(
        interior_kernel,
        in_specs=[vmem] * 7,
        out_specs=vmem,
        out_shape=jax.ShapeDtypeStruct((4, 4, points, 128), BF16),
        scratch_shapes=[
            pltpu.VMEM((2, NWIN * 16, 128), BF16),
            pltpu.VMEM((PHASES + 2, points, 128), BF16),
            pltpu.VMEM((PHASES + 2, points, 128), BF16),
        ],
        compiler_params=pltpu.CompilerParams(vmem_limit_bytes=32 * MIB),
        cost_estimate=pl.CostEstimate(
            flops=2 * points * 8 * (512 * 512 + 512 * 256),
            bytes_accessed=16 * MIB,
            transcendentals=0,
        ),
        name="interior",
    )(main, lower, from_left, from_right, spread, one, down2)


def encoder_kernel(
    inner_hbm, top_ref, bottom_ref, fl_ref, fr_ref, above_ref, below_ref, spread_ref, one_ref,
    down2_ref, two_hbm, down3_hbm, three_hbm, down4_hbm, four_hbm,
    out_ref,
    inner_ref, ext1, ext2, x1, x2, d2, d3, d4, stage, total_ref,
    two_ref, down3_ref, three_ref, down4_ref, four_ref, sems,
):
    copies = [
        pltpu.make_async_copy(src, dst, sems.at[i])
        for i, (src, dst) in enumerate(
            (
                (down3_hbm, down3_ref),
                (three_hbm, three_ref),
                (down4_hbm, down4_ref),
                (four_hbm, four_ref),
                (inner_hbm, inner_ref),
                (two_hbm, two_ref),
            )
        )
    ]
    for i in (4, 5, 0, 1, 2, 3):
        copies[i].start()
    for side in range(2):
        for p in range(4):
            stage[side, p, 0:MARGIN] = jnp.zeros((MARGIN, 128), F32)
            stage[side, p, MARGIN + POINTS:] = jnp.zeros((MARGIN, 128), F32)

    m = HALO * 128
    for h in range(HALO):
        for source, i in ((above_ref, h), (below_ref, 3 * HALO + 1 + h)):
            ext1[i, 0:128] = source[h * 128:(h + 1) * 128]
            ext1[i, 128:144] = source[m + h * 16:m + h * 16 + 16]
            ext1[i, 144:160] = source[m + (HALO + h) * 16:m + (HALO + h) * 16 + 16]
    near = [(HALO + k, top_ref, k, k) for k in range(HALO + 1)]
    near += [(2 * HALO + 1 + k, bottom_ref, k, NWIN - HALO + k) for k in range(HALO)]
    for i, source, k, w in near:
        ext1[i, 0:128] = source[k * 128:(k + 1) * 128]
        ext1[i, 128:144] = fl_ref[w * 16:(w + 1) * 16]
        ext1[i, 144:160] = fr_ref[w * 16:(w + 1) * 16]

    low = lax.broadcasted_iota(jnp.int32, (160, 128), 1) < 64
    edges = (0, GROUP + 1)
    for base in edges:
        for k in range(GROUP):
            i = base + k
            after = min(i + 1, ext1.shape[0] - 1)
            both = jnp.where(low, ext1[after].astype(F32), ext1[i].astype(F32))
            ext2[i] = pltpu.roll(both, 64, 1).astype(BF16)

    for e, base in enumerate(edges):
        for index in range(PHASES + 2):
            p = (index - 1) % PHASES
            sides = []
            for ext in (ext1, ext2):
                pieces = [ext[base + k, p * 16:(p + 1) * 16] for k in range(GROUP)]
                pieces += [ext[base + k, 128:144] for k in range(GROUP)]
                pieces += [ext[base + k, 144:160] for k in range(GROUP)]
                sides.append(pieces)
            laid = lay(spread_ref[index], *sides).astype(BF16)
            x1[index, e * GROUP_POINTS:(e + 1) * GROUP_POINTS] = laid[:, 0:128]
            x2[index, e * GROUP_POINTS:(e + 1) * GROUP_POINTS] = laid[:, 128:256]

    across, below = lax.axis_size("tx"), lax.axis_size("ty")
    x, y = lax.axis_index("tx"), lax.axis_index("ty")
    least_w, most_w = jnp.where(y > 0, 0, HALO), jnp.where(y < below - 1, TALL, HALO + NWIN)
    least_a, most_a = jnp.where(x > 0, 0, HALO), jnp.where(x < across - 1, WIDE, HALO + SPOTS)
    point = lax.broadcasted_iota(jnp.int32, (POINTS, 128), 0)
    w = (point * (65536 // WIDE + 1)) >> 16
    a = point - w * WIDE
    inside = (w >= least_w) & (w < most_w) & (a >= least_a) & (a < most_a)
    mask = inside.astype(F32)
    mask2 = jnp.concatenate([mask, mask], axis=1)
    mask4 = jnp.concatenate([mask2, mask2], axis=1)

    def put(dst, i, j, value, last):
        rows = [(i + 1, 0)]
        if i == last:
            rows.append((0, WIDE))
        if i == 0:
            rows.append((last + 2, -WIDE))
        cols = [(j + 1, 0)]
        if j == last:
            cols.append((0, 1))
        if j == 0:
            cols.append((last + 2, -1))
        dst[i + 1, j + 1] = value.astype(BF16)
        side = (i + j) % 2
        for p in range(value.shape[1] // 128):
            lanes = slice(p * 128, (p + 1) * 128)
            stage[side, p, MARGIN:MARGIN + POINTS] = value[:, lanes]
            for r, row_shift in rows:
                for c, col_shift in cols:
                    shift = row_shift + col_shift
                    if shift:
                        moved = stage[side, p, MARGIN - shift:MARGIN - shift + POINTS]
                        dst[r, c, :, lanes] = moved.astype(BF16)

    copies[4].wait()

    def store(rb, cb, down):
        inner = inner_ref[rb, cb].astype(F32)
        down = jnp.concatenate([down[:GROUP_POINTS], inner, down[GROUP_POINTS:]], axis=0)
        if rb == 3:
            down = pltpu.roll(down, WIDE, 0)
        put(d2, (rb + 1) % 4, cb, down * mask, 3)

    level_one(x1, x2, one_ref, down2_ref, store)

    copies[5].wait()
    copies[0].wait()
    for rp in range(2):
        for j in range(2):
            total_ref[:, 0:256] = jnp.zeros((POINTS, 256), F32)

            def column(v2, carry, rp=rp, j=j):
                spots = [(2 * rp + r, 2 * j + v2 + v) for r in range(4) for v in range(3)]
                pairs = [
                    lambda k=k: jnp.concatenate([d2[spots[2 * k]], d2[spots[2 * k + 1]]], axis=1)
                    for k in range(6)
                ]
                level = relu(summed(pairs, two_ref, 256)).astype(BF16)
                total_ref[:, 0:256] += dot(level, down3_ref[v2])
                return carry

            lax.fori_loop(0, 2, column, 0)
            put(d3, rp, j, relu(total_ref[:, 0:256]) * mask2, 1)

    copies[1].wait()
    copies[2].wait()
    total_ref[...] = jnp.zeros(total_ref.shape, F32)

    def phase(t, carry):
        i, j = t >> 1, t & 1
        taps = [lambda u=u, v=v: d3[i + u, j + v] for u in range(3) for v in range(3)]
        level = relu(summed(taps, three_ref, 256)).astype(BF16)
        total_ref[...] += dot(level, down4_ref[t])
        return carry

    lax.fori_loop(0, 4, phase, 0)
    value = relu(total_ref[...]) * mask4

    for p in range(4):
        stage[0, p, MARGIN:MARGIN + POINTS] = value[:, p * 128:(p + 1) * 128]

    def pack(p, carry):
        lanes = pl.ds(pl.multiple_of(p * 128, 128), 128)
        for w in range(NWIN):
            for u in range(3):
                for v in range(3):
                    start = MARGIN + (w + HALO + u - 1) * WIDE + HALO + v - 1
                    tap = stage[0, p, start:start + SPOTS]
                    d4[u, v, w * SPOTS:(w + 1) * SPOTS, lanes] = tap.astype(BF16)
        return carry

    lax.fori_loop(0, 4, pack, 0)

    copies[3].wait()
    taps = [lambda u=u, v=v: d4[u, v] for u in range(3) for v in range(3)]
    out_ref[...] = relu(summed(taps, four_ref, 512)).astype(BF16)


def encoder(inner, edges, spread, one, down2, two, down3, three, down4, four):
    vmem = pl.BlockSpec(memory_space=pltpu.VMEM)
    hbm = pl.BlockSpec(memory_space=pl.ANY)
    rim = 2 * GROUP_POINTS
    return pl.pallas_call(
        encoder_kernel,
        in_specs=[hbm] + [vmem] * 9 + [hbm] * 5,
        out_specs=vmem,
        out_shape=jax.ShapeDtypeStruct((NWIN * SPOTS, four.shape[-1]), BF16),
        scratch_shapes=[
            pltpu.VMEM(inner.shape, BF16),
            pltpu.VMEM((2 * GROUP + 1, 160, 128), BF16),
            pltpu.VMEM((2 * GROUP + 1, 160, 128), BF16),
            pltpu.VMEM((PHASES + 2, rim, 128), BF16),
            pltpu.VMEM((PHASES + 2, rim, 128), BF16),
            pltpu.VMEM((6, 6, POINTS, 128), BF16),
            pltpu.VMEM((4, 4, POINTS, 256), BF16),
            pltpu.VMEM((3, 3, NWIN * SPOTS, 512), BF16),
            pltpu.VMEM((2, 4, POINTS + 2 * MARGIN, 128), F32),
            pltpu.VMEM((POINTS, 512), F32),
            pltpu.VMEM(two.shape, BF16),
            pltpu.VMEM(down3.shape, BF16),
            pltpu.VMEM(three.shape, BF16),
            pltpu.VMEM(down4.shape, BF16),
            pltpu.VMEM(four.shape, BF16),
            pltpu.SemaphoreType.DMA((6,)),
        ],
        compiler_params=pltpu.CompilerParams(vmem_limit_bytes=44 * MIB),
        name="encoder",
    )(inner, *edges, spread, one, down2, two, down3, three, down4, four)


def level_one_weights(kernel):
    kernel = jnp.pad(kernel, ((0, 0), (0, 0), (0, 16 - BANDS), (0, 0)))
    columns = []
    for rb in range(2):
        for i in range(2):
            for j in range(2):
                top = 1 + 2 * rb + i
                wide = jnp.pad(kernel, ((top, 5 - top), (j, 1 - j), (0, 0), (0, 0)))
                columns.append(wide.transpose(1, 0, 2, 3).reshape(4 * 8 * 16, -1))
    return jnp.concatenate(columns, axis=1)


def level_two_weights(kernel):
    none = ((0, 0),) * 3
    pair = [jnp.pad(kernel, ((i, 1 - i),) + none) for i in range(2)]
    return jnp.concatenate(pair, axis=3).reshape(12 * kernel.shape[2], -1)


def body(
    granule_blocks, row_weights, column_bank, destination, window_index, bank_index,
    kernel_one, reduce_two, kernel_two, reduce_three, kernel_three, reduce_four, kernel_four,
):
    axes = ("tx", "ty")
    tiles = lax.axis_size("tx") * lax.axis_size("ty")
    slots = resample(
        granule_blocks, row_weights, column_bank, destination, window_index, bank_index, tiles
    )
    received = lax.all_to_all(slots, axes, split_axis=0, concat_axis=0, tiled=True)
    one = level_one_weights(kernel_one)
    two = level_two_weights(kernel_two)
    down3 = reduce_three.transpose(1, 0, 2, 3).reshape(2, 256, 256)
    received, one, two, down3 = lax.optimization_barrier((received, one, two, down3))
    gridded, lines, left, right = grid(received)
    from_left, from_right = exchange_columns(left, right)
    main, lower, top, bottom = turn(lines)
    above, below = exchange_rows(top, bottom, from_left, from_right)
    spread = jnp.asarray(spread_matrix(), BF16)
    down2 = reduce_two.reshape(256, 128)
    inner = interior(main, lower, from_left, from_right, spread, one, down2)
    flat = encoder(
        inner, (top, bottom, from_left, from_right, above, below), spread, one, down2,
        two, down3,
        kernel_three.reshape(9 * 256, 256),
        reduce_four.reshape(4, 256, 512),
        kernel_four.reshape(9 * 512, 512),
    )
    return gridded, flat.reshape(NWIN, SPOTS, -1).transpose(2, 0, 1)


def solution(mesh):
    both = P(("tx", "ty"))
    in_specs = (both, both, P(), both, both, both) + (P(),) * 7
    out_specs = (P(None, "ty", "tx"), P(None, "ty", "tx"))
    return jax.shard_map(body, mesh=mesh, in_specs=in_specs, out_specs=out_specs, check_vma=False)
```

```python
import functools

import jax
import jax.numpy as jnp
import numpy as np
from jax import lax
from jax.experimental import pallas as pl
from jax.experimental.pallas import tpu as pltpu
from jax.sharding import PartitionSpec as P

BF16 = jnp.bfloat16
F32 = jnp.float32
BANDS = 13
SRC_ROWS = 16
WIN_ROWS = 8
CAP = 2
NWIN = 32
TILE_COLS = 128
LINES = BANDS * WIN_ROWS
PACKED = CAP * LINES + WIN_ROWS
STEP_BLOCKS = 16
PIECES = 4
PHASES = 8
SPOTS = TILE_COLS // PHASES
HALO = 2
WIDE = SPOTS + 2 * HALO
TALL = NWIN + 2 * HALO
POINTS = WIDE * TALL
GROUP = 4
GROUP_POINTS = GROUP * WIDE
MARGIN = 24
MIB = 1024 * 1024


def dot(a, b):
    return jnp.dot(a, b, preferred_element_type=F32)


def dot_nt(a, b):
    return lax.dot_general(a, b, (((1,), (1,)), ((), ())), preferred_element_type=F32)


def resample_kernel(
    dest_ref, win_ref, choice_ref, weight_ref, raw_hbm, bank_ref, out_ref,
    raw_ref, rows_ref, held_ref, slot_win_ref, sems,
):
    tiles, blocks = held_ref.shape[0], dest_ref.shape[0]
    deep = BANDS * SRC_ROWS

    def fetch(group):
        part = pl.ds(group * STEP_BLOCKS, STEP_BLOCKS)
        return pltpu.make_async_copy(raw_hbm.at[part], raw_ref.at[part], sems.at[group])

    for group in range(blocks // STEP_BLOCKS):
        fetch(group).start()

    def clear(i, carry):
        held_ref[i] = 0
        for k in range(CAP):
            slot_win_ref[i * CAP + k] = -1
        return carry

    lax.fori_loop(0, tiles, clear, 0, unroll=8)

    turned = jnp.transpose(weight_ref[...].astype(F32)).astype(BF16)
    depth = lax.broadcasted_iota(jnp.int32, (WIN_ROWS * SRC_ROWS, 256), 0)
    lane = lax.broadcasted_iota(jnp.int32, (WIN_ROWS * SRC_ROWS, 256), 1)
    offset = depth - (lane & (SRC_ROWS - 1))
    for r in range(WIN_ROWS):
        wide = dot(turned, (offset == r * SRC_ROWS).astype(F32).astype(BF16))
        for h in range(2):
            rows_ref[h, pl.ds(r, blocks, stride=WIN_ROWS), :] = wide[:, h * 128:(h + 1) * 128]

    line = lax.broadcasted_iota(jnp.int32, (LINES, 256), 0)
    lane = lax.broadcasted_iota(jnp.int32, (LINES, 256), 1)
    own = (line >> 3) == (lane >> 4)
    spot = lax.broadcasted_iota(jnp.int32, (WIN_ROWS, TILE_COLS), 1)

    def work(group, carry):
        fetch(group).wait()
        rowed = []
        for j in range(STEP_BLOCKS):
            n = group * STEP_BLOCKS + j
            row = pl.multiple_of(n * WIN_ROWS, WIN_ROWS)
            rows = jnp.concatenate(
                [rows_ref[h, pl.ds(row, WIN_ROWS), :] for h in range(2)], axis=1
            )
            weights = jnp.where(own, jnp.concatenate([rows] * BANDS, axis=0), 0.0)
            rowed.append(dot(weights.astype(BF16)[:, 0:deep], raw_ref[n]).astype(BF16))
        done = []
        for j in range(STEP_BLOCKS):
            n = group * STEP_BLOCKS + j
            done.append(dot(rowed[j], bank_ref[choice_ref[n]]).astype(BF16))
        for j in range(STEP_BLOCKS):
            n = group * STEP_BLOCKS + j
            tile = dest_ref[n]
            rank = held_ref[tile]
            held_ref[tile] = rank + 1
            slot_win_ref[tile * CAP + rank] = win_ref[n]
            place = pl.ds(pl.multiple_of(rank * LINES, WIN_ROWS), LINES)
            out_ref[tile, place, :] = done[j]
        return carry

    lax.fori_loop(0, blocks // STEP_BLOCKS, work, 0)

    def number(i, carry):
        window = jnp.where(spot == 0, slot_win_ref[i * CAP], slot_win_ref[i * CAP + 1])
        out_ref[i, CAP * LINES:] = window.astype(F32).astype(BF16)
        return carry

    lax.fori_loop(0, tiles, number, 0, unroll=4)


def resample(granule_blocks, row_weights, column_bank, destination, window_index, bank_index, tiles):
    blocks = granule_blocks.shape[0]
    deep = BANDS * SRC_ROWS
    vmem = pl.BlockSpec(memory_space=pltpu.VMEM)
    smem = pl.BlockSpec(memory_space=pltpu.SMEM)
    return pl.pallas_call(
        resample_kernel,
        in_specs=[smem, smem, smem, vmem, pl.BlockSpec(memory_space=pl.ANY), vmem],
        out_specs=vmem,
        scratch_shapes=[
            pltpu.VMEM((blocks, deep, TILE_COLS), BF16),
            pltpu.VMEM((2, blocks * WIN_ROWS, 128), F32),
            pltpu.SMEM((tiles,), jnp.int32),
            pltpu.SMEM((tiles * CAP,), jnp.int32),
            pltpu.SemaphoreType.DMA((blocks // STEP_BLOCKS,)),
        ],
        out_shape=jax.ShapeDtypeStruct((tiles, PACKED, TILE_COLS), BF16),
        compiler_params=pltpu.CompilerParams(vmem_limit_bytes=60 * MIB),
        name="resample",
    )(
        destination, window_index, bank_index,
        row_weights.transpose(1, 2, 0).reshape(WIN_ROWS * SRC_ROWS, blocks),
        granule_blocks.reshape(blocks, deep, TILE_COLS),
        column_bank,
    )


def grid_kernel(
    got_hbm, perm_ref, grid_ref, lines_ref, left_ref, right_ref,
    got_ref, sum_ref, number_ref, win_ref, count_ref, sem, sems,
):
    tiles = got_ref.shape[0]
    size = tiles // PIECES
    last = pl.ds(CAP * LINES, WIN_ROWS)
    head = pltpu.make_async_copy(got_hbm.at[:, last], got_ref.at[:, last], sems.at[PIECES])
    head.start()

    def fetch(piece):
        part = pl.ds(piece * size, size), pl.ds(0, CAP * LINES)
        return pltpu.make_async_copy(got_hbm.at[part], got_ref.at[part], sems.at[piece])

    for piece in range(PIECES):
        fetch(piece).start()
    head.wait()
    numbers = got_ref[:, CAP * LINES:, :].astype(F32)
    number_ref[...] = jnp.max(numbers, axis=1).astype(jnp.int32)
    copy = pltpu.make_async_copy(number_ref, win_ref, sem)
    copy.start()

    def clear(w, carry):
        sum_ref[w] = jnp.zeros(sum_ref.shape[1:], F32)
        count_ref[w] = 0
        return carry

    lax.fori_loop(0, NWIN + 1, clear, 0)
    copy.wait()

    def add(piece, i, carry):
        t = piece * size + i
        for k in range(CAP):
            w = win_ref[t, k]
            w = jnp.where(w < 0, NWIN, w)
            block = got_ref[t, k * LINES:(k + 1) * LINES].astype(F32)
            sum_ref[w, 0:LINES] = sum_ref[w, 0:LINES] + block
            count_ref[w] = count_ref[w] + 1
        return carry

    def add_piece(piece, carry):
        fetch(piece).wait()
        return lax.fori_loop(0, size, functools.partial(add, piece), carry, unroll=4)

    lax.fori_loop(0, PIECES, add_piece, 0)

    def finish(group, carry):
        first = group * GROUP
        means = []
        for k in range(GROUP):
            w = first + k
            divisor = jnp.maximum(count_ref[w], 1).astype(F32)
            mean = (sum_ref[w, 0:LINES] / divisor).astype(BF16).astype(F32)
            sum_ref[w, 0:LINES] = mean
            means.append(mean)
        row = pl.multiple_of(first * WIN_ROWS, GROUP * WIN_ROWS)
        for b in range(BANDS):
            part = jnp.concatenate([m[b * WIN_ROWS:(b + 1) * WIN_ROWS] for m in means], axis=0)
            grid_ref[b, pl.ds(row, GROUP * WIN_ROWS), :] = part.astype(BF16)
        for pair in range(GROUP // 2):
            lines = jnp.concatenate(
                [
                    sum_ref[first + pair * 2 + k, pl.ds(r, 16, stride=WIN_ROWS), :]
                    for k in range(2)
                    for r in range(WIN_ROWS)
                ],
                axis=0,
            ).astype(BF16)
            row = pl.multiple_of((first + pair * 2) * 128, 256)
            lines_ref[pl.ds(row, 256), :] = lines
            both = dot_nt(perm_ref[...], lines).astype(BF16)
            for k in range(2):
                w = first + pair * 2 + k
                turned = both[:, k * 128:(k + 1) * 128]
                left_ref[pl.ds(pl.multiple_of(w * 16, 16), 16), :] = turned[0:16]
                right_ref[pl.ds(pl.multiple_of(w * 16, 16), 16), :] = turned[16:32]
        return carry

    lax.fori_loop(0, NWIN // GROUP, finish, 0)


def grid(received):
    tiles = received.shape[0]
    perm = np.zeros((32, TILE_COLS), np.float32)
    for p in range(PHASES):
        for a in range(HALO):
            perm[p * HALO + a, a * PHASES + p] = 1.0
            perm[16 + p * HALO + a, (SPOTS - HALO + a) * PHASES + p] = 1.0
    vmem = pl.BlockSpec(memory_space=pltpu.VMEM)
    return pl.pallas_call(
        grid_kernel,
        in_specs=[pl.BlockSpec(memory_space=pl.ANY), vmem],
        out_specs=[vmem] * 4,
        out_shape=[
            jax.ShapeDtypeStruct((BANDS, NWIN * WIN_ROWS, TILE_COLS), BF16),
            jax.ShapeDtypeStruct((NWIN * 128, 128), BF16),
            jax.ShapeDtypeStruct((NWIN * 16, 128), BF16),
            jax.ShapeDtypeStruct((NWIN * 16, 128), BF16),
        ],
        scratch_shapes=[
            pltpu.VMEM(received.shape, BF16),
            pltpu.VMEM((NWIN + 1, 128, TILE_COLS), F32),
            pltpu.VMEM((tiles, TILE_COLS), jnp.int32),
            pltpu.SMEM((tiles, TILE_COLS), jnp.int32),
            pltpu.SMEM((NWIN + 1,), jnp.int32),
            pltpu.SemaphoreType.DMA,
            pltpu.SemaphoreType.DMA((PIECES + 1,)),
        ],
        compiler_params=pltpu.CompilerParams(vmem_limit_bytes=24 * MIB),
        name="grid",
    )(received, jnp.asarray(perm, BF16))


def turn_kernel(lines_ref, perm_ref, main_ref, lower_ref, top_ref, bottom_ref):
    def step(i, carry):
        for k in range(2):
            w = i * 2 + k
            start = pl.multiple_of(w * 128, 128)
            below = pl.multiple_of(jnp.minimum(w * 128 + 64, (NWIN - 1) * 128), 64)
            lines = jnp.concatenate(
                [lines_ref[pl.ds(start, 128), :], lines_ref[pl.ds(below, 128), :]], axis=0
            )
            both = dot_nt(perm_ref[...], lines).astype(BF16)
            main_ref[pl.ds(start, 128), :] = both[:, 0:128]
            lower_ref[pl.ds(start, 128), :] = both[:, 128:256]
        return carry

    lax.fori_loop(0, NWIN // 2, step, 0, unroll=2)
    top_ref[...] = main_ref[0:top_ref.shape[0]]
    bottom_ref[...] = main_ref[(NWIN - HALO) * 128:]


def turn(lines):
    perm = np.zeros((TILE_COLS, TILE_COLS), np.float32)
    for p in range(PHASES):
        for a in range(SPOTS):
            perm[p * SPOTS + a, a * PHASES + p] = 1.0
    vmem = pl.BlockSpec(memory_space=pltpu.VMEM)
    return pl.pallas_call(
        turn_kernel,
        in_specs=[vmem] * 2,
        out_specs=[vmem] * 4,
        out_shape=[
            jax.ShapeDtypeStruct((NWIN * 128, 128), BF16),
            jax.ShapeDtypeStruct((NWIN * 128, 128), BF16),
            jax.ShapeDtypeStruct(((HALO + 1) * 128, 128), BF16),
            jax.ShapeDtypeStruct((HALO * 128, 128), BF16),
        ],
        compiler_params=pltpu.CompilerParams(vmem_limit_bytes=16 * MIB),
        cost_estimate=pl.CostEstimate(
            flops=2 * NWIN * 128 ** 3 * 2, bytes_accessed=8 * MIB, transcendentals=0
        ),
        name="turn",
    )(lines, jnp.asarray(perm, BF16))


def exchange_columns(left, right):
    across = lax.axis_size("tx")
    right_ward = [(i, i + 1) for i in range(across - 1)]
    left_ward = [(t, s) for s, t in right_ward]
    return lax.ppermute(right, "tx", right_ward), lax.ppermute(left, "tx", left_ward)


def exchange_rows(top, bottom, from_left, from_right):
    down = lax.axis_size("ty")
    down_ward = [(i, i + 1) for i in range(down - 1)]
    up_ward = [(t, s) for s, t in down_ward]
    m, h = HALO * 128, HALO * 16
    first = jnp.concatenate([top[:m], from_left[:h], from_right[:h]], axis=0)
    last = jnp.concatenate([bottom, from_left[-h:], from_right[-h:]], axis=0)
    return lax.ppermute(last, "ty", down_ward), lax.ppermute(first, "ty", up_ward)


def spread_matrix():
    out = np.zeros((PHASES + 2, GROUP_POINTS, GROUP * 48), np.float32)
    for index in range(PHASES + 2):
        p = (index - 1) % PHASES
        shift = -1 if index == 0 else (1 if index == PHASES + 1 else 0)
        for k in range(GROUP):
            for a in range(WIDE):
                s = a + shift
                row = k * WIDE + a
                if s < 0 or s >= WIDE:
                    continue
                if s < HALO:
                    out[index, row, GROUP * 16 + k * 16 + p * HALO + s] = 1.0
                elif s < HALO + SPOTS:
                    out[index, row, k * 16 + s - HALO] = 1.0
                else:
                    out[index, row, GROUP * 32 + k * 16 + p * HALO + s - HALO - SPOTS] = 1.0
    return out


def relu(x):
    return jnp.maximum(x, 0.0)


def summed(taps, weights_ref, depth, lanes=slice(None)):
    total = None
    for k, tap in enumerate(taps):
        part = dot(tap(), weights_ref[k * depth:(k + 1) * depth, lanes])
        total = part if total is None else total + part
    return total


def level_one(x1, x2, one_ref, down2_ref, store):
    for cb in range(4):
        for version, x in enumerate((x1, x2)):
            taps = jnp.concatenate([x[2 * cb + k] for k in range(4)], axis=1)
            level = relu(dot(taps, one_ref[...])).astype(BF16)
            for half in range(2):
                down = relu(dot(level[:, half * 256:(half + 1) * 256], down2_ref[...]))
                store(2 * version + half, cb, down)


def lay(spread, first, second):
    return dot(spread, jnp.concatenate([jnp.concatenate(p, axis=0) for p in (first, second)], axis=1))


def interior_kernel(
    main_ref, lower_ref, fl_ref, fr_ref, spread_ref, one_ref, down2_ref, out_ref, side_ref, x1, x2
):
    low = lax.broadcasted_iota(jnp.int32, (16, 128), 1) < 64
    for s, side in enumerate((fl_ref, fr_ref)):
        for w in range(NWIN - 1):
            after = side[(w + 1) * 16:(w + 2) * 16].astype(F32)
            both = jnp.where(low, after, side[w * 16:(w + 1) * 16].astype(F32))
            side_ref[s, w * 16:(w + 1) * 16] = pltpu.roll(both, 64, 1).astype(BF16)

    def place(g, carry):
        row = pl.multiple_of(g * GROUP_POINTS, GROUP_POINTS)
        w = g * GROUP + GROUP - HALO
        edge = [pl.ds(pl.multiple_of((w + k) * 16, 16), 16) for k in range(GROUP)]
        for index in range(PHASES + 2):
            p = (index - 1) % PHASES
            own = [
                pl.ds(pl.multiple_of((w + k) * 128 + p * 16, 16), 16) for k in range(GROUP)
            ]
            first = [main_ref[o, :] for o in own]
            first += [ref[e, :] for ref in (fl_ref, fr_ref) for e in edge]
            second = [lower_ref[o, :] for o in own]
            second += [side_ref[s, e, :] for s in range(2) for e in edge]
            laid = lay(spread_ref[index], first, second).astype(BF16)
            x1[index, pl.ds(row, GROUP_POINTS), :] = laid[:, 0:128]
            x2[index, pl.ds(row, GROUP_POINTS), :] = laid[:, 128:256]
        return carry

    lax.fori_loop(0, TALL // GROUP - 2, place, 0)

    def store(rb, cb, down):
        out_ref[rb, cb] = down.astype(BF16)

    level_one(x1, x2, one_ref, down2_ref, store)


def interior(main, lower, from_left, from_right, spread, one, down2):
    vmem = pl.BlockSpec(memory_space=pltpu.VMEM)
    points = POINTS - 2 * GROUP_POINTS
    return pl.pallas_call(
        interior_kernel,
        in_specs=[vmem] * 7,
        out_specs=vmem,
        out_shape=jax.ShapeDtypeStruct((4, 4, points, 128), BF16),
        scratch_shapes=[
            pltpu.VMEM((2, NWIN * 16, 128), BF16),
            pltpu.VMEM((PHASES + 2, points, 128), BF16),
            pltpu.VMEM((PHASES + 2, points, 128), BF16),
        ],
        compiler_params=pltpu.CompilerParams(vmem_limit_bytes=32 * MIB),
        cost_estimate=pl.CostEstimate(
            flops=2 * points * 8 * (512 * 512 + 512 * 256),
            bytes_accessed=16 * MIB,
            transcendentals=0,
        ),
        name="interior",
    )(main, lower, from_left, from_right, spread, one, down2)


def encoder_kernel(
    inner_hbm, top_ref, bottom_ref, fl_ref, fr_ref, above_ref, below_ref, spread_ref, one_ref,
    down2_ref, two_hbm, down3_hbm, three_hbm, down4_hbm, four_hbm,
    out_ref,
    inner_ref, ext1, ext2, x1, x2, d2, d3, d4, stage,
    two_ref, down3_ref, three_ref, down4_ref, four_ref, sems,
):
    copies = [
        pltpu.make_async_copy(src, dst, sems.at[i])
        for i, (src, dst) in enumerate(
            (
                (down3_hbm, down3_ref),
                (three_hbm, three_ref),
                (down4_hbm, down4_ref),
                (four_hbm, four_ref),
                (inner_hbm, inner_ref),
                (two_hbm, two_ref),
            )
        )
    ]
    for i in (4, 5, 0, 1, 2, 3):
        copies[i].start()
    for side in range(2):
        for p in range(4):
            stage[side, p, 0:MARGIN] = jnp.zeros((MARGIN, 128), F32)
            stage[side, p, MARGIN + POINTS:] = jnp.zeros((MARGIN, 128), F32)

    m = HALO * 128
    for h in range(HALO):
        for source, i in ((above_ref, h), (below_ref, 3 * HALO + 1 + h)):
            ext1[i, 0:128] = source[h * 128:(h + 1) * 128]
            ext1[i, 128:144] = source[m + h * 16:m + h * 16 + 16]
            ext1[i, 144:160] = source[m + (HALO + h) * 16:m + (HALO + h) * 16 + 16]
    near = [(HALO + k, top_ref, k, k) for k in range(HALO + 1)]
    near += [(2 * HALO + 1 + k, bottom_ref, k, NWIN - HALO + k) for k in range(HALO)]
    for i, source, k, w in near:
        ext1[i, 0:128] = source[k * 128:(k + 1) * 128]
        ext1[i, 128:144] = fl_ref[w * 16:(w + 1) * 16]
        ext1[i, 144:160] = fr_ref[w * 16:(w + 1) * 16]

    low = lax.broadcasted_iota(jnp.int32, (160, 128), 1) < 64
    edges = (0, GROUP + 1)
    for base in edges:
        for k in range(GROUP):
            i = base + k
            after = min(i + 1, ext1.shape[0] - 1)
            both = jnp.where(low, ext1[after].astype(F32), ext1[i].astype(F32))
            ext2[i] = pltpu.roll(both, 64, 1).astype(BF16)

    for e, base in enumerate(edges):
        for index in range(PHASES + 2):
            p = (index - 1) % PHASES
            sides = []
            for ext in (ext1, ext2):
                pieces = [ext[base + k, p * 16:(p + 1) * 16] for k in range(GROUP)]
                pieces += [ext[base + k, 128:144] for k in range(GROUP)]
                pieces += [ext[base + k, 144:160] for k in range(GROUP)]
                sides.append(pieces)
            laid = lay(spread_ref[index], *sides).astype(BF16)
            x1[index, e * GROUP_POINTS:(e + 1) * GROUP_POINTS] = laid[:, 0:128]
            x2[index, e * GROUP_POINTS:(e + 1) * GROUP_POINTS] = laid[:, 128:256]

    across, below = lax.axis_size("tx"), lax.axis_size("ty")
    x, y = lax.axis_index("tx"), lax.axis_index("ty")
    least_w, most_w = jnp.where(y > 0, 0, HALO), jnp.where(y < below - 1, TALL, HALO + NWIN)
    least_a, most_a = jnp.where(x > 0, 0, HALO), jnp.where(x < across - 1, WIDE, HALO + SPOTS)
    point = lax.broadcasted_iota(jnp.int32, (POINTS, 128), 0)
    w = (point * (65536 // WIDE + 1)) >> 16
    a = point - w * WIDE
    inside = (w >= least_w) & (w < most_w) & (a >= least_a) & (a < most_a)
    mask = inside.astype(F32)
    mask2 = jnp.concatenate([mask, mask], axis=1)
    mask4 = jnp.concatenate([mask2, mask2], axis=1)

    def put(dst, i, j, value, last, first=0):
        rows = [(i + 1, 0)]
        if i == last:
            rows.append((0, WIDE))
        if i == 0:
            rows.append((last + 2, -WIDE))
        cols = [(j + 1, 0)]
        if j == last:
            cols.append((0, 1))
        if j == 0:
            cols.append((last + 2, -1))
        height = value.shape[0]
        dst[i + 1, j + 1, first:first + height] = value.astype(BF16)
        side = (i + j) % 2
        for p in range(value.shape[1] // 128):
            lanes = slice(p * 128, (p + 1) * 128)
            stage[side, p, MARGIN + first:MARGIN + first + height] = value[:, lanes]
            for r, row_shift in rows:
                for c, col_shift in cols:
                    shift = row_shift + col_shift
                    if shift:
                        moved = stage[side, p, MARGIN - shift:MARGIN - shift + POINTS]
                        dst[r, c, :, lanes] = moved.astype(BF16)

    copies[4].wait()

    def store(rb, cb, down):
        inner = inner_ref[rb, cb].astype(F32)
        down = jnp.concatenate([down[:GROUP_POINTS], inner, down[GROUP_POINTS:]], axis=0)
        if rb == 3:
            down = pltpu.roll(down, WIDE, 0)
        put(d2, (rb + 1) % 4, cb, down * mask, 3)

    level_one(x1, x2, one_ref, down2_ref, store)

    copies[5].wait()
    copies[0].wait()
    for rp in range(2):
        keep = slice(16, POINTS) if rp == 0 else slice(0, POINTS - 16)
        for j in range(2):
            total = None
            for v2 in range(2):
                spots = [(2 * rp + r, 2 * j + v2 + v) for r in range(4) for v in range(3)]
                pairs = [
                    lambda k=k: jnp.concatenate(
                        [d2[(*spots[2 * k], keep)], d2[(*spots[2 * k + 1], keep)]], axis=1
                    )
                    for k in range(6)
                ]
                level = relu(summed(pairs, two_ref, 256)).astype(BF16)
                part = dot(level, down3_ref[v2])
                total = part if total is None else total + part
            put(d3, rp, j, relu(total) * mask2[keep], 1, keep.start)

    copies[1].wait()
    copies[2].wait()
    total, keep = None, slice(16, POINTS - 16)
    for i in range(2):
        for j in range(2):
            taps = [lambda u=u, v=v: d3[i + u, j + v, keep] for u in range(3) for v in range(3)]
            level = relu(summed(taps, three_ref, 256)).astype(BF16)
            part = dot(level, down4_ref[i * 2 + j])
            total = part if total is None else total + part
    value = relu(total) * mask4[keep]

    for p in range(4):
        lanes = slice(p * 128, (p + 1) * 128)
        stage[0, p, MARGIN + keep.start:MARGIN + keep.stop] = value[:, lanes]
        for w in range(NWIN):
            for u in range(3):
                for v in range(3):
                    start = MARGIN + (w + HALO + u - 1) * WIDE + HALO + v - 1
                    tap = stage[0, p, start:start + SPOTS]
                    d4[u, v, w * SPOTS:(w + 1) * SPOTS, lanes] = tap.astype(BF16)

    copies[3].wait()
    taps = [lambda u=u, v=v: d4[u, v] for u in range(3) for v in range(3)]
    for half in range(2):
        lanes = slice(half * 256, (half + 1) * 256)
        out_ref[:, lanes] = relu(summed(taps, four_ref, 512, lanes)).astype(BF16)


def encoder(inner, edges, spread, one, down2, two, down3, three, down4, four):
    vmem = pl.BlockSpec(memory_space=pltpu.VMEM)
    hbm = pl.BlockSpec(memory_space=pl.ANY)
    rim = 2 * GROUP_POINTS
    return pl.pallas_call(
        encoder_kernel,
        in_specs=[hbm] + [vmem] * 9 + [hbm] * 5,
        out_specs=vmem,
        out_shape=jax.ShapeDtypeStruct((NWIN * SPOTS, four.shape[-1]), BF16),
        scratch_shapes=[
            pltpu.VMEM(inner.shape, BF16),
            pltpu.VMEM((2 * GROUP + 1, 160, 128), BF16),
            pltpu.VMEM((2 * GROUP + 1, 160, 128), BF16),
            pltpu.VMEM((PHASES + 2, rim, 128), BF16),
            pltpu.VMEM((PHASES + 2, rim, 128), BF16),
            pltpu.VMEM((6, 6, POINTS, 128), BF16),
            pltpu.VMEM((4, 4, POINTS, 256), BF16),
            pltpu.VMEM((3, 3, NWIN * SPOTS, 512), BF16),
            pltpu.VMEM((2, 4, POINTS + 2 * MARGIN, 128), F32),
            pltpu.VMEM(two.shape, BF16),
            pltpu.VMEM(down3.shape, BF16),
            pltpu.VMEM(three.shape, BF16),
            pltpu.VMEM(down4.shape, BF16),
            pltpu.VMEM(four.shape, BF16),
            pltpu.SemaphoreType.DMA((6,)),
        ],
        compiler_params=pltpu.CompilerParams(vmem_limit_bytes=44 * MIB),
        name="encoder",
    )(inner, *edges, spread, one, down2, two, down3, three, down4, four)


def level_one_weights(kernel):
    kernel = jnp.pad(kernel, ((0, 0), (0, 0), (0, 16 - BANDS), (0, 0)))
    columns = []
    for rb in range(2):
        for i in range(2):
            for j in range(2):
                top = 1 + 2 * rb + i
                wide = jnp.pad(kernel, ((top, 5 - top), (j, 1 - j), (0, 0), (0, 0)))
                columns.append(wide.transpose(1, 0, 2, 3).reshape(4 * 8 * 16, -1))
    return jnp.concatenate(columns, axis=1)


def level_two_weights(kernel):
    none = ((0, 0),) * 3
    pair = [jnp.pad(kernel, ((i, 1 - i),) + none) for i in range(2)]
    return jnp.concatenate(pair, axis=3).reshape(12 * kernel.shape[2], -1)


def body(
    granule_blocks, row_weights, column_bank, destination, window_index, bank_index,
    kernel_one, reduce_two, kernel_two, reduce_three, kernel_three, reduce_four, kernel_four,
):
    axes = ("tx", "ty")
    tiles = lax.axis_size("tx") * lax.axis_size("ty")
    slots = resample(
        granule_blocks, row_weights, column_bank, destination, window_index, bank_index, tiles
    )
    received = lax.all_to_all(slots, axes, split_axis=0, concat_axis=0, tiled=True)
    one = level_one_weights(kernel_one)
    two = level_two_weights(kernel_two)
    down3 = reduce_three.transpose(1, 0, 2, 3).reshape(2, 256, 256)
    received, one, two, down3 = lax.optimization_barrier((received, one, two, down3))
    gridded, lines, left, right = grid(received)
    from_left, from_right = exchange_columns(left, right)
    main, lower, top, bottom = turn(lines)
    above, below = exchange_rows(top, bottom, from_left, from_right)
    spread = jnp.asarray(spread_matrix(), BF16)
    down2 = reduce_two.reshape(256, 128)
    inner = interior(main, lower, from_left, from_right, spread, one, down2)
    flat = encoder(
        inner, (top, bottom, from_left, from_right, above, below), spread, one, down2,
        two, down3,
        kernel_three.reshape(9 * 256, 256),
        reduce_four.reshape(4, 256, 512),
        kernel_four.reshape(9 * 512, 512),
    )
    return gridded, flat.reshape(NWIN, SPOTS, -1).transpose(2, 0, 1)


def solution(mesh):
    both = P(("tx", "ty"))
    in_specs = (both, both, P(), both, both, both) + (P(),) * 7
    out_specs = (P(None, "ty", "tx"), P(None, "ty", "tx"))
    return jax.shard_map(body, mesh=mesh, in_specs=in_specs, out_specs=out_specs, check_vma=False)
```

```python
import functools

import jax
import jax.numpy as jnp
import numpy as np
from jax import lax
from jax.experimental import pallas as pl
from jax.experimental.pallas import tpu as pltpu
from jax.sharding import PartitionSpec as P

BF16 = jnp.bfloat16
F32 = jnp.float32
BANDS = 13
SRC_ROWS = 16
WIN_ROWS = 8
CAP = 2
NWIN = 32
TILE_COLS = 128
LINES = BANDS * WIN_ROWS
PACKED = CAP * LINES + WIN_ROWS
STEP_BLOCKS = 16
PIECES = 4
PHASES = 8
SPOTS = TILE_COLS // PHASES
HALO = 2
WIDE = SPOTS + 2 * HALO
TALL = NWIN + 2 * HALO
POINTS = WIDE * TALL
GROUP = 4
GROUP_POINTS = GROUP * WIDE
MARGIN = 24
MIB = 1024 * 1024


def dot(a, b):
    return jnp.dot(a, b, preferred_element_type=F32)


def dot_nt(a, b):
    return lax.dot_general(a, b, (((1,), (1,)), ((), ())), preferred_element_type=F32)


def resample_kernel(
    dest_ref, win_ref, choice_ref, weight_ref, raw_hbm, bank_ref, out_ref,
    raw_ref, rows_ref, held_ref, slot_win_ref, sems,
):
    tiles, blocks = held_ref.shape[0], dest_ref.shape[0]
    deep = BANDS * SRC_ROWS

    def fetch(group):
        part = pl.ds(group * STEP_BLOCKS, STEP_BLOCKS)
        return pltpu.make_async_copy(raw_hbm.at[part], raw_ref.at[part], sems.at[group])

    for group in range(blocks // STEP_BLOCKS):
        fetch(group).start()

    def clear(i, carry):
        held_ref[i] = 0
        for k in range(CAP):
            slot_win_ref[i * CAP + k] = -1
        return carry

    lax.fori_loop(0, tiles, clear, 0, unroll=8)

    turned = jnp.transpose(weight_ref[...].astype(F32)).astype(BF16)
    depth = lax.broadcasted_iota(jnp.int32, (WIN_ROWS * SRC_ROWS, 256), 0)
    lane = lax.broadcasted_iota(jnp.int32, (WIN_ROWS * SRC_ROWS, 256), 1)
    offset = depth - (lane & (SRC_ROWS - 1))
    for r in range(WIN_ROWS):
        wide = dot(turned, (offset == r * SRC_ROWS).astype(F32).astype(BF16))
        for h in range(2):
            rows_ref[h, pl.ds(r, blocks, stride=WIN_ROWS), :] = wide[:, h * 128:(h + 1) * 128]

    line = lax.broadcasted_iota(jnp.int32, (LINES, 256), 0)
    lane = lax.broadcasted_iota(jnp.int32, (LINES, 256), 1)
    own = (line >> 3) == (lane >> 4)
    spot = lax.broadcasted_iota(jnp.int32, (WIN_ROWS, TILE_COLS), 1)

    def work(group, carry):
        fetch(group).wait()
        rowed = []
        for j in range(STEP_BLOCKS):
            n = group * STEP_BLOCKS + j
            row = pl.multiple_of(n * WIN_ROWS, WIN_ROWS)
            rows = jnp.concatenate(
                [rows_ref[h, pl.ds(row, WIN_ROWS), :] for h in range(2)], axis=1
            )
            weights = jnp.where(own, jnp.concatenate([rows] * BANDS, axis=0), 0.0)
            rowed.append(dot(weights.astype(BF16)[:, 0:deep], raw_ref[n]).astype(BF16))
        done = []
        for j in range(STEP_BLOCKS):
            n = group * STEP_BLOCKS + j
            done.append(dot(rowed[j], bank_ref[choice_ref[n]]).astype(BF16))
        for j in range(STEP_BLOCKS):
            n = group * STEP_BLOCKS + j
            tile = dest_ref[n]
            rank = held_ref[tile]
            held_ref[tile] = rank + 1
            slot_win_ref[tile * CAP + rank] = win_ref[n]
            place = pl.ds(pl.multiple_of(rank * LINES, WIN_ROWS), LINES)
            out_ref[tile, place, :] = done[j]
        return carry

    lax.fori_loop(0, blocks // STEP_BLOCKS, work, 0)

    def number(i, carry):
        window = jnp.where(spot == 0, slot_win_ref[i * CAP], slot_win_ref[i * CAP + 1])
        out_ref[i, CAP * LINES:] = window.astype(F32).astype(BF16)
        return carry

    lax.fori_loop(0, tiles, number, 0, unroll=4)


def resample(granule_blocks, row_weights, column_bank, destination, window_index, bank_index, tiles):
    blocks = granule_blocks.shape[0]
    deep = BANDS * SRC_ROWS
    vmem = pl.BlockSpec(memory_space=pltpu.VMEM)
    smem = pl.BlockSpec(memory_space=pltpu.SMEM)
    return pl.pallas_call(
        resample_kernel,
        in_specs=[smem, smem, smem, vmem, pl.BlockSpec(memory_space=pl.ANY), vmem],
        out_specs=vmem,
        scratch_shapes=[
            pltpu.VMEM((blocks, deep, TILE_COLS), BF16),
            pltpu.VMEM((2, blocks * WIN_ROWS, 128), F32),
            pltpu.SMEM((tiles,), jnp.int32),
            pltpu.SMEM((tiles * CAP,), jnp.int32),
            pltpu.SemaphoreType.DMA((blocks // STEP_BLOCKS,)),
        ],
        out_shape=jax.ShapeDtypeStruct((tiles, PACKED, TILE_COLS), BF16),
        compiler_params=pltpu.CompilerParams(vmem_limit_bytes=60 * MIB),
        name="resample",
    )(
        destination, window_index, bank_index,
        row_weights.transpose(1, 2, 0).reshape(WIN_ROWS * SRC_ROWS, blocks),
        granule_blocks.reshape(blocks, deep, TILE_COLS),
        column_bank,
    )


def grid_kernel(
    got_hbm, perm_ref, grid_ref, lines_ref, left_ref, right_ref,
    got_ref, sum_ref, number_ref, win_ref, count_ref, sem, sems,
):
    tiles = got_ref.shape[0]
    size = tiles // PIECES
    last = pl.ds(CAP * LINES, WIN_ROWS)
    head = pltpu.make_async_copy(got_hbm.at[:, last], got_ref.at[:, last], sems.at[PIECES])
    head.start()

    def fetch(piece):
        part = pl.ds(piece * size, size), pl.ds(0, CAP * LINES)
        return pltpu.make_async_copy(got_hbm.at[part], got_ref.at[part], sems.at[piece])

    for piece in range(PIECES):
        fetch(piece).start()
    head.wait()
    numbers = got_ref[:, CAP * LINES:, :].astype(F32)
    number_ref[...] = jnp.max(numbers, axis=1).astype(jnp.int32)
    copy = pltpu.make_async_copy(number_ref, win_ref, sem)
    copy.start()

    def clear(w, carry):
        sum_ref[w] = jnp.zeros(sum_ref.shape[1:], F32)
        count_ref[w] = 0
        return carry

    lax.fori_loop(0, NWIN + 1, clear, 0)
    copy.wait()

    def add(piece, i, carry):
        t = piece * size + i
        for k in range(CAP):
            w = win_ref[t, k]
            w = jnp.where(w < 0, NWIN, w)
            block = got_ref[t, k * LINES:(k + 1) * LINES].astype(F32)
            sum_ref[w, 0:LINES] = sum_ref[w, 0:LINES] + block
            count_ref[w] = count_ref[w] + 1
        return carry

    def add_piece(piece, carry):
        fetch(piece).wait()
        return lax.fori_loop(0, size, functools.partial(add, piece), carry, unroll=4)

    lax.fori_loop(0, PIECES, add_piece, 0)

    def finish(group, carry):
        first = group * GROUP
        means = []
        for k in range(GROUP):
            w = first + k
            divisor = jnp.maximum(count_ref[w], 1).astype(F32)
            mean = (sum_ref[w, 0:LINES] / divisor).astype(BF16).astype(F32)
            sum_ref[w, 0:LINES] = mean
            means.append(mean)
        row = pl.multiple_of(first * WIN_ROWS, GROUP * WIN_ROWS)
        for b in range(BANDS):
            part = jnp.concatenate([m[b * WIN_ROWS:(b + 1) * WIN_ROWS] for m in means], axis=0)
            grid_ref[b, pl.ds(row, GROUP * WIN_ROWS), :] = part.astype(BF16)
        for pair in range(GROUP // 2):
            lines = jnp.concatenate(
                [
                    sum_ref[first + pair * 2 + k, pl.ds(r, 16, stride=WIN_ROWS), :]
                    for k in range(2)
                    for r in range(WIN_ROWS)
                ],
                axis=0,
            ).astype(BF16)
            row = pl.multiple_of((first + pair * 2) * 128, 256)
            lines_ref[pl.ds(row, 256), :] = lines
            both = dot_nt(perm_ref[...], lines).astype(BF16)
            for k in range(2):
                w = first + pair * 2 + k
                turned = both[:, k * 128:(k + 1) * 128]
                left_ref[pl.ds(pl.multiple_of(w * 16, 16), 16), :] = turned[0:16]
                right_ref[pl.ds(pl.multiple_of(w * 16, 16), 16), :] = turned[16:32]
        return carry

    lax.fori_loop(0, NWIN // GROUP, finish, 0)


def grid(received):
    tiles = received.shape[0]
    perm = np.zeros((32, TILE_COLS), np.float32)
    for p in range(PHASES):
        for a in range(HALO):
            perm[p * HALO + a, a * PHASES + p] = 1.0
            perm[16 + p * HALO + a, (SPOTS - HALO + a) * PHASES + p] = 1.0
    vmem = pl.BlockSpec(memory_space=pltpu.VMEM)
    return pl.pallas_call(
        grid_kernel,
        in_specs=[pl.BlockSpec(memory_space=pl.ANY), vmem],
        out_specs=[vmem] * 4,
        out_shape=[
            jax.ShapeDtypeStruct((BANDS, NWIN * WIN_ROWS, TILE_COLS), BF16),
            jax.ShapeDtypeStruct((NWIN * 128, 128), BF16),
            jax.ShapeDtypeStruct((NWIN * 16, 128), BF16),
            jax.ShapeDtypeStruct((NWIN * 16, 128), BF16),
        ],
        scratch_shapes=[
            pltpu.VMEM(received.shape, BF16),
            pltpu.VMEM((NWIN + 1, 128, TILE_COLS), F32),
            pltpu.VMEM((tiles, TILE_COLS), jnp.int32),
            pltpu.SMEM((tiles, TILE_COLS), jnp.int32),
            pltpu.SMEM((NWIN + 1,), jnp.int32),
            pltpu.SemaphoreType.DMA,
            pltpu.SemaphoreType.DMA((PIECES + 1,)),
        ],
        compiler_params=pltpu.CompilerParams(vmem_limit_bytes=24 * MIB),
        name="grid",
    )(received, jnp.asarray(perm, BF16))


def turn_kernel(lines_ref, perm_ref, main_ref, lower_ref, top_ref, bottom_ref):
    def step(i, carry):
        for k in range(2):
            w = i * 2 + k
            start = pl.multiple_of(w * 128, 128)
            below = pl.multiple_of(jnp.minimum(w * 128 + 64, (NWIN - 1) * 128), 64)
            lines = jnp.concatenate(
                [lines_ref[pl.ds(start, 128), :], lines_ref[pl.ds(below, 128), :]], axis=0
            )
            both = dot_nt(perm_ref[...], lines).astype(BF16)
            main_ref[pl.ds(start, 128), :] = both[:, 0:128]
            lower_ref[pl.ds(start, 128), :] = both[:, 128:256]
        return carry

    lax.fori_loop(0, NWIN // 2, step, 0, unroll=2)
    top_ref[...] = main_ref[0:top_ref.shape[0]]
    bottom_ref[...] = main_ref[(NWIN - HALO) * 128:]


def turn(lines):
    perm = np.zeros((TILE_COLS, TILE_COLS), np.float32)
    for p in range(PHASES):
        for a in range(SPOTS):
            perm[p * SPOTS + a, a * PHASES + p] = 1.0
    vmem = pl.BlockSpec(memory_space=pltpu.VMEM)
    return pl.pallas_call(
        turn_kernel,
        in_specs=[vmem] * 2,
        out_specs=[vmem] * 4,
        out_shape=[
            jax.ShapeDtypeStruct((NWIN * 128, 128), BF16),
            jax.ShapeDtypeStruct((NWIN * 128, 128), BF16),
            jax.ShapeDtypeStruct(((HALO + 1) * 128, 128), BF16),
            jax.ShapeDtypeStruct((HALO * 128, 128), BF16),
        ],
        compiler_params=pltpu.CompilerParams(vmem_limit_bytes=16 * MIB),
        cost_estimate=pl.CostEstimate(
            flops=2 * NWIN * 128 ** 3 * 2, bytes_accessed=8 * MIB, transcendentals=0
        ),
        name="turn",
    )(lines, jnp.asarray(perm, BF16))


def exchange_columns(left, right):
    across = lax.axis_size("tx")
    right_ward = [(i, i + 1) for i in range(across - 1)]
    left_ward = [(t, s) for s, t in right_ward]
    return lax.ppermute(right, "tx", right_ward), lax.ppermute(left, "tx", left_ward)


def exchange_rows(top, bottom, from_left, from_right):
    down = lax.axis_size("ty")
    down_ward = [(i, i + 1) for i in range(down - 1)]
    up_ward = [(t, s) for s, t in down_ward]
    m, h = HALO * 128, HALO * 16
    first = jnp.concatenate([top[:m], from_left[:h], from_right[:h]], axis=0)
    last = jnp.concatenate([bottom, from_left[-h:], from_right[-h:]], axis=0)
    return lax.ppermute(last, "ty", down_ward), lax.ppermute(first, "ty", up_ward)


def spread_matrix():
    out = np.zeros((PHASES + 2, GROUP_POINTS, GROUP * 48), np.float32)
    for index in range(PHASES + 2):
        p = (index - 1) % PHASES
        shift = -1 if index == 0 else (1 if index == PHASES + 1 else 0)
        for k in range(GROUP):
            for a in range(WIDE):
                s = a + shift
                row = k * WIDE + a
                if s < 0 or s >= WIDE:
                    continue
                if s < HALO:
                    out[index, row, GROUP * 16 + k * 16 + p * HALO + s] = 1.0
                elif s < HALO + SPOTS:
                    out[index, row, k * 16 + s - HALO] = 1.0
                else:
                    out[index, row, GROUP * 32 + k * 16 + p * HALO + s - HALO - SPOTS] = 1.0
    return out


def relu(x):
    return jnp.maximum(x, 0.0)


def summed(taps, weights_ref, depth, lanes=slice(None)):
    total = None
    for k, tap in enumerate(taps):
        part = dot(tap(), weights_ref[k * depth:(k + 1) * depth, lanes])
        total = part if total is None else total + part
    return total


def level_one(x1, x2, one_ref, down2_ref, store):
    for cb in range(4):
        for version, x in enumerate((x1, x2)):
            pairs = [
                lambda k=k: jnp.concatenate([x[2 * cb + k], x[2 * cb + k + 1]], axis=1)
                for k in (0, 2)
            ]
            for half in range(2):
                lanes = slice(half * 256, (half + 1) * 256)
                level = relu(summed(pairs, one_ref, 256, lanes)).astype(BF16)
                down = relu(dot(level, down2_ref[...]))
                store(2 * version + half, cb, down)


def lay(spread, first, second):
    return dot(spread, jnp.concatenate([jnp.concatenate(p, axis=0) for p in (first, second)], axis=1))


def interior_kernel(
    main_ref, lower_ref, fl_ref, fr_ref, spread_ref, one_ref, down2_ref, out_ref, side_ref, x1, x2
):
    low = lax.broadcasted_iota(jnp.int32, (16, 128), 1) < 64
    for s, side in enumerate((fl_ref, fr_ref)):
        for w in range(NWIN - 1):
            after = side[(w + 1) * 16:(w + 2) * 16].astype(F32)
            both = jnp.where(low, after, side[w * 16:(w + 1) * 16].astype(F32))
            side_ref[s, w * 16:(w + 1) * 16] = pltpu.roll(both, 64, 1).astype(BF16)

    def place(g, carry):
        row = pl.multiple_of(g * GROUP_POINTS, GROUP_POINTS)
        w = g * GROUP + GROUP - HALO
        edge = [pl.ds(pl.multiple_of((w + k) * 16, 16), 16) for k in range(GROUP)]
        for index in range(PHASES + 2):
            p = (index - 1) % PHASES
            own = [
                pl.ds(pl.multiple_of((w + k) * 128 + p * 16, 16), 16) for k in range(GROUP)
            ]
            first = [main_ref[o, :] for o in own]
            first += [ref[e, :] for ref in (fl_ref, fr_ref) for e in edge]
            second = [lower_ref[o, :] for o in own]
            second += [side_ref[s, e, :] for s in range(2) for e in edge]
            laid = lay(spread_ref[index], first, second).astype(BF16)
            x1[index, pl.ds(row, GROUP_POINTS), :] = laid[:, 0:128]
            x2[index, pl.ds(row, GROUP_POINTS), :] = laid[:, 128:256]
        return carry

    lax.fori_loop(0, TALL // GROUP - 2, place, 0)

    def store(rb, cb, down):
        out_ref[rb, cb] = down.astype(BF16)

    level_one(x1, x2, one_ref, down2_ref, store)


def interior(main, lower, from_left, from_right, spread, one, down2):
    vmem = pl.BlockSpec(memory_space=pltpu.VMEM)
    points = POINTS - 2 * GROUP_POINTS
    return pl.pallas_call(
        interior_kernel,
        in_specs=[vmem] * 7,
        out_specs=vmem,
        out_shape=jax.ShapeDtypeStruct((4, 4, points, 128), BF16),
        scratch_shapes=[
            pltpu.VMEM((2, NWIN * 16, 128), BF16),
            pltpu.VMEM((PHASES + 2, points, 128), BF16),
            pltpu.VMEM((PHASES + 2, points, 128), BF16),
        ],
        compiler_params=pltpu.CompilerParams(vmem_limit_bytes=32 * MIB),
        cost_estimate=pl.CostEstimate(
            flops=2 * points * 8 * (512 * 512 + 512 * 256),
            bytes_accessed=16 * MIB,
            transcendentals=0,
        ),
        name="interior",
    )(main, lower, from_left, from_right, spread, one, down2)


def encoder_kernel(
    inner_hbm, top_ref, bottom_ref, fl_ref, fr_ref, above_ref, below_ref, spread_ref, one_ref,
    down2_ref, two_hbm, down3_hbm, three_hbm, down4_hbm, four_hbm,
    out_ref,
    inner_ref, ext1, ext2, x1, x2, d2, d3, d4, stage,
    two_ref, down3_ref, three_ref, down4_ref, four_ref, sems,
):
    copies = [
        pltpu.make_async_copy(src, dst, sems.at[i])
        for i, (src, dst) in enumerate(
            (
                (down3_hbm, down3_ref),
                (three_hbm, three_ref),
                (down4_hbm, down4_ref),
                (four_hbm, four_ref),
                (inner_hbm, inner_ref),
                (two_hbm, two_ref),
            )
        )
    ]
    for i in (4, 5, 0, 1, 2, 3):
        copies[i].start()
    for side in range(2):
        for p in range(4):
            stage[side, p, 0:MARGIN] = jnp.zeros((MARGIN, 128), F32)
            stage[side, p, MARGIN + POINTS:] = jnp.zeros((MARGIN, 128), F32)

    m = HALO * 128
    for h in range(HALO):
        for source, i in ((above_ref, h), (below_ref, 3 * HALO + 1 + h)):
            ext1[i, 0:128] = source[h * 128:(h + 1) * 128]
            ext1[i, 128:144] = source[m + h * 16:m + h * 16 + 16]
            ext1[i, 144:160] = source[m + (HALO + h) * 16:m + (HALO + h) * 16 + 16]
    near = [(HALO + k, top_ref, k, k) for k in range(HALO + 1)]
    near += [(2 * HALO + 1 + k, bottom_ref, k, NWIN - HALO + k) for k in range(HALO)]
    for i, source, k, w in near:
        ext1[i, 0:128] = source[k * 128:(k + 1) * 128]
        ext1[i, 128:144] = fl_ref[w * 16:(w + 1) * 16]
        ext1[i, 144:160] = fr_ref[w * 16:(w + 1) * 16]

    low = lax.broadcasted_iota(jnp.int32, (160, 128), 1) < 64
    edges = (0, GROUP + 1)
    for base in edges:
        for k in range(GROUP):
            i = base + k
            after = min(i + 1, ext1.shape[0] - 1)
            both = jnp.where(low, ext1[after].astype(F32), ext1[i].astype(F32))
            ext2[i] = pltpu.roll(both, 64, 1).astype(BF16)

    for e, base in enumerate(edges):
        for index in range(PHASES + 2):
            p = (index - 1) % PHASES
            sides = []
            for ext in (ext1, ext2):
                pieces = [ext[base + k, p * 16:(p + 1) * 16] for k in range(GROUP)]
                pieces += [ext[base + k, 128:144] for k in range(GROUP)]
                pieces += [ext[base + k, 144:160] for k in range(GROUP)]
                sides.append(pieces)
            laid = lay(spread_ref[index], *sides).astype(BF16)
            x1[index, e * GROUP_POINTS:(e + 1) * GROUP_POINTS] = laid[:, 0:128]
            x2[index, e * GROUP_POINTS:(e + 1) * GROUP_POINTS] = laid[:, 128:256]

    across, below = lax.axis_size("tx"), lax.axis_size("ty")
    x, y = lax.axis_index("tx"), lax.axis_index("ty")
    least_w, most_w = jnp.where(y > 0, 0, HALO), jnp.where(y < below - 1, TALL, HALO + NWIN)
    least_a, most_a = jnp.where(x > 0, 0, HALO), jnp.where(x < across - 1, WIDE, HALO + SPOTS)
    point = lax.broadcasted_iota(jnp.int32, (POINTS, 128), 0)
    w = (point * (65536 // WIDE + 1)) >> 16
    a = point - w * WIDE
    inside = (w >= least_w) & (w < most_w) & (a >= least_a) & (a < most_a)
    mask = inside.astype(F32)
    mask2 = jnp.concatenate([mask, mask], axis=1)
    mask4 = jnp.concatenate([mask2, mask2], axis=1)

    def put(dst, i, j, value, last, first=0):
        rows = [(i + 1, 0)]
        if i == last:
            rows.append((0, WIDE))
        if i == 0:
            rows.append((last + 2, -WIDE))
        cols = [(j + 1, 0)]
        if j == last:
            cols.append((0, 1))
        if j == 0:
            cols.append((last + 2, -1))
        height = value.shape[0]
        dst[i + 1, j + 1, first:first + height] = value.astype(BF16)
        side = (i + j) % 2
        for p in range(value.shape[1] // 128):
            lanes = slice(p * 128, (p + 1) * 128)
            stage[side, p, MARGIN + first:MARGIN + first + height] = value[:, lanes]
            for r, row_shift in rows:
                for c, col_shift in cols:
                    shift = row_shift + col_shift
                    if shift:
                        moved = stage[side, p, MARGIN - shift:MARGIN - shift + POINTS]
                        dst[r, c, :, lanes] = moved.astype(BF16)

    copies[4].wait()

    def store(rb, cb, down):
        inner = inner_ref[rb, cb].astype(F32)
        down = jnp.concatenate([down[:GROUP_POINTS], inner, down[GROUP_POINTS:]], axis=0)
        if rb == 3:
            down = pltpu.roll(down, WIDE, 0)
        put(d2, (rb + 1) % 4, cb, down * mask, 3)

    level_one(x1, x2, one_ref, down2_ref, store)

    copies[5].wait()
    copies[0].wait()
    for rp in range(2):
        keep = slice(16, POINTS) if rp == 0 else slice(0, POINTS - 16)
        for j in range(2):
            total = None
            for v2 in range(2):
                spots = [(2 * rp + r, 2 * j + v2 + v) for r in range(4) for v in range(3)]
                pairs = [
                    lambda k=k: jnp.concatenate(
                        [d2[(*spots[2 * k], keep)], d2[(*spots[2 * k + 1], keep)]], axis=1
                    )
                    for k in range(6)
                ]
                level = relu(summed(pairs, two_ref, 256)).astype(BF16)
                part = dot(level, down3_ref[v2])
                total = part if total is None else total + part
            put(d3, rp, j, relu(total) * mask2[keep], 1, keep.start)

    copies[1].wait()
    copies[2].wait()
    total, keep = None, slice(16, POINTS - 16)
    for i in range(2):
        for j in range(2):
            taps = [lambda u=u, v=v: d3[i + u, j + v, keep] for u in range(3) for v in range(3)]
            level = relu(summed(taps, three_ref, 256)).astype(BF16)
            part = dot(level, down4_ref[i * 2 + j])
            total = part if total is None else total + part
    value = relu(total) * mask4[keep]

    for p in range(4):
        lanes = slice(p * 128, (p + 1) * 128)
        stage[0, p, MARGIN + keep.start:MARGIN + keep.stop] = value[:, lanes]
        for w in range(NWIN):
            for u in range(3):
                for v in range(3):
                    start = MARGIN + (w + HALO + u - 1) * WIDE + HALO + v - 1
                    tap = stage[0, p, start:start + SPOTS]
                    d4[u, v, w * SPOTS:(w + 1) * SPOTS, lanes] = tap.astype(BF16)

    copies[3].wait()
    taps = [lambda u=u, v=v: d4[u, v] for u in range(3) for v in range(3)]
    for half in range(2):
        lanes = slice(half * 256, (half + 1) * 256)
        out_ref[:, lanes] = relu(summed(taps, four_ref, 512, lanes)).astype(BF16)


def encoder(inner, edges, spread, one, down2, two, down3, three, down4, four):
    vmem = pl.BlockSpec(memory_space=pltpu.VMEM)
    hbm = pl.BlockSpec(memory_space=pl.ANY)
    rim = 2 * GROUP_POINTS
    return pl.pallas_call(
        encoder_kernel,
        in_specs=[hbm] + [vmem] * 9 + [hbm] * 5,
        out_specs=vmem,
        out_shape=jax.ShapeDtypeStruct((NWIN * SPOTS, four.shape[-1]), BF16),
        scratch_shapes=[
            pltpu.VMEM(inner.shape, BF16),
            pltpu.VMEM((2 * GROUP + 1, 160, 128), BF16),
            pltpu.VMEM((2 * GROUP + 1, 160, 128), BF16),
            pltpu.VMEM((PHASES + 2, rim, 128), BF16),
            pltpu.VMEM((PHASES + 2, rim, 128), BF16),
            pltpu.VMEM((6, 6, POINTS, 128), BF16),
            pltpu.VMEM((4, 4, POINTS, 256), BF16),
            pltpu.VMEM((3, 3, NWIN * SPOTS, 512), BF16),
            pltpu.VMEM((2, 4, POINTS + 2 * MARGIN, 128), F32),
            pltpu.VMEM(two.shape, BF16),
            pltpu.VMEM(down3.shape, BF16),
            pltpu.VMEM(three.shape, BF16),
            pltpu.VMEM(down4.shape, BF16),
            pltpu.VMEM(four.shape, BF16),
            pltpu.SemaphoreType.DMA((6,)),
        ],
        compiler_params=pltpu.CompilerParams(vmem_limit_bytes=44 * MIB),
        name="encoder",
    )(inner, *edges, spread, one, down2, two, down3, three, down4, four)


def level_one_weights(kernel):
    kernel = jnp.pad(kernel, ((0, 0), (0, 0), (0, 16 - BANDS), (0, 0)))
    columns = []
    for rb in range(2):
        for i in range(2):
            for j in range(2):
                top = 1 + 2 * rb + i
                wide = jnp.pad(kernel, ((top, 5 - top), (j, 1 - j), (0, 0), (0, 0)))
                columns.append(wide.transpose(1, 0, 2, 3).reshape(4 * 8 * 16, -1))
    return jnp.concatenate(columns, axis=1)


def level_two_weights(kernel):
    none = ((0, 0),) * 3
    pair = [jnp.pad(kernel, ((i, 1 - i),) + none) for i in range(2)]
    return jnp.concatenate(pair, axis=3).reshape(12 * kernel.shape[2], -1)


def body(
    granule_blocks, row_weights, column_bank, destination, window_index, bank_index,
    kernel_one, reduce_two, kernel_two, reduce_three, kernel_three, reduce_four, kernel_four,
):
    axes = ("tx", "ty")
    tiles = lax.axis_size("tx") * lax.axis_size("ty")
    slots = resample(
        granule_blocks, row_weights, column_bank, destination, window_index, bank_index, tiles
    )
    received = lax.all_to_all(slots, axes, split_axis=0, concat_axis=0, tiled=True)
    one = level_one_weights(kernel_one)
    two = level_two_weights(kernel_two)
    down3 = reduce_three.transpose(1, 0, 2, 3).reshape(2, 256, 256)
    received, one, two, down3 = lax.optimization_barrier((received, one, two, down3))
    gridded, lines, left, right = grid(received)
    from_left, from_right = exchange_columns(left, right)
    main, lower, top, bottom = turn(lines)
    above, below = exchange_rows(top, bottom, from_left, from_right)
    spread = jnp.asarray(spread_matrix(), BF16)
    down2 = reduce_two.reshape(256, 128)
    inner = interior(main, lower, from_left, from_right, spread, one, down2)
    flat = encoder(
        inner, (top, bottom, from_left, from_right, above, below), spread, one, down2,
        two, down3,
        kernel_three.reshape(9 * 256, 256),
        reduce_four.reshape(4, 256, 512),
        kernel_four.reshape(9 * 512, 512),
    )
    return gridded, flat.reshape(NWIN, SPOTS, -1).transpose(2, 0, 1)


def solution(mesh):
    both = P(("tx", "ty"))
    in_specs = (both, both, P(), both, both, both) + (P(),) * 7
    out_specs = (P(None, "ty", "tx"), P(None, "ty", "tx"))
    return jax.shard_map(body, mesh=mesh, in_specs=in_specs, out_specs=out_specs, check_vma=False)
```
